256 devices in a mesh: dp: 4 (over x), tm: 64 (over y, z, core).
Axes of the slice: x: 4, y: 4, z: 8, core: 2. Of those that a mesh axis runs over, the one named last changes fastest.
Arguments:
- frames: bfloat16 [4, 8192, 1536], P('dp', 'tm'), may hold values from -48 to 48
- taps: float32 [31, 1536], replicated, may hold values from -1 to 1
- batchnorm_gain_scale: float32 [1536], replicated, may hold values from 0.25 to 1.75
- batchnorm_shift_bias: float32 [1536], replicated, may hold values from -3 to 3
- w_router: bfloat16 [1536, 8], replicated, may hold values from -0.3125 to 0.3125
- w_in: bfloat16 [1536, 24576], P(None, 'tm'), may hold values from -0.15625 to 0.15625
- w_out: bfloat16 [24576, 1536], P('tm'), may hold values from -0.109375 to 0.109375
- choices: int32 [4, 8192, 2], P('dp', 'tm'), may hold values from 0 to 7, all different within a row; in each aligned block of 128 rows (0 to 127, 128 to 255, ..., all dimensions but the last counted through in order) at most 32 rows name the same one
- cotangent: bfloat16 [4, 8192, 1536], P('dp', 'tm'), may hold values from -48 to 48
Outputs:
- mixed: bfloat16 [4, 8192, 1536], P('dp', 'tm')
- grad_frames: bfloat16 [4, 8192, 1536], P('dp', 'tm')
- grad_taps: float32 [31, 1536], replicated
- grad_w_in: float32 [1536, 24576], P('dp', 'tm')
- grad_w_out: float32 [24576, 1536], P('tm', 'dp')
The draws below stay inside these ranges and needn't reach their ends.
Inputs may be any that keep to these rules, and one draw needn't show every extreme that they name: `choices`: within the 128 frames of one device the two experts of a frame differ, and every expert is named exactly 32 times.
All inputs are finite; a program needn't handle non-finite values.
Results may differ from the reference program's by a relative error of at most 0.0063.
Values may be sent and summed in bfloat16 or wider, within the bound.
A program may use at most 192 MiB of HBM per device.

```python
import math
import jax
import jax.numpy as jnp
import numpy as np
from jax import lax

D = 1536
FF = 3072
EXPERTS = 8
TOP = 2
TAPS = 31
T_DEV = 128
SEQ = 8192
UTTERANCES = 4
CAP = 32
N_TM = 64


def scaled_field(noise, rows, cols):
    ramp = (1.0 + 2.0 * jnp.arange(SEQ, dtype=jnp.float32) / (SEQ - 1))[None, :, None]
    return jnp.clip(noise * ramp * rows * cols, -48.0, 48.0)


def draw_frames(key, part):
    key = jax.random.fold_in(key, 11)
    key_noise, key_rows, key_cols = jax.random.split(key, 3)
    shape = (UTTERANCES, SEQ, D)
    noise = jax.random.normal(key_noise, shape, jnp.float32)
    rows = jnp.exp(jax.random.uniform(key_rows, (UTTERANCES, SEQ, 1), jnp.float32, 0.0, 1.2)) / 2.0
    cols = jnp.exp(jax.random.uniform(key_cols, (1, 1, D), jnp.float32, -1.15, 1.15))
    return scaled_field(noise, rows, cols).astype(jnp.bfloat16)


def draw_cotangent(key, part):
    key = jax.random.fold_in(key, 23)
    key_noise, key_rows, key_cols = jax.random.split(key, 3)
    shape = (UTTERANCES, SEQ, D)
    noise = jax.random.normal(key_noise, shape, jnp.float32)
    rows = jnp.exp(jax.random.uniform(key_rows, (UTTERANCES, SEQ, 1), jnp.float32, 0.0, 1.2)) / 2.0
    cols = jnp.exp(jax.random.uniform(key_cols, (1, 1, D), jnp.float32, -1.15, 1.15))
    return scaled_field(noise, rows, cols).astype(jnp.bfloat16)


def block_scale(rng, shape, cuts, smallest, largest):
    gain = 1.0
    for axis_at, shards_of in cuts:
        steps = jax.random.uniform(jax.random.fold_in(jax.random.fold_in(rng, 6), axis_at), (shards_of,), jnp.float32, smallest / len(cuts), largest / len(cuts))
        gain = gain * jnp.repeat(jnp.exp(steps), shape[axis_at] // shards_of).reshape((-1,) + (1,) * (len(shape) - 1 - axis_at))
    return gain


def assign_block(own_key, own, number, rows, amount, top, limit, skew):
    sequence = jax.random.permutation(own_key, amount)
    packed, common = portions_of(amount, rows * top, limit, skew, True), portions_of(amount, rows * top, limit, skew, False)
    places = jnp.arange(amount)

    def named(sizes, turn):
        used = int((sizes > 0).sum())
        fixed = max(1, used // 4)
        moved = fixed + (places - fixed + turn * (used - fixed)) % max(1, amount - fixed)
        return jnp.zeros((amount,), jnp.int32).at[sequence[jnp.where(places < fixed, places, moved)]].set(jnp.asarray(sizes, jnp.int32))

    sizes = jnp.where(number % 4 == 0, named(packed, number // 4), named(common, number - number // 4 - 1))
    mixed = jax.random.permutation(jax.random.fold_in(own, 3), amount)
    source_of, receiver = mixed[0:amount // 2 * 2:2], mixed[1:amount // 2 * 2:2]
    room = jnp.minimum(sizes[source_of] - 1, limit - sizes[receiver]) // 2
    room = jnp.where((source_of == sequence[0]) | (receiver == sequence[0]) | (sizes[receiver] == 0), 0, jnp.maximum(room, 0))
    moved = jax.random.randint(jax.random.fold_in(own, 4), (amount // 2,), 0, 1 << 20) % (room + 1)
    sizes = sizes.at[source_of].add(-moved).at[receiver].add(moved)
    items = jnp.searchsorted(jnp.cumsum(sizes), jnp.arange(rows * top), side="right").astype(jnp.int32)
    table = items.reshape(top, rows).T
    table = table[jax.random.permutation(jax.random.fold_in(own, 1), rows)]
    turn = jax.random.randint(jax.random.fold_in(own, 2), (rows, 1), 0, top)
    return jnp.take_along_axis(table, (jnp.arange(top)[None, :] + turn) % top, axis=1)


def portions_of(amount, total, bound, skew, full):
    weights = [(1 << 20) // math.isqrt(grade ** skew) + 1 for grade in range(1, amount + 1)]
    largest = bound if full else min(bound, max(-(-total // amount), total * weights[0] // sum(weights)))
    least = 1 if total - largest >= amount - 1 else 0
    given, spare = [largest] + [least] * (amount - 1), total - largest - least * (amount - 1)
    while spare > 0:
        free = [i for i in range(1, amount) if given[i] < largest] or [i for i in range(1, amount) if given[i] < bound]
        whole, budget = sum([weights[i] for i in free]), spare
        for i in free:
            extra = min(bound - given[i], max(1, budget * weights[i] // whole), spare)
            given[i] = given[i] + extra
            spare = spare - extra
    return np.array(given)


def centred(stream_key, dims, scale, reach, cuts=(), kind=jnp.bfloat16):
    entries = jax.random.normal(stream_key, dims, jnp.float32) * scale
    if len(cuts) > 0:
        entries = block_scale(stream_key, dims, cuts, -0.22, 0.18) * entries
    return jnp.clip(entries, min=-reach, max=reach).astype(kind)


def setup_inputs(seed: int = 0) -> dict:
    key_list = jax.random.split(jax.random.key(seed), 10)
    frames = draw_frames(jax.random.fold_in(key_list[9], 71), 0)
    taps = centred(key_list[1], (TAPS, D), TAPS ** -0.5, 1.0, (), jnp.float32)
    batchnorm_gain_scale = jnp.clip(1.0 + 0.15 * jax.random.normal(key_list[2], (D,), jnp.float32), 0.25, 1.75)
    batchnorm_shift_bias = centred(key_list[3], (D,), 0.5, 3.0, (), jnp.float32)
    w_router = centred(key_list[4], (D, EXPERTS), (D // 4) ** -0.5, 0.3125)
    w_in = centred(key_list[5], (D, EXPERTS * FF), D ** -0.5, 0.15625, ((1, 64),))
    w_out = centred(key_list[6], (EXPERTS * FF, D), FF ** -0.5, 0.109375, ((0, 64),))
    choices_keys = jax.random.split(jax.random.fold_in(key_list[7], 1), UTTERANCES * SEQ // T_DEV)
    choices_turns = jax.random.permutation(jax.random.fold_in(key_list[7], 3), UTTERANCES * SEQ // T_DEV)
    choices = jax.vmap(lambda own, number: assign_block(jax.random.fold_in(key_list[7], 2), own, number, T_DEV, EXPERTS, TOP, CAP, 1))(choices_keys, choices_turns).reshape((UTTERANCES, SEQ, TOP))
    cotangent = draw_cotangent(jax.random.fold_in(key_list[9], 71), 0)
    return dict(frames=frames, taps=taps, batchnorm_gain_scale=batchnorm_gain_scale, batchnorm_shift_bias=batchnorm_shift_bias, w_router=w_router, w_in=w_in, w_out=w_out, choices=choices, cotangent=cotangent)


EPS = 1e-05
CONTRACT_ROWS = (((0,), (0,)), ((), ()))
CONTRACT_COLS = (((1,), (1,)), ((), ()))

def swish_slope(pre):
    sigma = jax.nn.sigmoid(pre)
    return sigma * (1.0 + pre * (1.0 - sigma))

def rounded_add(total, partial_value):
    kept = lax.optimization_barrier(partial_value.astype(jnp.bfloat16))
    return total + kept.astype(jnp.float32)

def conv_time(signal, taps):
    half = TAPS // 2
    length = signal.shape[1]
    padded = jnp.pad(signal, ((0, 0), (half, half), (0, 0)))
    total = jnp.zeros(signal.shape, jnp.float32)
    for lag in range(TAPS):
        total = total + taps[lag] * padded[:, lag:lag + length, :]
    return (total, padded)

def conv_adjoint(grad, taps):
    half = TAPS // 2
    length = grad.shape[1]
    padded = jnp.pad(grad, ((0, 0), (half, half), (0, 0)))
    total = jnp.zeros(grad.shape, jnp.float32)
    for lag in range(TAPS):
        total = total + taps[lag] * padded[:, 2 * half - lag:2 * half - lag + length, :]
    return total

def expert_rows(rows, w_in_e, w_out_e, group):
    width = w_in_e.shape[1] // group
    output = jnp.zeros((rows.shape[0], D), jnp.float32)
    for block in range(group):
        pre = jnp.dot(rows, w_in_e[:, block * width:(block + 1) * width], preferred_element_type=jnp.float32)
        hidden = jax.nn.silu(pre).astype(jnp.bfloat16)
        output = rounded_add(output, jnp.dot(hidden, w_out_e[block * width:(block + 1) * width], preferred_element_type=jnp.float32))
    return output

def expert_grads(rows, upstream, w_in_e, w_out_e, group):
    width = w_in_e.shape[1] // group
    back = jnp.zeros((rows.shape[0], D), jnp.float32)
    grads_in = []
    grads_out = []
    for block in range(group):
        w_in_b = w_in_e[:, block * width:(block + 1) * width]
        w_out_b = w_out_e[block * width:(block + 1) * width]
        pre = jnp.dot(rows, w_in_b, preferred_element_type=jnp.float32)
        hidden = jax.nn.silu(pre).astype(jnp.bfloat16)
        dhidden = lax.dot_general(upstream, w_out_b, CONTRACT_COLS, preferred_element_type=jnp.float32)
        dpre = (dhidden * swish_slope(pre)).astype(jnp.bfloat16)
        grads_out.append(lax.dot_general(hidden, upstream, CONTRACT_ROWS, preferred_element_type=jnp.float32))
        grads_in.append(lax.dot_general(rows, dpre, CONTRACT_ROWS, preferred_element_type=jnp.float32))
        back = rounded_add(back, lax.dot_general(dpre, w_in_b, CONTRACT_COLS, preferred_element_type=jnp.float32))
    return (back, jnp.concatenate(grads_in, axis=1), jnp.concatenate(grads_out, axis=0))

def reference(frames, taps, batchnorm_gain_scale, batchnorm_shift_bias, w_router, w_in, w_out, choices, cotangent):
    element_count = UTTERANCES * SEQ
    group = N_TM // EXPERTS
    signal = frames.astype(jnp.float32)
    conv, padded = conv_time(signal, taps)
    mean = lax.optimization_barrier(jnp.sum(conv, axis=(0, 1))) / element_count
    centered_values = conv - mean
    inverse_deviation = lax.rsqrt(lax.optimization_barrier(jnp.sum(centered_values * centered_values, axis=(0, 1))) / element_count + EPS)
    normalized_input = centered_values * inverse_deviation
    before_activation = normalized_input * batchnorm_gain_scale + batchnorm_shift_bias
    resid = (signal + jax.nn.silu(before_activation)).reshape(element_count, D)
    lcent = resid - lax.optimization_barrier(jnp.mean(resid, axis=-1, keepdims=True))
    lrstd = lax.rsqrt(lax.optimization_barrier(jnp.mean(lcent * lcent, axis=-1, keepdims=True)) + EPS)
    vhat = lcent * lrstd
    normed = vhat.astype(jnp.bfloat16)
    logits = jnp.dot(normed, w_router, preferred_element_type=jnp.float32)
    ids = choices.reshape(element_count, TOP)
    onehot = (ids[:, :, None] == jnp.arange(EXPERTS, dtype=jnp.int32)[None, None, :]).astype(jnp.float32)
    picked = lax.optimization_barrier(jnp.sum(onehot * logits[:, None, :], axis=-1))
    first = jax.nn.sigmoid(picked[:, 0] - picked[:, 1])
    gates = jnp.stack([first, 1.0 - first], axis=1)
    flat_ids = ids.reshape(-1)
    per_expert = UTTERANCES * N_TM * CAP
    outputs = jnp.zeros((element_count * TOP, D), jnp.float32)
    members = []
    for expert in range(EXPERTS):
        member = jnp.nonzero(flat_ids == expert, size=per_expert)[0].astype(jnp.int32)
        members.append(member)
        w_in_e = w_in[:, expert * FF:(expert + 1) * FF]
        w_out_e = w_out[expert * FF:(expert + 1) * FF]
        outputs = outputs.at[member].set(expert_rows(normed[member // TOP], w_in_e, w_out_e, group))
    expert_out = outputs.reshape(element_count, TOP, D)
    mixed = (resid + lax.optimization_barrier(jnp.sum(gates[:, :, None] * expert_out, axis=1))).astype(jnp.bfloat16)
    upstream = cotangent.reshape(element_count, D).astype(jnp.float32)
    dgate = lax.optimization_barrier(jnp.sum(upstream[:, None, :] * expert_out, axis=-1))
    dpick = (dgate[:, 0] - dgate[:, 1]) * first * (1.0 - first)
    dlogits = (onehot[:, 0] - onehot[:, 1]) * dpick[:, None]
    dnormed = jnp.dot(dlogits, w_router.astype(jnp.float32).T, precision=lax.Precision.HIGHEST)
    sent = (gates[:, :, None] * upstream[:, None, :]).astype(jnp.bfloat16).reshape(element_count * TOP, D)
    back = jnp.zeros((element_count * TOP, D), jnp.float32)
    grads_in = []
    grads_out = []
    for expert in range(EXPERTS):
        member = members[expert]
        w_in_e = w_in[:, expert * FF:(expert + 1) * FF]
        w_out_e = w_out[expert * FF:(expert + 1) * FF]
        back_e, grad_in_e, grad_out_e = expert_grads(normed[member // TOP], sent[member], w_in_e, w_out_e, group)
        back = back.at[member].set(back_e)
        grads_in.append(grad_in_e)
        grads_out.append(grad_out_e)
    dnormed = dnormed + lax.optimization_barrier(jnp.sum(back.reshape(element_count, TOP, D), axis=1))
    dmean = lax.optimization_barrier(jnp.mean(dnormed, axis=-1, keepdims=True))
    dproj = lax.optimization_barrier(jnp.mean(dnormed * vhat, axis=-1, keepdims=True))
    dresid = upstream + lrstd * (dnormed - dmean - vhat * dproj)
    dresid = dresid.reshape(UTTERANCES, SEQ, D)
    normalized_gradient = dresid * swish_slope(before_activation) * batchnorm_gain_scale
    first_moment_sum = lax.optimization_barrier(jnp.sum(normalized_gradient, axis=(0, 1)))
    second_moment_sum = lax.optimization_barrier(jnp.sum(normalized_gradient * normalized_input, axis=(0, 1)))
    convolution_gradient = (inverse_deviation * (normalized_gradient - first_moment_sum / element_count - normalized_input * second_moment_sum / element_count)).astype(jnp.bfloat16)
    dconv_f = convolution_gradient.astype(jnp.float32)
    grad_frames = (dresid + conv_adjoint(dconv_f, taps)).astype(jnp.bfloat16)
    grad_taps = jnp.stack([lax.optimization_barrier(jnp.sum(dconv_f * padded[:, lag:lag + SEQ, :], axis=(0, 1))) for lag in range(TAPS)])
    grad_w_in = jnp.concatenate(grads_in, axis=1)
    grad_w_out = jnp.concatenate(grads_out, axis=0)
    return (mixed.reshape(UTTERANCES, SEQ, D), grad_frames, grad_taps, grad_w_in, grad_w_out)
```

```python
import functools

import jax
import jax.numpy as jnp
from jax import lax
from jax.experimental import pallas as pl
from jax.experimental.pallas import tpu as pltpu
from jax.sharding import PartitionSpec as P

D = 1536
EXPERTS = 8
TOP = 2
TAPS = 31
EPS = 1e-05
NEAR = 16
MESH = pl.DeviceIdType.MESH
CONTRACT_ROWS = (((0,), (0,)), ((), ()))
CONTRACT_COLS = (((1,), (1,)), ((), ()))
EXACT = lax.Precision.HIGHEST


def extended(block, sides, width):
    for axis, dim in sides:
        count = lax.axis_size(axis)
        forward = [(i, i + 1) for i in range(count - 1)]
        backward = [(target, source) for source, target in forward]
        low = lax.ppermute(
            lax.slice_in_dim(block, block.shape[dim] - width, None, axis=dim), axis, forward
        )
        high = lax.ppermute(lax.slice_in_dim(block, 0, width, axis=dim), axis, backward)
        block = jnp.concatenate([low, block, high], axis=dim)
    return block


def swish_slope(pre):
    sigma = jax.nn.sigmoid(pre)
    return sigma * (1.0 + pre * (1.0 - sigma))


def conv_lags(rimmed, taps, length, reverse):
    total = jnp.zeros((length, rimmed.shape[1]), jnp.float32)
    last = taps.shape[0] - 1
    for lag in range(taps.shape[0]):
        start = last - lag if reverse else lag
        total = total + taps[lag] * rimmed[start : start + length]
    return total


class Groups:
    def __init__(self):
        dp_size, tm_size = lax.axis_size("dp"), lax.axis_size("tm")
        self.dp, self.tm = lax.axis_index("dp"), lax.axis_index("tm")
        self.lines = tm_size // NEAR
        self.near_size, self.far_size = NEAR, dp_size * self.lines
        self.near_rank = self.tm % NEAR
        self.far_rank = self.dp * self.lines + self.tm // NEAR

    def near(self, rank):
        return (self.dp, (self.tm // NEAR) * NEAR + rank)

    def far(self, rank):
        return (rank // self.lines, (rank % self.lines) * NEAR + self.near_rank)

    def enter(self):
        barrier = pltpu.get_barrier_semaphore()

        def greet(size, rank, place):
            def step(k, carry):
                pl.semaphore_signal(
                    barrier, inc=1, device_id=place((rank + k) % size), device_id_type=MESH
                )
                return carry

            lax.fori_loop(1, size, step, 0)

        greet(self.near_size, self.near_rank, self.near)
        greet(self.far_size, self.far_rank, self.far)
        pl.semaphore_wait(barrier, self.near_size + self.far_size - 2)


def trade(size, rank, place, source, held, send_sem, recv_sem):
    def copy(k):
        peer = (rank + k) % size
        return pltpu.make_async_remote_copy(
            src_ref=source(peer),
            dst_ref=held.at[rank],
            send_sem=send_sem.at[k],
            recv_sem=recv_sem.at[rank],
            device_id=place(peer),
            device_id_type=MESH,
        )

    def start(k, carry):
        copy(k).start()
        return carry

    def finish(k, carry):
        origin = (rank + k) % size
        pltpu.make_async_remote_copy(
            src_ref=held.at[origin],
            dst_ref=held.at[origin],
            send_sem=send_sem.at[k],
            recv_sem=recv_sem.at[origin],
            device_id=place(origin),
            device_id_type=MESH,
        ).wait_recv()
        return carry

    def sent(k, carry):
        copy(k).wait_send()
        return carry

    lax.fori_loop(1, size, start, 0)
    lax.fori_loop(1, size, finish, 0)
    lax.fori_loop(1, size, sent, 0)


def moments_merge(held, count):
    means = held[:, 0, :]
    mean = jnp.sum(means, axis=0) / means.shape[0]
    spread = means - mean[None]
    squares = jnp.sum(held[:, 1, :], axis=0) + count * jnp.sum(spread * spread, axis=0)
    return mean, squares


def sums_kernel(count, x_ref, o_ref, near_held, far_held, near_send, near_recv, far_send, far_recv):
    groups = Groups()
    near_held[groups.near_rank] = x_ref[...]
    groups.enter()

    def merge(held, parts):
        if count is None:
            return jnp.sum(held[...], axis=0)
        return jnp.stack(moments_merge(held[...], float(parts)))

    mine = near_held.at[groups.near_rank]
    trade(groups.near_size, groups.near_rank, groups.near, lambda p: mine, near_held, near_send, near_recv)
    far_held[groups.far_rank] = merge(near_held, count)
    mine = far_held.at[groups.far_rank]
    trade(groups.far_size, groups.far_rank, groups.far, lambda p: mine, far_held, far_send, far_recv)
    o_ref[...] = merge(far_held, None if count is None else count * groups.near_size)


def all_sums(x, count, collective_id):
    far_size = lax.axis_size("dp") * (lax.axis_size("tm") // NEAR)
    return pl.pallas_call(
        functools.partial(sums_kernel, count),
        out_shape=jax.ShapeDtypeStruct(x.shape, x.dtype),
        in_specs=[pl.BlockSpec(memory_space=pltpu.VMEM)],
        out_specs=pl.BlockSpec(memory_space=pltpu.VMEM),
        scratch_shapes=[
            pltpu.VMEM((NEAR,) + x.shape, x.dtype),
            pltpu.VMEM((far_size,) + x.shape, x.dtype),
            pltpu.SemaphoreType.DMA((NEAR,)),
            pltpu.SemaphoreType.DMA((NEAR,)),
            pltpu.SemaphoreType.DMA((far_size,)),
            pltpu.SemaphoreType.DMA((far_size,)),
        ],
        compiler_params=pltpu.CompilerParams(collective_id=collective_id, has_side_effects=True),
    )(x)


def taps_kernel(
    x_ref, o_ref, near_held, far_held, near_send, near_recv, far_send, far_recv, out_send, out_recv
):
    groups = Groups()
    rank = groups.near_rank
    near_held[rank] = x_ref[rank]
    groups.enter()
    trade(groups.near_size, rank, groups.near, lambda p: x_ref.at[p], near_held, near_send, near_recv)
    far_held[groups.far_rank] = jnp.sum(near_held[...], axis=0)
    mine = far_held.at[groups.far_rank]
    trade(groups.far_size, groups.far_rank, groups.far, lambda p: mine, far_held, far_send, far_recv)
    o_ref[rank] = jnp.sum(far_held[...], axis=0)
    done = o_ref.at[rank]
    trade(groups.near_size, rank, groups.near, lambda p: done, o_ref, out_send, out_recv)


def taps_sum(x, collective_id):
    far_size = lax.axis_size("dp") * (lax.axis_size("tm") // NEAR)
    padded = jnp.pad(x, ((0, 2 * NEAR - x.shape[0]), (0, 0))).reshape(NEAR, 2, x.shape[1])
    total = pl.pallas_call(
        taps_kernel,
        out_shape=jax.ShapeDtypeStruct(padded.shape, padded.dtype),
        in_specs=[pl.BlockSpec(memory_space=pltpu.VMEM)],
        out_specs=pl.BlockSpec(memory_space=pltpu.VMEM),
        scratch_shapes=[
            pltpu.VMEM(padded.shape, padded.dtype),
            pltpu.VMEM((far_size,) + padded.shape[1:], padded.dtype),
            pltpu.SemaphoreType.DMA((NEAR,)),
            pltpu.SemaphoreType.DMA((NEAR,)),
            pltpu.SemaphoreType.DMA((far_size,)),
            pltpu.SemaphoreType.DMA((far_size,)),
            pltpu.SemaphoreType.DMA((NEAR,)),
            pltpu.SemaphoreType.DMA((NEAR,)),
        ],
        compiler_params=pltpu.CompilerParams(collective_id=collective_id, has_side_effects=True),
    )(padded)
    return total.reshape(2 * NEAR, x.shape[1])[: x.shape[0]]


def to_experts(buffer):
    tm_size = lax.axis_size("tm")
    group = tm_size // EXPERTS
    capacity = buffer.shape[1]
    width = buffer.shape[2]
    copies = jnp.repeat(buffer, group, axis=0)
    received = lax.all_to_all(copies, "tm", split_axis=0, concat_axis=0, tiled=True)
    return received.reshape(tm_size * capacity, width)


def return_sums(partial_value, capacity):
    tm_size = lax.axis_size("tm")
    group = tm_size // EXPERTS
    width = partial_value.shape[1]
    returned = lax.all_to_all(
        partial_value.reshape(tm_size, capacity, width),
        "tm",
        split_axis=0,
        concat_axis=0,
        tiled=True,
    )
    return jnp.sum(returned.reshape(EXPERTS, group, capacity, width).astype(jnp.float32), axis=1)


def body(
    frames,
    taps,
    batchnorm_gain_scale,
    batchnorm_shift_bias,
    w_router,
    w_in,
    w_out,
    choices,
    cotangent,
):
    length = frames.shape[1]
    half = TAPS // 2
    element_count = lax.axis_size("dp") * lax.axis_size("tm") * length
    capacity = length * TOP // EXPERTS
    signal = frames[0].astype(jnp.float32)
    rimmed = extended(frames, (("tm", 1),), half)[0].astype(jnp.float32)
    conv = conv_lags(rimmed, taps, length, False)
    local_mean = jnp.sum(conv, axis=0) / length
    local_spread = conv - local_mean
    moments = all_sums(
        jnp.stack([local_mean, jnp.sum(local_spread * local_spread, axis=0)]), length, 0
    )
    mean, variance = moments[0], moments[1] / element_count
    centered_values = conv - mean
    inverse_deviation = lax.rsqrt(variance + EPS)
    normalized_input = centered_values * inverse_deviation
    before_activation = normalized_input * batchnorm_gain_scale + batchnorm_shift_bias
    resid = signal + jax.nn.silu(before_activation)
    lcent = resid - jnp.mean(resid, axis=-1, keepdims=True)
    lrstd = lax.rsqrt(jnp.mean(lcent * lcent, axis=-1, keepdims=True) + EPS)
    vhat = lcent * lrstd
    normed = vhat.astype(jnp.bfloat16)
    logits = jnp.dot(normed, w_router, preferred_element_type=jnp.float32)
    ids = choices[0]
    onehot = (ids[:, :, None] == jnp.arange(EXPERTS, dtype=jnp.int32)[None, None, :]).astype(
        jnp.float32
    )
    picked = jnp.sum(onehot * logits[:, None, :], axis=-1)
    first = jax.nn.sigmoid(picked[:, 0] - picked[:, 1])
    gates = jnp.stack([first, 1.0 - first], axis=1)
    flat_ids = ids.reshape(-1)
    expert_hot = (flat_ids[:, None] == jnp.arange(EXPERTS, dtype=jnp.int32)[None, :]).astype(
        jnp.int32
    )
    slots = jnp.sum((jnp.cumsum(expert_hot, axis=0) - 1) * expert_hot, axis=1)
    places = (flat_ids * capacity + slots).reshape(length, TOP)
    place_hot = places[:, :, None] == jnp.arange(EXPERTS * capacity, dtype=jnp.int32)[None, None, :]
    place_any = jnp.any(place_hot, axis=1).astype(jnp.bfloat16)
    place_hot = place_hot.astype(jnp.float32)
    gate_rows = jnp.sum(place_hot * gates[:, :, None], axis=(0, 1))

    def bucketed(rows):
        return lax.dot_general(place_any, rows, CONTRACT_ROWS, preferred_element_type=jnp.float32)

    buffer = bucketed(normed).astype(jnp.bfloat16).reshape(EXPERTS, capacity, D)
    sent_buffer = (gate_rows[:, None] * bucketed(cotangent[0])).astype(jnp.bfloat16)
    rows = to_experts(buffer)
    upstream_rows = to_experts(sent_buffer.reshape(EXPERTS, capacity, D))
    pre = jnp.dot(rows, w_in, preferred_element_type=jnp.float32)
    hidden = jax.nn.silu(pre).astype(jnp.bfloat16)
    partial_value = jnp.dot(hidden, w_out, preferred_element_type=jnp.float32).astype(jnp.bfloat16)
    combined = return_sums(partial_value, capacity).reshape(EXPERTS * capacity, D)
    expert_out = [
        jnp.dot(place_hot[:, k], combined, precision=EXACT) for k in range(TOP)
    ]
    mixed = (resid + sum(gates[:, k, None] * expert_out[k] for k in range(TOP))).astype(jnp.bfloat16)
    upstream = cotangent[0].astype(jnp.float32)
    dgate = [jnp.sum(upstream * expert_out[k], axis=-1) for k in range(TOP)]
    dpick = (dgate[0] - dgate[1]) * first * (1.0 - first)
    dlogits = (onehot[:, 0] - onehot[:, 1]) * dpick[:, None]
    dnormed = jnp.dot(dlogits, w_router.astype(jnp.float32).T, precision=EXACT)
    dhidden = lax.dot_general(
        upstream_rows, w_out, CONTRACT_COLS, preferred_element_type=jnp.float32
    )
    dpre = (dhidden * swish_slope(pre)).astype(jnp.bfloat16)
    grad_in_local = lax.dot_general(rows, dpre, CONTRACT_ROWS, preferred_element_type=jnp.float32)
    grad_out_local = lax.dot_general(
        hidden, upstream_rows, CONTRACT_ROWS, preferred_element_type=jnp.float32
    )
    back_rows = lax.dot_general(
        dpre, w_in, CONTRACT_COLS, preferred_element_type=jnp.float32
    ).astype(jnp.bfloat16)
    back = return_sums(back_rows, capacity).reshape(EXPERTS * capacity, D)
    dnormed = dnormed + jnp.dot(jnp.sum(place_hot, axis=1), back, precision=EXACT)
    dmean = jnp.mean(dnormed, axis=-1, keepdims=True)
    dproj = jnp.mean(dnormed * vhat, axis=-1, keepdims=True)
    dresid = upstream + lrstd * (dnormed - dmean - vhat * dproj)
    normalized_gradient = dresid * swish_slope(before_activation) * batchnorm_gain_scale
    moment_sums = all_sums(
        jnp.stack(
            [
                jnp.sum(normalized_gradient, axis=0),
                jnp.sum(normalized_gradient * normalized_input, axis=0),
            ]
        ),
        None,
        1,
    )
    convolution_gradient = (
        inverse_deviation
        * (
            normalized_gradient
            - moment_sums[0] / element_count
            - normalized_input * moment_sums[1] / element_count
        )
    ).astype(jnp.bfloat16)
    grad_rimmed = extended(convolution_gradient[None], (("tm", 1),), half)[0].astype(jnp.float32)
    grad_frames = (dresid + conv_lags(grad_rimmed, taps, length, True)).astype(jnp.bfloat16)
    dconv_f = convolution_gradient.astype(jnp.float32)
    local_taps = jnp.stack(
        [jnp.sum(dconv_f * rimmed[lag : lag + length], axis=0) for lag in range(TAPS)]
    )
    grad_taps = taps_sum(local_taps, 2)
    grad_w_in, grad_w_out = (
        lax.psum_scatter(grad_in_local, "dp", scatter_dimension=0, tiled=True),
        lax.psum_scatter(grad_out_local, "dp", scatter_dimension=1, tiled=True),
    )
    return (mixed[None], grad_frames[None], grad_taps, grad_w_in, grad_w_out)


def solution(mesh):
    return jax.shard_map(
        body,
        mesh=mesh,
        in_specs=(
            P("dp", "tm", None),
            P(),
            P(),
            P(),
            P(),
            P(None, "tm"),
            P("tm", None),
            P("dp", "tm", None),
            P("dp", "tm", None),
        ),
        out_specs=(P("dp", "tm", None), P("dp", "tm", None), P(), P("dp", "tm"), P("tm", "dp")),
        check_vma=False,
    )
```

```python
import functools

import jax
import jax.numpy as jnp
from jax import lax
from jax.experimental import pallas as pl
from jax.experimental.pallas import tpu as pltpu
from jax.sharding import PartitionSpec as P

D = 1536
EXPERTS = 8
TOP = 2
TAPS = 31
EPS = 1e-05
NEAR = 16
MESH = pl.DeviceIdType.MESH
CONTRACT_ROWS = (((0,), (0,)), ((), ()))
CONTRACT_COLS = (((1,), (1,)), ((), ()))
EXACT = lax.Precision.HIGHEST


def extended(block, sides, width):
    for axis, dim in sides:
        count = lax.axis_size(axis)
        forward = [(i, i + 1) for i in range(count - 1)]
        backward = [(target, source) for source, target in forward]
        low = lax.ppermute(
            lax.slice_in_dim(block, block.shape[dim] - width, None, axis=dim), axis, forward
        )
        high = lax.ppermute(lax.slice_in_dim(block, 0, width, axis=dim), axis, backward)
        block = jnp.concatenate([low, block, high], axis=dim)
    return block


def swish_slope(pre):
    sigma = jax.nn.sigmoid(pre)
    return sigma * (1.0 + pre * (1.0 - sigma))


def conv_lags(rimmed, taps, length, reverse):
    total = jnp.zeros((length, rimmed.shape[1]), jnp.float32)
    last = taps.shape[0] - 1
    for lag in range(taps.shape[0]):
        start = last - lag if reverse else lag
        total = total + taps[lag] * rimmed[start : start + length]
    return total


class Groups:
    def __init__(self):
        dp_size, tm_size = lax.axis_size("dp"), lax.axis_size("tm")
        self.dp, self.tm = lax.axis_index("dp"), lax.axis_index("tm")
        self.lines = tm_size // NEAR
        self.near_size, self.far_size = NEAR, dp_size * self.lines
        self.near_rank = self.tm % NEAR
        self.far_rank = self.dp * self.lines + self.tm // NEAR

    def near(self, rank):
        return (self.dp, (self.tm // NEAR) * NEAR + rank)

    def far(self, rank):
        return (rank // self.lines, (rank % self.lines) * NEAR + self.near_rank)

    def enter(self):
        barrier = pltpu.get_barrier_semaphore()

        def greet(size, rank, place):
            def step(k, carry):
                pl.semaphore_signal(
                    barrier, inc=1, device_id=place((rank + k) % size), device_id_type=MESH
                )
                return carry

            lax.fori_loop(1, size, step, 0)

        greet(self.near_size, self.near_rank, self.near)
        greet(self.far_size, self.far_rank, self.far)
        pl.semaphore_wait(barrier, self.near_size + self.far_size - 2)


def trade(size, rank, place, source, held, send_sem, recv_sem):
    def copy(k):
        peer = (rank + k) % size
        return pltpu.make_async_remote_copy(
            src_ref=source(peer),
            dst_ref=held.at[rank],
            send_sem=send_sem.at[k],
            recv_sem=recv_sem.at[rank],
            device_id=place(peer),
            device_id_type=MESH,
        )

    def start(k, carry):
        copy(k).start()
        return carry

    def finish(k, carry):
        origin = (rank + k) % size
        pltpu.make_async_remote_copy(
            src_ref=held.at[origin],
            dst_ref=held.at[origin],
            send_sem=send_sem.at[k],
            recv_sem=recv_sem.at[origin],
            device_id=place(origin),
            device_id_type=MESH,
        ).wait_recv()
        return carry

    def sent(k, carry):
        copy(k).wait_send()
        return carry

    lax.fori_loop(1, size, start, 0)
    lax.fori_loop(1, size, finish, 0)
    lax.fori_loop(1, size, sent, 0)


def moments_merge(held, count):
    means = held[:, 0, :]
    mean = jnp.sum(means, axis=0) / means.shape[0]
    spread = means - mean[None]
    squares = jnp.sum(held[:, 1, :], axis=0) + count * jnp.sum(spread * spread, axis=0)
    return mean, squares


def sums_kernel(count, x_ref, o_ref, near_held, far_held, near_send, near_recv, far_send, far_recv):
    groups = Groups()
    near_held[groups.near_rank] = x_ref[...]
    groups.enter()

    def merge(held, parts):
        if count is None:
            return jnp.sum(held[...], axis=0)
        return jnp.stack(moments_merge(held[...], float(parts)))

    mine = near_held.at[groups.near_rank]
    trade(groups.near_size, groups.near_rank, groups.near, lambda p: mine, near_held, near_send, near_recv)
    far_held[groups.far_rank] = merge(near_held, count)
    mine = far_held.at[groups.far_rank]
    trade(groups.far_size, groups.far_rank, groups.far, lambda p: mine, far_held, far_send, far_recv)
    o_ref[...] = merge(far_held, None if count is None else count * groups.near_size)


def all_sums(x, count, collective_id):
    far_size = lax.axis_size("dp") * (lax.axis_size("tm") // NEAR)
    return pl.pallas_call(
        functools.partial(sums_kernel, count),
        out_shape=jax.ShapeDtypeStruct(x.shape, x.dtype),
        in_specs=[pl.BlockSpec(memory_space=pltpu.VMEM)],
        out_specs=pl.BlockSpec(memory_space=pltpu.VMEM),
        scratch_shapes=[
            pltpu.VMEM((NEAR,) + x.shape, x.dtype),
            pltpu.VMEM((far_size,) + x.shape, x.dtype),
            pltpu.SemaphoreType.DMA((NEAR,)),
            pltpu.SemaphoreType.DMA((NEAR,)),
            pltpu.SemaphoreType.DMA((far_size,)),
            pltpu.SemaphoreType.DMA((far_size,)),
        ],
        compiler_params=pltpu.CompilerParams(collective_id=collective_id, has_side_effects=True),
    )(x)


def taps_kernel(
    x_ref, o_ref, near_held, far_held, near_send, near_recv, far_send, far_recv, out_send, out_recv
):
    groups = Groups()
    rank = groups.near_rank
    near_held[rank] = x_ref[rank]
    groups.enter()
    trade(groups.near_size, rank, groups.near, lambda p: x_ref.at[p], near_held, near_send, near_recv)
    far_held[groups.far_rank] = jnp.sum(near_held[...], axis=0)
    mine = far_held.at[groups.far_rank]
    trade(groups.far_size, groups.far_rank, groups.far, lambda p: mine, far_held, far_send, far_recv)
    o_ref[rank] = jnp.sum(far_held[...], axis=0)
    done = o_ref.at[rank]
    trade(groups.near_size, rank, groups.near, lambda p: done, o_ref, out_send, out_recv)


def taps_sum(x, collective_id):
    far_size = lax.axis_size("dp") * (lax.axis_size("tm") // NEAR)
    padded = jnp.pad(x, ((0, 2 * NEAR - x.shape[0]), (0, 0))).reshape(NEAR, 2, x.shape[1])
    total = pl.pallas_call(
        taps_kernel,
        out_shape=jax.ShapeDtypeStruct(padded.shape, padded.dtype),
        in_specs=[pl.BlockSpec(memory_space=pltpu.VMEM)],
        out_specs=pl.BlockSpec(memory_space=pltpu.VMEM),
        scratch_shapes=[
            pltpu.VMEM(padded.shape, padded.dtype),
            pltpu.VMEM((far_size,) + padded.shape[1:], padded.dtype),
            pltpu.SemaphoreType.DMA((NEAR,)),
            pltpu.SemaphoreType.DMA((NEAR,)),
            pltpu.SemaphoreType.DMA((far_size,)),
            pltpu.SemaphoreType.DMA((far_size,)),
            pltpu.SemaphoreType.DMA((NEAR,)),
            pltpu.SemaphoreType.DMA((NEAR,)),
        ],
        compiler_params=pltpu.CompilerParams(collective_id=collective_id, has_side_effects=True),
    )(padded)
    return total.reshape(2 * NEAR, x.shape[1])[: x.shape[0]]


CORES = 2
LINES = 4
ZEDS = EXPERTS
SPAN = ZEDS * CORES
HALF = ZEDS // 2
TURN = ((3, 1, 0, 2), (1, 3, 2, 0), (0, 2, 1, 3), (2, 0, 3, 1))
SWEEP = (0, 1, 7, 2, 6, 3, 5, 4)


def position(ids):
    return HALF * (ids % 2) + ids // 2


def home_to_work():
    pairs = []
    for y in range(LINES):
        for z in range(ZEDS):
            line, half = z % HALF, z // HALF
            source_z = HALF * half + TURN[y][line]
            for core in range(CORES):
                pairs.append((line * SPAN + source_z * CORES + core, y * SPAN + z * CORES + core))
    return pairs


class Place:
    def __init__(self):
        self.dp, tm = lax.axis_index("dp"), lax.axis_index("tm")
        self.core, self.z, self.y = tm % CORES, (tm // CORES) % ZEDS, tm // SPAN

    def at(self, y, z, core):
        return (self.dp, (y % LINES) * SPAN + z * CORES + core)

    def sibling(self):
        return self.at(self.y, self.z, 1 - self.core)

    def line(self, step):
        return self.at(self.y + step + LINES, self.z, self.core)

    def zed(self, z):
        return self.at(self.y, z, self.core)

    def enter(self):
        barrier = pltpu.get_barrier_semaphore()
        peers = [self.sibling(), self.line(1), self.line(-1)]
        peers += [self.zed((self.z + k) % ZEDS) for k in range(1, ZEDS)]
        for peer in peers:
            pl.semaphore_signal(barrier, inc=1, device_id=peer, device_id_type=MESH)
        pl.semaphore_wait(barrier, len(peers))


def remote(source, target, send_sem, recv_sem, device):
    return pltpu.make_async_remote_copy(
        src_ref=source,
        dst_ref=target,
        send_sem=send_sem,
        recv_sem=recv_sem,
        device_id=device,
        device_id_type=MESH,
    )


def dispatch_kernel(
    x_ref, u_ref, rx_ref, ru_ref, own_sem, z_send, z_recv, pair_send, pair_recv, y_send, y_recv
):
    place = Place()
    y, z, core = place.y, place.z, place.core
    arrays = ((x_ref, rx_ref), (u_ref, ru_ref))
    place.enter()
    waits = []

    def z_copy(a, k):
        source, rows = arrays[a]
        target = (z + k) % ZEDS
        return remote(
            source.at[target], rows.at[core, y, z], z_send.at[a, k], z_recv.at[a, k], place.zed(target)
        )

    def own_copy(a):
        source, rows = arrays[a]
        return pltpu.make_async_copy(source.at[z], rows.at[core, y, z], own_sem.at[a])

    def block(a, from_core, step, k):
        return arrays[a][1].at[from_core, (y + step + LINES) % LINES, (z - k + ZEDS) % ZEDS]

    def pass_on(a, step, k, send_sem, recv_sem, device):
        ref = block(a, core, step, k)
        copy = remote(ref, ref, send_sem, recv_sem, device)
        copy.start()
        waits.append(copy)

    def arrived(a, from_core, step, k, send_sem, recv_sem):
        ref = block(a, from_core, step, k)
        remote(ref, ref, send_sem, recv_sem, place.sibling()).wait_recv()

    def to_pair(a, step, k):
        index = step % LINES * ZEDS + k
        pass_on(a, step, k, pair_send.at[a, index], pair_recv.at[a, index], place.sibling())

    for a in range(2):
        own_copy(a).start()
        for k in SWEEP[1:]:
            z_copy(a, k).start()
    items = [(a, i, k) for a in range(2) for i, k in enumerate(SWEEP)]
    for m in range(len(items) + 4):
        if m < len(items):
            a, i, k = items[m]
            if k == 0:
                own_copy(a).wait()
            else:
                arrived(a, core, 0, k, z_send.at[a, k], z_recv.at[a, k])
            for way, step in ((0, 1), (1, -1)):
                pass_on(a, 0, k, y_send.at[a, way, k], y_recv.at[a, way, k], place.line(step))
            to_pair(a, 0, k)
        if 0 <= m - 2 < len(items):
            a, i, k = items[m - 2]
            for way, step in ((0, 1), (1, -1)):
                arrived(a, core, -step, k, y_send.at[a, way, k], y_recv.at[a, way, k])
                if i % 2 == way:
                    pass_on(a, -step, k, y_send.at[a, 2, k], y_recv.at[a, 2, k], place.line(step))
                to_pair(a, -step, k)
        if m >= 4:
            a, i, k = items[m - 4]
            arrived(a, core, 2, k, y_send.at[a, 2, k], y_recv.at[a, 2, k])
            to_pair(a, 2, k)
    for a in range(2):
        for step in range(LINES):
            for k in range(ZEDS):
                index = step * ZEDS + k
                arrived(a, 1 - core, step, k, pair_send.at[a, index], pair_recv.at[a, index])
    for a in range(2):
        for k in SWEEP[1:]:
            z_copy(a, k).wait_send()
    for copy in waits:
        copy.wait_send()


def dispatch(x, u, collective_id):
    rows = jax.ShapeDtypeStruct((CORES, LINES) + x.shape, x.dtype)
    dma = pltpu.SemaphoreType.DMA
    return pl.pallas_call(
        dispatch_kernel,
        out_shape=(rows, rows),
        in_specs=[pl.BlockSpec(memory_space=pl.ANY)] * 2,
        out_specs=[pl.BlockSpec(memory_space=pl.ANY)] * 2,
        scratch_shapes=[
            dma((2,)),
            dma((2, ZEDS)),
            dma((2, ZEDS)),
            dma((2, LINES * ZEDS)),
            dma((2, LINES * ZEDS)),
            dma((2, 3, ZEDS)),
            dma((2, 3, ZEDS)),
        ],
        compiler_params=pltpu.CompilerParams(collective_id=collective_id, has_side_effects=True),
    )(x, u)


PIECES = ((2, 0, 1, None), (2, 1, -1, None), (1, 1, 1, None), (-1, 0, -1, None), (1, 0, 1, 0), (-1, 1, -1, 1))
PAIR_ORDER = ((2, 0), (2, 1), (1, 1), (3, 0), (1, 0), (3, 1), (0, 0), (0, 1))


def return_kernel(
    p0_ref,
    p1_ref,
    o0_ref,
    o1_ref,
    pair_held,
    leaving,
    line_held,
    total,
    pair_send,
    pair_recv,
    y_send,
    y_recv,
    z_send,
    z_recv,
):
    place = Place()
    y, z, core = place.y, place.z, place.core
    arrays = ((p0_ref, o0_ref), (p1_ref, o1_ref))
    place.enter()

    def pair_copy(a, step, half):
        source = arrays[a][0].at[1 - core, (y + step) % LINES, pl.ds(half * HALF, HALF)]
        return remote(
            source,
            pair_held.at[a, step, half],
            pair_send.at[a, step, half],
            pair_recv.at[a, step, half],
            place.sibling(),
        )

    def y_copy(a, piece):
        return remote(
            leaving.at[a, piece],
            line_held.at[a, piece],
            y_send.at[a, piece],
            y_recv.at[a, piece],
            place.line(PIECES[piece][2]),
        )

    def z_copy(a, target):
        return remote(
            total.at[a, target], arrays[a][1].at[z], z_send.at[a, target], z_recv.at[a, z], place.zed(target)
        )

    def add_up(a, step, half, pieces, store):
        pair_copy(a, step, half).wait_recv()

        def one(i, carry):
            value = arrays[a][0][core, (y + step) % LINES, half * HALF + i].astype(jnp.float32)
            value = value + pair_held[a, step, half, i].astype(jnp.float32)
            for piece in pieces:
                value = value + line_held[a, piece, i].astype(jnp.float32)
            store(i, value.astype(jnp.bfloat16))
            return carry

        lax.fori_loop(0, HALF, one, 0)

    def send_piece(a, piece):
        step, half, _, extra = PIECES[piece]
        if extra is not None:
            y_copy(a, extra).wait_recv()

        def store(i, value):
            leaving[a, piece, i] = value

        add_up(a, step % LINES, half, () if extra is None else (extra,), store)
        y_copy(a, piece).start()

    def finish(a, half):
        pieces = (4, 3) if half == 0 else (2, 5)
        for piece in pieces:
            y_copy(a, piece).wait_recv()

        def store(i, value):
            total[a, half * HALF + i] = value

        add_up(a, 0, half, pieces, store)
        for i in range(HALF):
            target = half * HALF + i

            @pl.when(target != z)
            def _():
                z_copy(a, target).start()

            @pl.when(target == z)
            def _():
                arrays[a][1][target] = total[a, target]

    for a in range(2):
        for step, half in PAIR_ORDER:
            pair_copy(a, step, half).start()
    for piece in range(4):
        send_piece(0, piece)
    for piece in range(2):
        send_piece(1, piece)
    for piece in range(4, 6):
        send_piece(0, piece)
    for piece in range(2, 4):
        send_piece(1, piece)
    for half in range(2):
        finish(0, half)
    for piece in range(4, 6):
        send_piece(1, piece)
    for half in range(2):
        finish(1, half)
    for a in range(2):
        for k in range(1, ZEDS):
            other = (z + k) % ZEDS
            remote(
                total.at[a, other], arrays[a][1].at[other], z_send.at[a, other], z_recv.at[a, other], place.zed(other)
            ).wait_recv()
    for a in range(2):
        for step, half in PAIR_ORDER:
            pair_copy(a, step, half).wait_send()
        for piece in range(len(PIECES)):
            y_copy(a, piece).wait_send()
        for k in range(1, ZEDS):
            z_copy(a, (z + k) % ZEDS).wait_send()


def give_back(p0, p1, collective_id):
    tile = p0.shape[3:]
    out = jax.ShapeDtypeStruct((ZEDS,) + tile, p0.dtype)
    dma = pltpu.SemaphoreType.DMA
    return pl.pallas_call(
        return_kernel,
        out_shape=(out, out),
        in_specs=[pl.BlockSpec(memory_space=pltpu.VMEM)] * 2,
        out_specs=[pl.BlockSpec(memory_space=pltpu.VMEM)] * 2,
        scratch_shapes=[
            pltpu.VMEM((2, LINES, 2, HALF) + tile, p0.dtype),
            pltpu.VMEM((2, len(PIECES), HALF) + tile, p0.dtype),
            pltpu.VMEM((2, len(PIECES), HALF) + tile, p0.dtype),
            pltpu.VMEM((2, ZEDS) + tile, p0.dtype),
            dma((2, LINES, 2)),
            dma((2, LINES, 2)),
            dma((2, len(PIECES))),
            dma((2, len(PIECES))),
            dma((2, ZEDS)),
            dma((2, ZEDS)),
        ],
        compiler_params=pltpu.CompilerParams(
            collective_id=collective_id, has_side_effects=True, vmem_limit_bytes=48 << 20
        ),
    )(p0, p1)


def body(
    frames,
    taps,
    batchnorm_gain_scale,
    batchnorm_shift_bias,
    w_router,
    w_in,
    w_out,
    choices,
    cotangent,
):
    length = frames.shape[1]
    half = TAPS // 2
    moves = home_to_work()
    w_in = lax.ppermute(w_in, "tm", moves)
    w_out = lax.ppermute(w_out, "tm", moves)
    element_count = lax.axis_size("dp") * lax.axis_size("tm") * length
    capacity = length * TOP // EXPERTS
    signal = frames[0].astype(jnp.float32)
    rimmed = extended(frames, (("tm", 1),), half)[0].astype(jnp.float32)
    conv = conv_lags(rimmed, taps, length, False)
    local_mean = jnp.sum(conv, axis=0) / length
    local_spread = conv - local_mean
    moments = all_sums(
        jnp.stack([local_mean, jnp.sum(local_spread * local_spread, axis=0)]), length, 0
    )
    mean, variance = moments[0], moments[1] / element_count
    centered_values = conv - mean
    inverse_deviation = lax.rsqrt(variance + EPS)
    normalized_input = centered_values * inverse_deviation
    before_activation = normalized_input * batchnorm_gain_scale + batchnorm_shift_bias
    resid = signal + jax.nn.silu(before_activation)
    lcent = resid - jnp.mean(resid, axis=-1, keepdims=True)
    lrstd = lax.rsqrt(jnp.mean(lcent * lcent, axis=-1, keepdims=True) + EPS)
    vhat = lcent * lrstd
    normed = vhat.astype(jnp.bfloat16)
    logits = jnp.dot(normed, w_router, preferred_element_type=jnp.float32)
    ids = choices[0]
    onehot = (ids[:, :, None] == jnp.arange(EXPERTS, dtype=jnp.int32)[None, None, :]).astype(
        jnp.float32
    )
    picked = jnp.sum(onehot * logits[:, None, :], axis=-1)
    first = jax.nn.sigmoid(picked[:, 0] - picked[:, 1])
    gates = jnp.stack([first, 1.0 - first], axis=1)
    flat_ids = ids.reshape(-1)
    expert_hot = (flat_ids[:, None] == jnp.arange(EXPERTS, dtype=jnp.int32)[None, :]).astype(
        jnp.int32
    )
    slots = jnp.sum((jnp.cumsum(expert_hot, axis=0) - 1) * expert_hot, axis=1)
    places = (position(flat_ids) * capacity + slots).reshape(length, TOP)
    place_hot = places[:, :, None] == jnp.arange(EXPERTS * capacity, dtype=jnp.int32)[None, None, :]
    place_any = jnp.any(place_hot, axis=1).astype(jnp.bfloat16)
    place_hot = place_hot.astype(jnp.float32)
    gate_rows = jnp.sum(place_hot * gates[:, :, None], axis=(0, 1))

    def bucketed(rows):
        return lax.dot_general(place_any, rows, CONTRACT_ROWS, preferred_element_type=jnp.float32)

    buffer = bucketed(normed).astype(jnp.bfloat16).reshape(EXPERTS, capacity, D)
    sent_buffer = (gate_rows[:, None] * bucketed(cotangent[0])).astype(jnp.bfloat16)
    sent_buffer = sent_buffer.reshape(EXPERTS, capacity, D)
    rows, upstream_rows = dispatch(buffer, sent_buffer, 3)
    rows_shape = rows.shape
    rows, upstream_rows = rows.reshape(-1, D), upstream_rows.reshape(-1, D)
    pre = jnp.dot(rows, w_in, preferred_element_type=jnp.float32)
    hidden = jax.nn.silu(pre).astype(jnp.bfloat16)
    partial_value = jnp.dot(hidden, w_out, preferred_element_type=jnp.float32).astype(jnp.bfloat16)
    dhidden = lax.dot_general(
        upstream_rows, w_out, CONTRACT_COLS, preferred_element_type=jnp.float32
    )
    dpre = (dhidden * swish_slope(pre)).astype(jnp.bfloat16)
    back_rows = lax.dot_general(
        dpre, w_in, CONTRACT_COLS, preferred_element_type=jnp.float32
    ).astype(jnp.bfloat16)
    grad_in_local = lax.dot_general(rows, dpre, CONTRACT_ROWS, preferred_element_type=jnp.float32)
    grad_out_local = lax.dot_general(
        hidden, upstream_rows, CONTRACT_ROWS, preferred_element_type=jnp.float32
    )
    combined, back = give_back(partial_value.reshape(rows_shape), back_rows.reshape(rows_shape), 4)
    combined = combined.reshape(EXPERTS * capacity, D).astype(jnp.float32)
    back = back.reshape(EXPERTS * capacity, D).astype(jnp.float32)
    expert_out = [
        jnp.dot(place_hot[:, k], combined, precision=EXACT) for k in range(TOP)
    ]
    mixed = (resid + sum(gates[:, k, None] * expert_out[k] for k in range(TOP))).astype(jnp.bfloat16)
    upstream = cotangent[0].astype(jnp.float32)
    dgate = [jnp.sum(upstream * expert_out[k], axis=-1) for k in range(TOP)]
    dpick = (dgate[0] - dgate[1]) * first * (1.0 - first)
    dlogits = (onehot[:, 0] - onehot[:, 1]) * dpick[:, None]
    dnormed = jnp.dot(dlogits, w_router.astype(jnp.float32).T, precision=EXACT)
    dnormed = dnormed + jnp.dot(jnp.sum(place_hot, axis=1), back, precision=EXACT)
    dmean = jnp.mean(dnormed, axis=-1, keepdims=True)
    dproj = jnp.mean(dnormed * vhat, axis=-1, keepdims=True)
    dresid = upstream + lrstd * (dnormed - dmean - vhat * dproj)
    normalized_gradient = dresid * swish_slope(before_activation) * batchnorm_gain_scale
    moment_sums = all_sums(
        jnp.stack(
            [
                jnp.sum(normalized_gradient, axis=0),
                jnp.sum(normalized_gradient * normalized_input, axis=0),
            ]
        ),
        None,
        1,
    )
    convolution_gradient = (
        inverse_deviation
        * (
            normalized_gradient
            - moment_sums[0] / element_count
            - normalized_input * moment_sums[1] / element_count
        )
    ).astype(jnp.bfloat16)
    grad_rimmed = extended(convolution_gradient[None], (("tm", 1),), half)[0].astype(jnp.float32)
    grad_frames = (dresid + conv_lags(grad_rimmed, taps, length, True)).astype(jnp.bfloat16)
    dconv_f = convolution_gradient.astype(jnp.float32)
    local_taps = jnp.stack(
        [jnp.sum(dconv_f * rimmed[lag : lag + length], axis=0) for lag in range(TAPS)]
    )
    grad_taps = taps_sum(local_taps, 2)
    returns = [(target, source) for source, target in moves]
    grad_w_in, grad_w_out = (
        lax.psum_scatter(grad_in_local, "dp", scatter_dimension=0, tiled=True),
        lax.psum_scatter(grad_out_local, "dp", scatter_dimension=1, tiled=True),
    )
    grad_w_in = lax.ppermute(grad_w_in, "tm", returns)
    grad_w_out = lax.ppermute(grad_w_out, "tm", returns)
    return (mixed[None], grad_frames[None], grad_taps, grad_w_in, grad_w_out)


def solution(mesh):
    return jax.shard_map(
        body,
        mesh=mesh,
        in_specs=(
            P("dp", "tm", None),
            P(),
            P(),
            P(),
            P(),
            P(None, "tm"),
            P("tm", None),
            P("dp", "tm", None),
            P("dp", "tm", None),
        ),
        out_specs=(P("dp", "tm", None), P("dp", "tm", None), P(), P("dp", "tm"), P("tm", "dp")),
        check_vma=False,
    )
```

```python
import functools

import jax
import jax.numpy as jnp
from jax import lax
from jax.experimental import pallas as pl
from jax.experimental.pallas import tpu as pltpu
from jax.sharding import PartitionSpec as P

D = 1536
EXPERTS = 8
TOP = 2
TAPS = 31
EPS = 1e-05
NEAR = 16
MESH = pl.DeviceIdType.MESH
CONTRACT_ROWS = (((0,), (0,)), ((), ()))
CONTRACT_COLS = (((1,), (1,)), ((), ()))
EXACT = lax.Precision.HIGHEST


def extended(block, sides, width):
    for axis, dim in sides:
        count = lax.axis_size(axis)
        forward = [(i, i + 1) for i in range(count - 1)]
        backward = [(target, source) for source, target in forward]
        low = lax.ppermute(
            lax.slice_in_dim(block, block.shape[dim] - width, None, axis=dim), axis, forward
        )
        high = lax.ppermute(lax.slice_in_dim(block, 0, width, axis=dim), axis, backward)
        block = jnp.concatenate([low, block, high], axis=dim)
    return block


def swish_slope(pre):
    sigma = jax.nn.sigmoid(pre)
    return sigma * (1.0 + pre * (1.0 - sigma))


def conv_lags(rimmed, taps, length, reverse):
    total = jnp.zeros((length, rimmed.shape[1]), jnp.float32)
    last = taps.shape[0] - 1
    for lag in range(taps.shape[0]):
        start = last - lag if reverse else lag
        total = total + taps[lag] * rimmed[start : start + length]
    return total


def lag_sums(value, rimmed):
    length = value.shape[0]
    return [jnp.sum(value * rimmed[lag : lag + length], axis=0) for lag in range(TAPS)]


class Groups:
    def __init__(self):
        dp_size, tm_size = lax.axis_size("dp"), lax.axis_size("tm")
        self.dp, self.tm = lax.axis_index("dp"), lax.axis_index("tm")
        self.lines = tm_size // NEAR
        self.near_size, self.far_size = NEAR, dp_size * self.lines
        self.near_rank = self.tm % NEAR
        self.far_rank = self.dp * self.lines + self.tm // NEAR

    def near(self, rank):
        return (self.dp, (self.tm // NEAR) * NEAR + rank)

    def far(self, rank):
        return (rank // self.lines, (rank % self.lines) * NEAR + self.near_rank)

    def enter(self):
        barrier = pltpu.get_barrier_semaphore()

        def greet(size, rank, place):
            def step(k, carry):
                pl.semaphore_signal(
                    barrier, inc=1, device_id=place((rank + k) % size), device_id_type=MESH
                )
                return carry

            lax.fori_loop(1, size, step, 0)

        greet(self.near_size, self.near_rank, self.near)
        greet(self.far_size, self.far_rank, self.far)
        pl.semaphore_wait(barrier, self.near_size + self.far_size - 2)


CORES = 2
LINES = 4
ZEDS = EXPERTS
SPAN = ZEDS * CORES
HALF = ZEDS // 2
TURN = ((3, 1, 0, 2), (1, 3, 2, 0), (0, 2, 1, 3), (2, 0, 3, 1))
SWEEP = (0, 1, 7, 2, 6, 3, 5, 4)


def position(ids):
    return HALF * (ids % 2) + ids // 2


class Place:
    def __init__(self):
        self.dp, tm = lax.axis_index("dp"), lax.axis_index("tm")
        self.core, self.z, self.y = tm % CORES, (tm // CORES) % ZEDS, tm // SPAN

    def at(self, y, z, core):
        return (self.dp, (y % LINES) * SPAN + z * CORES + core)

    def sibling(self):
        return self.at(self.y, self.z, 1 - self.core)

    def line(self, step):
        return self.at(self.y + step + LINES, self.z, self.core)

    def zed(self, z):
        return self.at(self.y, z, self.core)

    def other_dp(self, step):
        dp_size = lax.axis_size("dp")
        return (self.dp + step + dp_size) % dp_size

    def on_dp(self, dp):
        return (dp, self.at(self.y, self.z, self.core)[1])

    def enter(self):
        barrier = pltpu.get_barrier_semaphore()
        peers = [self.sibling(), self.line(1), self.line(-1)]
        peers += [self.on_dp(self.other_dp(step)) for step in range(1, lax.axis_size("dp"))]
        peers += [self.zed((self.z + k) % ZEDS) for k in range(1, ZEDS)]
        for peer in peers:
            pl.semaphore_signal(barrier, inc=1, device_id=peer, device_id_type=MESH)
        pl.semaphore_wait(barrier, len(peers))


def remote(source, target, send_sem, recv_sem, device):
    return pltpu.make_async_remote_copy(
        src_ref=source,
        dst_ref=target,
        send_sem=send_sem,
        recv_sem=recv_sem,
        device_id=device,
        device_id_type=MESH,
    )


class Trade:
    def __init__(self, size, rank, place, source, held, send_sem, recv_sem):
        self.size, self.rank, self.place, self.source = size, rank, place, source
        self.held, self.send_sem, self.recv_sem = held, send_sem, recv_sem

    def copy(self, k):
        peer = (self.rank + k) % self.size
        return remote(
            self.source(peer),
            self.held.at[self.rank],
            self.send_sem.at[k],
            self.recv_sem.at[self.rank],
            self.place(peer),
        )

    def each(self, act):
        def step(k, carry):
            act(k)
            return carry

        lax.fori_loop(1, self.size, step, 0)

    def start(self):
        self.each(lambda k: self.copy(k).start())

    def finish(self):
        def arrival(k):
            origin = (self.rank + k) % self.size
            ref = self.held.at[origin]
            remote(
                ref, ref, self.send_sem.at[k], self.recv_sem.at[origin], self.place(origin)
            ).wait_recv()

        self.each(arrival)
        self.each(lambda k: self.copy(k).wait_send())


class Hop:
    def __init__(self, source, target, stays, device, sems):
        self.stays = stays
        self.local = pltpu.make_async_copy(source, target, sems.at[0])
        self.far = remote(source, target, sems.at[1], sems.at[2], device)

    def start(self):
        pl.when(self.stays)(self.local.start)
        pl.when(jnp.logical_not(self.stays))(self.far.start)

    def finish(self):
        pl.when(self.stays)(self.local.wait)

        @pl.when(jnp.logical_not(self.stays))
        def _():
            self.far.wait_recv()
            self.far.wait_send()


def look(table, index):
    value = table[0]
    for i, entry in enumerate(table):
        value = jnp.where(index == i, entry, value)
    return value


def work_line(place):
    table = [[row[line] for row in TURN].index(turn) for line in range(LINES) for turn in range(HALF)]
    return look(table, place.y * HALF + place.z % HALF)


def home_line(place):
    table = [row.index(turn) for row in TURN for turn in range(HALF)]
    return look(table, place.y * HALF + place.z % HALF)


def moments_merge(held, count):
    means = held[:, 0, :]
    mean = jnp.sum(means, axis=0) / means.shape[0]
    spread = means - mean[None]
    squares = jnp.sum(held[:, 1, :], axis=0) + count * jnp.sum(spread * spread, axis=0)
    return jnp.stack([mean, squares])


def moments_kernel(
    count,
    x_ref,
    w_in_ref,
    w_out_ref,
    o_ref,
    w_in_share,
    w_out_share,
    near_held,
    far_held,
    w_in_mid,
    w_out_mid,
    near_send,
    near_recv,
    far_send,
    far_recv,
    y_sems,
    z_sems,
):
    groups, place = Groups(), Place()
    near_held[groups.near_rank] = x_ref[...]
    line = work_line(place)
    zed = place.z // HALF * HALF + home_line(place)
    y_hops, z_hops = [], []
    cargo = ((w_in_ref, w_in_mid, w_in_share), (w_out_ref, w_out_mid, w_out_share))
    for i, (source, mid, share) in enumerate(cargo):
        depth = share.shape[0]
        mine = source.at[pl.ds(pl.multiple_of(place.dp * depth, depth), depth)]
        y_hops.append(Hop(mine, mid, line == place.y, place.at(line, place.z, place.core), y_sems.at[i]))
        z_hops.append(Hop(mid, share, zed == place.z, place.zed(zed), z_sems.at[i]))
    groups.enter()
    mine = near_held.at[groups.near_rank]
    near = Trade(
        groups.near_size, groups.near_rank, groups.near, lambda p: mine, near_held, near_send, near_recv
    )
    near.start()
    for hop in y_hops:
        hop.start()
    near.finish()
    far_held[groups.far_rank] = moments_merge(near_held[...], float(count))
    mine_far = far_held.at[groups.far_rank]
    far = Trade(
        groups.far_size, groups.far_rank, groups.far, lambda p: mine_far, far_held, far_send, far_recv
    )
    far.start()
    for y_hop, z_hop in zip(y_hops, z_hops):
        y_hop.finish()
        z_hop.start()
    far.finish()
    o_ref[...] = moments_merge(far_held[...], float(count * groups.near_size))
    for hop in z_hops:
        hop.finish()


def moments_and_weights(x, count, w_in, w_out, collective_id):
    dp_size = lax.axis_size("dp")
    far_size = dp_size * (lax.axis_size("tm") // NEAR)
    shares = [
        jax.ShapeDtypeStruct((w.shape[0] // dp_size, w.shape[1]), w.dtype) for w in (w_in, w_out)
    ]
    dma = pltpu.SemaphoreType.DMA
    return pl.pallas_call(
        functools.partial(moments_kernel, count),
        out_shape=(jax.ShapeDtypeStruct(x.shape, x.dtype), *shares),
        in_specs=[pl.BlockSpec(memory_space=pltpu.VMEM)] + [pl.BlockSpec(memory_space=pl.ANY)] * 2,
        out_specs=[pl.BlockSpec(memory_space=pltpu.VMEM)] + [pl.BlockSpec(memory_space=pl.ANY)] * 2,
        scratch_shapes=[
            pltpu.VMEM((NEAR,) + x.shape, x.dtype),
            pltpu.VMEM((far_size,) + x.shape, x.dtype),
            *[pltpu.VMEM(share.shape, share.dtype) for share in shares],
            dma((NEAR,)),
            dma((NEAR,)),
            dma((far_size,)),
            dma((far_size,)),
            dma((2, 3)),
            dma((2, 3)),
        ],
        compiler_params=pltpu.CompilerParams(
            collective_id=collective_id, has_side_effects=True, vmem_limit_bytes=16 << 20
        ),
    )(x, w_in, w_out)


def sums_kernel(
    x_ref,
    g0_ref,
    g1_ref,
    o_ref,
    h0_ref,
    h1_ref,
    near_held,
    far_held,
    mids,
    near_send,
    near_recv,
    far_send,
    far_recv,
    out_send,
    out_recv,
    y_sems,
    z_sems,
):
    groups, place = Groups(), Place()
    rank = groups.near_rank
    near_held[rank] = x_ref[rank]
    half, line = place.z // HALF * HALF, place.z % HALF
    turn = look([entry for row in TURN for entry in row], place.y * HALF + line)
    home = home_line(place)
    y_hops, z_hops = [], []
    for i, (source, target) in enumerate(((g0_ref, h0_ref), (g1_ref, h1_ref))):
        z_hops.append(
            Hop(source, mids.at[i], half + turn == place.z, place.zed(half + turn), z_sems.at[i])
        )
        y_hops.append(
            Hop(mids.at[i], target, home == place.y, place.at(home, place.z, place.core), y_sems.at[i])
        )
    groups.enter()
    near = Trade(
        groups.near_size, rank, groups.near, lambda p: x_ref.at[p], near_held, near_send, near_recv
    )
    near.start()
    for hop in z_hops:
        hop.start()
    near.finish()
    far_held[groups.far_rank] = jnp.sum(near_held[...], axis=0)
    mine = far_held.at[groups.far_rank]
    far = Trade(
        groups.far_size, groups.far_rank, groups.far, lambda p: mine, far_held, far_send, far_recv
    )
    far.start()
    for y_hop, z_hop in zip(y_hops, z_hops):
        z_hop.finish()
        y_hop.start()
    far.finish()
    o_ref[rank] = jnp.sum(far_held[...], axis=0)
    done = o_ref.at[rank]
    out = Trade(groups.near_size, rank, groups.near, lambda p: done, o_ref, out_send, out_recv)
    out.start()
    out.finish()
    for hop in y_hops:
        hop.finish()


def sums_and_gradients(x, g0, g1, collective_id):
    far_size = lax.axis_size("dp") * (lax.axis_size("tm") // NEAR)
    dma = pltpu.SemaphoreType.DMA
    gradient = jax.ShapeDtypeStruct(g0.shape, g0.dtype)
    return pl.pallas_call(
        sums_kernel,
        out_shape=(jax.ShapeDtypeStruct(x.shape, x.dtype), gradient, gradient),
        in_specs=[pl.BlockSpec(memory_space=pltpu.VMEM)] + [pl.BlockSpec(memory_space=pl.ANY)] * 2,
        out_specs=[pl.BlockSpec(memory_space=pltpu.VMEM)] + [pl.BlockSpec(memory_space=pl.ANY)] * 2,
        scratch_shapes=[
            pltpu.VMEM(x.shape, x.dtype),
            pltpu.VMEM((far_size,) + x.shape[1:], x.dtype),
            pltpu.VMEM((2,) + g0.shape, g0.dtype),
            dma((NEAR,)),
            dma((NEAR,)),
            dma((far_size,)),
            dma((far_size,)),
            dma((NEAR,)),
            dma((NEAR,)),
            dma((2, 3)),
            dma((2, 3)),
        ],
        compiler_params=pltpu.CompilerParams(
            collective_id=collective_id, has_side_effects=True, vmem_limit_bytes=16 << 20
        ),
    )(x, g0, g1)


CHUNKS = ((2, 0, 1, None), (2, 1, -1, None), (1, 1, 1, None), (3, 0, -1, None), (1, 0, 1, 0), (3, 1, -1, 1), (0, 0, 0, None), (0, 1, 0, None))
LEAVING = 6
LAG = 4
WIDE = 512


def experts_kernel(shares, x_ref, u_ref, in_share, out_share, *refs):
    o_refs, g_refs, refs = refs[:2], refs[2:4], refs[4:]
    (
        rows_x,
        rows_u,
        w_in,
        w_out,
        pre_held,
        hid_held,
        dpre_held,
        results,
        pair_held,
        line_held,
        gradient,
        parting,
        parts,
        weight_own,
        weight_send,
        weight_recv,
        part_send,
        part_recv,
        own_sem,
        zin_send,
        zin_recv,
        share_send,
        share_recv,
        yin_send,
        yin_recv,
        pair_send,
        pair_recv,
        y_send,
        y_recv,
        z_send,
        z_recv,
    ) = refs
    place = Place()
    y, z, core = place.y, place.z, place.core
    arrays = ((x_ref, rows_x), (u_ref, rows_u))
    waits = []

    weights = ((in_share, w_in), (out_share, w_out))

    def weight_own_copy(i):
        share, held = weights[i]
        return pltpu.make_async_copy(share, held.at[place.dp], weight_own.at[i])

    def weight_copy(i, step):
        share, held = weights[i]
        return remote(
            share,
            held.at[place.dp],
            weight_send.at[i, step],
            weight_recv.at[i, step],
            place.on_dp(place.other_dp(step)),
        )

    def weights_arrive():
        for i, (_, held) in enumerate(weights):
            weight_own_copy(i).wait()
            for step in range(1, shares):
                ref = held.at[place.other_dp(-step)]
                remote(
                    ref, ref, weight_send.at[i, step], weight_recv.at[i, step], place.sibling()
                ).wait_recv()


    def zin_copy(a, k):
        source, rows = arrays[a]
        target = (z + k) % ZEDS
        return remote(
            source.at[target], rows.at[core, y, z], zin_send.at[a, k], zin_recv.at[a, k], place.zed(target)
        )

    def own_copy(a):
        source, rows = arrays[a]
        return pltpu.make_async_copy(source.at[z], rows.at[core, y, z], own_sem.at[a])

    def block(a, from_core, step, k):
        return arrays[a][1].at[from_core, (y + step + LINES) % LINES, (z - k + ZEDS) % ZEDS]

    def pass_on(a, step, k, send_sem, recv_sem, device):
        ref = block(a, core, step, k)
        copy = remote(ref, ref, send_sem, recv_sem, device)
        copy.start()
        waits.append(copy)

    def arrived(a, from_core, step, k, send_sem, recv_sem):
        ref = block(a, from_core, step, k)
        remote(ref, ref, send_sem, recv_sem, place.sibling()).wait_recv()

    def share(a, step, k):
        index = step % LINES * ZEDS + k
        pass_on(a, step, k, share_send.at[a, index], share_recv.at[a, index], place.sibling())

    def spread(a, m):
        if m < ZEDS:
            k = SWEEP[m]
            if k == 0:
                own_copy(a).wait()
            else:
                arrived(a, core, 0, k, zin_send.at[a, k], zin_recv.at[a, k])
            for way, step in ((0, 1), (1, -1)):
                pass_on(a, 0, k, yin_send.at[a, way, k], yin_recv.at[a, way, k], place.line(step))
            share(a, 0, k)
        if 0 <= m - LAG // 2 < ZEDS:
            i = m - LAG // 2
            k = SWEEP[i]
            for way, step in ((0, 1), (1, -1)):
                arrived(a, core, -step, k, yin_send.at[a, way, k], yin_recv.at[a, way, k])
                if i % 2 == way:
                    pass_on(a, -step, k, yin_send.at[a, 2, k], yin_recv.at[a, 2, k], place.line(step))
                share(a, -step, k)
        if 0 <= m - LAG < ZEDS:
            k = SWEEP[m - LAG]
            arrived(a, core, 2, k, yin_send.at[a, 2, k], yin_recv.at[a, 2, k])
            share(a, 2, k)

    def all_shared(a):
        for step in range(LINES):
            for k in range(ZEDS):
                index = step * ZEDS + k
                arrived(a, 1 - core, step, k, share_send.at[a, index], share_recv.at[a, index])


    def chunk_of(ref, i):
        step, half = CHUNKS[i][:2]
        return ref.at[:, (y + step) % LINES, pl.ds(half * HALF, HALF)]

    def flat(value):
        return value.reshape(-1, value.shape[-1])

    def keep(ref, i, value):
        target = chunk_of(ref, i)
        target[...] = value.astype(ref.dtype).reshape(target.shape)

    def put(a, i, columns, value):
        target = results.at[a, i, :, :, :, pl.ds(columns, WIDE)]
        target[...] = value.astype(results.dtype).reshape(target.shape)

    w_in_rows, w_out_rows = w_in.shape[1] * shares, w_out.shape[1] * shares

    def forward(i):
        pre = jnp.dot(
            flat(chunk_of(rows_x, i)[...]),
            w_in[...].reshape(w_in_rows, -1),
            preferred_element_type=jnp.float32,
        )
        keep(pre_held, i, pre)
        hidden = (pre * jax.nn.sigmoid(pre)).astype(jnp.bfloat16)
        keep(hid_held, i, hidden)
        for columns in range(0, D, WIDE):
            weights = w_out[:, :, pl.ds(columns, WIDE)].reshape(w_out_rows, WIDE)
            put(0, i, columns, jnp.dot(hidden, weights, preferred_element_type=jnp.float32))
        pair_copy(0, i).start()

    def backward(i):
        dhidden = lax.dot_general(
            flat(chunk_of(rows_u, i)[...]),
            w_out[...].reshape(w_out_rows, -1),
            CONTRACT_COLS,
            preferred_element_type=jnp.float32,
        )
        dpre = (dhidden * swish_slope(flat(chunk_of(pre_held, i)[...]))).astype(jnp.bfloat16)
        keep(dpre_held, i, dpre)
        weights_all = w_in[...].reshape(w_in_rows, -1)
        for columns in range(0, D, WIDE):
            weights = weights_all[columns : columns + WIDE]
            put(
                1,
                i,
                columns,
                lax.dot_general(dpre, weights, CONTRACT_COLS, preferred_element_type=jnp.float32),
            )
        pair_copy(1, i).start()

    def part_copy(i, step):
        target = place.other_dp(step)
        return remote(
            parting.at[i, target],
            parts.at[i, place.dp],
            part_send.at[i, step],
            part_recv.at[i, step],
            place.on_dp(target),
        )

    def weight_gradient(i, left, right):
        def line(step, carry):
            for columns in range(0, D, WIDE):
                value = lax.dot_general(
                    flat(left[:, step]),
                    flat(right[:, step, :, :, pl.ds(columns, WIDE)]),
                    CONTRACT_ROWS,
                    preferred_element_type=jnp.float32,
                )
                gradient[:, pl.ds(columns, WIDE)] += value
            return carry

        gradient[...] = jnp.zeros_like(gradient)
        lax.fori_loop(0, LINES, line, 0)
        width = D // shares
        for part in range(shares):
            parting[i, part] = gradient[:, part * width : (part + 1) * width].astype(parting.dtype)
        for step in range(1, shares):
            part_copy(i, step).start()

    def gather_gradient(i):
        total = parting[i, place.dp].astype(jnp.float32)
        for step in range(1, shares):
            origin = place.other_dp(-step)
            ref = parts.at[i, origin]
            remote(
                ref, ref, part_send.at[i, step], part_recv.at[i, step], place.sibling()
            ).wait_recv()
            total = total + parts[i, origin].astype(jnp.float32)
        g_refs[i][...] = total.astype(g_refs[i].dtype)


    def pair_copy(a, i):
        return remote(
            results.at[a, i, 1 - core],
            pair_held.at[a, i],
            pair_send.at[a, i],
            pair_recv.at[a, i],
            place.sibling(),
        )

    def y_copy(a, i):
        return remote(
            results.at[a, i, core],
            line_held.at[a, i],
            y_send.at[a, i],
            y_recv.at[a, i],
            place.line(CHUNKS[i][2]),
        )

    def z_copy(a, target):
        source = results.at[a, LEAVING + target // HALF, core, target % HALF]
        return remote(source, o_refs[a].at[z], z_send.at[a, target], z_recv.at[a, z], place.zed(target))

    def settle(a, i, extras):
        pair_copy(a, i).wait_recv()
        for extra in extras:
            y_copy(a, extra).wait_recv()

        def one(j, carry):
            value = results[a, i, core, j].astype(jnp.float32) + pair_held[a, i, j].astype(jnp.float32)
            for extra in extras:
                value = value + line_held[a, extra, j].astype(jnp.float32)
            results[a, i, core, j] = value.astype(results.dtype)
            return carry

        lax.fori_loop(0, HALF, one, 0)

    def leave(a, i):
        extra = CHUNKS[i][3]
        settle(a, i, () if extra is None else (extra,))
        y_copy(a, i).start()

    def finish(a, half):
        settle(a, LEAVING + half, (4, 3) if half == 0 else (2, 5))
        for j in range(HALF):
            target = half * HALF + j

            @pl.when(target != z)
            def _():
                z_copy(a, target).start()

            @pl.when(target == z)
            def _():
                o_refs[a][target] = results[a, LEAVING + half, core, j]

    place.enter()
    for a in range(2):
        own_copy(a).start()
        for k in SWEEP[1:]:
            zin_copy(a, k).start()
    for i in range(2):
        weight_own_copy(i).start()
        for step in range(1, shares):
            weight_copy(i, step).start()
    for m in range(ZEDS + LAG):
        spread(0, m)
    all_shared(0)
    weights_arrive()
    for m in range(ZEDS + LAG):
        spread(1, m)
        if m < len(CHUNKS):
            forward(m)
        if 1 <= m <= 4:
            leave(0, m - 1)
    for i in (4, 5):
        leave(0, i)
    all_shared(1)
    for i in range(len(CHUNKS)):
        backward(i)
        if 1 <= i <= 4:
            leave(1, i - 1)
        if i == 6:
            finish(0, 0)
        if i == 7:
            finish(0, 1)
    weight_gradient(1, hid_held, rows_u)
    for i in (4, 5):
        leave(1, i)
    weight_gradient(0, dpre_held, rows_x)
    for half in range(2):
        finish(1, half)
    for i in (1, 0):
        gather_gradient(i)
    for a in range(2):
        for k in range(1, ZEDS):
            other = (z + k) % ZEDS
            ref = o_refs[a].at[other]
            remote(ref, ref, z_send.at[a, other], z_recv.at[a, other], place.zed(other)).wait_recv()
    for a in range(2):
        for k in SWEEP[1:]:
            zin_copy(a, k).wait_send()
        for i in range(len(CHUNKS)):
            pair_copy(a, i).wait_send()
        for i in range(LEAVING):
            y_copy(a, i).wait_send()
        for k in range(1, ZEDS):
            z_copy(a, (z + k) % ZEDS).wait_send()
    for copy in waits:
        copy.wait_send()
    for i in range(2):
        for step in range(1, shares):
            weight_copy(i, step).wait_send()
            part_copy(i, step).wait_send()


def experts(x, u, in_share, out_share, collective_id):
    shares = lax.axis_size("dp")
    hidden = in_share.shape[1]
    tile = x.shape[1:]
    lines = (CORES, LINES, ZEDS)
    chunk = (HALF,) + tile
    bf16, f32, dma = jnp.bfloat16, jnp.float32, pltpu.SemaphoreType.DMA
    out = jax.ShapeDtypeStruct(x.shape, bf16)
    gradient = jax.ShapeDtypeStruct((hidden, D // shares), bf16)
    held = lines + (tile[0], hidden)
    sems = [
        (2,),
        (2, shares),
        (2, shares),
        (2, shares),
        (2, shares),
        (2,),
        (2, ZEDS),
        (2, ZEDS),
        (2, LINES * ZEDS),
        (2, LINES * ZEDS),
        (2, 3, ZEDS),
        (2, 3, ZEDS),
        (2, len(CHUNKS)),
        (2, len(CHUNKS)),
        (2, LEAVING),
        (2, LEAVING),
        (2, ZEDS),
        (2, ZEDS),
    ]
    return pl.pallas_call(
        functools.partial(experts_kernel, shares),
        out_shape=(out, out, gradient, gradient),
        in_specs=[pl.BlockSpec(memory_space=pl.ANY)] * 4,
        out_specs=[pl.BlockSpec(memory_space=pltpu.VMEM)] * 4,
        scratch_shapes=[
            pltpu.VMEM(lines + tile, bf16),
            pltpu.VMEM(lines + tile, bf16),
            pltpu.VMEM((shares,) + in_share.shape, bf16),
            pltpu.VMEM((shares,) + out_share.shape, bf16),
            pltpu.VMEM(held, f32),
            pltpu.VMEM(held, bf16),
            pltpu.VMEM(held, bf16),
            pltpu.VMEM((2, len(CHUNKS), CORES) + chunk, bf16),
            pltpu.VMEM((2, len(CHUNKS)) + chunk, bf16),
            pltpu.VMEM((2, LEAVING) + chunk, bf16),
            pltpu.VMEM((hidden, D), f32),
            pltpu.VMEM((2, shares) + gradient.shape, bf16),
            pltpu.VMEM((2, shares) + gradient.shape, bf16),
        ]
        + [dma(shape) for shape in sems],
        compiler_params=pltpu.CompilerParams(
            collective_id=collective_id, has_side_effects=True, vmem_limit_bytes=58 << 20
        ),
    )(x, u, in_share, out_share)


def body(
    frames,
    taps,
    batchnorm_gain_scale,
    batchnorm_shift_bias,
    w_router,
    w_in,
    w_out,
    choices,
    cotangent,
):
    length = frames.shape[1]
    half = TAPS // 2
    element_count = lax.axis_size("dp") * lax.axis_size("tm") * length
    capacity = length * TOP // EXPERTS
    signal = frames[0].astype(jnp.float32)
    rimmed = extended(frames, (("tm", 1),), half)[0].astype(jnp.float32)
    conv = conv_lags(rimmed, taps, length, False)
    local_mean = jnp.sum(conv, axis=0) / length
    local_spread = conv - local_mean
    moments, w_in_share, w_out_share = moments_and_weights(
        jnp.stack([local_mean, jnp.sum(local_spread * local_spread, axis=0)]), length, w_in, w_out, 0
    )
    mean, variance = moments[0], moments[1] / element_count
    centered_values = conv - mean
    inverse_deviation = lax.rsqrt(variance + EPS)
    normalized_input = centered_values * inverse_deviation
    before_activation = normalized_input * batchnorm_gain_scale + batchnorm_shift_bias
    resid = signal + jax.nn.silu(before_activation)
    lcent = resid - jnp.mean(resid, axis=-1, keepdims=True)
    lrstd = lax.rsqrt(jnp.mean(lcent * lcent, axis=-1, keepdims=True) + EPS)
    vhat = lcent * lrstd
    normed = vhat.astype(jnp.bfloat16)
    logits = jnp.dot(normed, w_router, preferred_element_type=jnp.float32)
    ids = choices[0]
    onehot = (ids[:, :, None] == jnp.arange(EXPERTS, dtype=jnp.int32)[None, None, :]).astype(
        jnp.float32
    )
    picked = jnp.sum(onehot * logits[:, None, :], axis=-1)
    first = jax.nn.sigmoid(picked[:, 0] - picked[:, 1])
    gates = jnp.stack([first, 1.0 - first], axis=1)
    flat_ids = ids.reshape(-1)
    expert_hot = (flat_ids[:, None] == jnp.arange(EXPERTS, dtype=jnp.int32)[None, :]).astype(
        jnp.int32
    )
    slots = jnp.sum((jnp.cumsum(expert_hot, axis=0) - 1) * expert_hot, axis=1)
    places = (position(flat_ids) * capacity + slots).reshape(length, TOP)
    place_hot = places[:, :, None] == jnp.arange(EXPERTS * capacity, dtype=jnp.int32)[None, None, :]
    place_any = jnp.any(place_hot, axis=1).astype(jnp.bfloat16)
    place_hot = place_hot.astype(jnp.float32)
    gate_rows = jnp.sum(place_hot * gates[:, :, None], axis=(0, 1))

    def bucketed(rows):
        return lax.dot_general(place_any, rows, CONTRACT_ROWS, preferred_element_type=jnp.float32)

    buffer = bucketed(normed).astype(jnp.bfloat16).reshape(EXPERTS, capacity, D)
    sent_buffer = (gate_rows[:, None] * bucketed(cotangent[0])).astype(jnp.bfloat16)
    sent_buffer = sent_buffer.reshape(EXPERTS, capacity, D)
    combined, back, grad_in_local, grad_out_local = experts(
        buffer, sent_buffer, w_in_share, w_out_share, 1
    )
    combined = combined.reshape(EXPERTS * capacity, D).astype(jnp.float32)
    back = back.reshape(EXPERTS * capacity, D).astype(jnp.float32)
    expert_out = [
        jnp.dot(place_hot[:, k], combined, precision=EXACT) for k in range(TOP)
    ]
    mixed = (resid + sum(gates[:, k, None] * expert_out[k] for k in range(TOP))).astype(jnp.bfloat16)
    upstream = cotangent[0].astype(jnp.float32)
    dgate = [jnp.sum(upstream * expert_out[k], axis=-1) for k in range(TOP)]
    dpick = (dgate[0] - dgate[1]) * first * (1.0 - first)
    dlogits = (onehot[:, 0] - onehot[:, 1]) * dpick[:, None]
    dnormed = jnp.dot(dlogits, w_router.astype(jnp.float32).T, precision=EXACT)
    dnormed = dnormed + jnp.dot(jnp.sum(place_hot, axis=1), back, precision=EXACT)
    dmean = jnp.mean(dnormed, axis=-1, keepdims=True)
    dproj = jnp.mean(dnormed * vhat, axis=-1, keepdims=True)
    dresid = upstream + lrstd * (dnormed - dmean - vhat * dproj)
    normalized_gradient = dresid * swish_slope(before_activation) * batchnorm_gain_scale
    signal_lags = [jnp.sum(rimmed[lag : lag + length], axis=0) for lag in range(TAPS)]
    normalized_lags = lag_sums(normalized_input, rimmed)
    gradient_lags = lag_sums(normalized_gradient, rimmed)
    moment_rows = [
        jnp.sum(normalized_gradient, axis=0),
        jnp.sum(normalized_gradient * normalized_input, axis=0),
    ]
    lag_rows = jnp.stack(gradient_lags + signal_lags + normalized_lags)
    per_rank = -(-lag_rows.shape[0] // NEAR)
    lag_rows = jnp.pad(lag_rows, ((0, NEAR * per_rank - lag_rows.shape[0]), (0, 0)))
    to_sum = jnp.concatenate(
        [
            lag_rows.reshape(NEAR, per_rank, D),
            jnp.broadcast_to(jnp.stack(moment_rows)[None], (NEAR, 2, D)),
        ],
        axis=1,
    )
    rims = extended(jnp.stack([normalized_gradient, normalized_input]), (("tm", 1),), half)
    summed, grad_w_in, grad_w_out = sums_and_gradients(to_sum, grad_in_local, grad_out_local, 2)
    first_mean, second_mean = (summed[0, per_rank + i] / element_count for i in range(2))
    lag_rows = summed[:, :per_rank].reshape(NEAR * per_rank, D)
    grad_taps = inverse_deviation * (
        lag_rows[:TAPS]
        - first_mean * lag_rows[TAPS : 2 * TAPS]
        - second_mean * lag_rows[2 * TAPS : 3 * TAPS]
    )
    convolution_gradient = (
        inverse_deviation * (rims[0] - first_mean - rims[1] * second_mean)
    ).astype(jnp.bfloat16)
    at = lax.axis_index("tm") * length - half + jnp.arange(length + 2 * half)
    inside = (at >= 0) & (at < lax.axis_size("tm") * length)
    grad_rimmed = jnp.where(inside[:, None], convolution_gradient, 0).astype(jnp.float32)
    grad_frames = (dresid + conv_lags(grad_rimmed, taps, length, True)).astype(jnp.bfloat16)
    grad_w_in, grad_w_out = grad_w_in.T.astype(jnp.float32), grad_w_out.astype(jnp.float32)
    return (mixed[None], grad_frames[None], grad_taps, grad_w_in, grad_w_out)


def solution(mesh):
    return jax.shard_map(
        body,
        mesh=mesh,
        in_specs=(
            P("dp", "tm", None),
            P(),
            P(),
            P(),
            P(),
            P(None, "tm"),
            P("tm", None),
            P("dp", "tm", None),
            P("dp", "tm", None),
        ),
        out_specs=(P("dp", "tm", None), P("dp", "tm", None), P(), P("dp", "tm"), P("tm", "dp")),
        check_vma=False,
    )
```

```python
import functools

import jax
import jax.numpy as jnp
from jax import lax
from jax.experimental import pallas as pl
from jax.experimental.pallas import tpu as pltpu
from jax.sharding import PartitionSpec as P

D = 1536
EXPERTS = 8
TOP = 2
TAPS = 31
EPS = 1e-05
NEAR = 16
MESH = pl.DeviceIdType.MESH
CONTRACT_ROWS = (((0,), (0,)), ((), ()))
CONTRACT_COLS = (((1,), (1,)), ((), ()))
EXACT = lax.Precision.HIGHEST


def extended(block, sides, width):
    for axis, dim in sides:
        count = lax.axis_size(axis)
        forward = [(i, i + 1) for i in range(count - 1)]
        backward = [(target, source) for source, target in forward]
        low = lax.ppermute(
            lax.slice_in_dim(block, block.shape[dim] - width, None, axis=dim), axis, forward
        )
        high = lax.ppermute(lax.slice_in_dim(block, 0, width, axis=dim), axis, backward)
        block = jnp.concatenate([low, block, high], axis=dim)
    return block


def swish_slope(pre):
    sigma = jax.nn.sigmoid(pre)
    return sigma * (1.0 + pre * (1.0 - sigma))


def conv_lags(rimmed, taps, length, reverse):
    total = jnp.zeros((length, rimmed.shape[1]), jnp.float32)
    last = taps.shape[0] - 1
    for lag in range(taps.shape[0]):
        start = last - lag if reverse else lag
        total = total + taps[lag] * rimmed[start : start + length]
    return total


def lag_sums(value, rimmed):
    length = value.shape[0]
    return [jnp.sum(value * rimmed[lag : lag + length], axis=0) for lag in range(TAPS)]


def by_rank(rows):
    short = -len(rows) % NEAR
    return jnp.pad(jnp.stack(rows), ((0, short), (0, 0))).reshape(NEAR, -1, D)


class Groups:
    def __init__(self):
        dp_size, tm_size = lax.axis_size("dp"), lax.axis_size("tm")
        self.dp, self.tm = lax.axis_index("dp"), lax.axis_index("tm")
        self.lines = tm_size // NEAR
        self.near_size, self.far_size = NEAR, dp_size * self.lines
        self.near_rank = self.tm % NEAR
        self.far_rank = self.dp * self.lines + self.tm // NEAR

    def near(self, rank):
        return (self.dp, (self.tm // NEAR) * NEAR + rank)

    def far(self, rank):
        return (rank // self.lines, (rank % self.lines) * NEAR + self.near_rank)

    def enter(self, others=()):
        barrier = pltpu.get_barrier_semaphore()
        for other in others:
            pl.semaphore_signal(barrier, inc=1, device_id=other, device_id_type=MESH)

        def greet(size, rank, place):
            def step(k, carry):
                pl.semaphore_signal(
                    barrier, inc=1, device_id=place((rank + k) % size), device_id_type=MESH
                )
                return carry

            lax.fori_loop(1, size, step, 0)

        greet(self.near_size, self.near_rank, self.near)
        greet(self.far_size, self.far_rank, self.far)
        pl.semaphore_wait(barrier, self.near_size + self.far_size - 2 + len(others))


CORES = 2
LINES = 4
ZEDS = EXPERTS
SPAN = ZEDS * CORES
HALF = ZEDS // 2
TURN = ((3, 1, 0, 2), (1, 3, 2, 0), (0, 2, 1, 3), (2, 0, 3, 1))
SWEEP = (0, 1, 7, 2, 6, 3, 5, 4)


def position(ids):
    return HALF * (ids % 2) + ids // 2


class Place:
    def __init__(self):
        self.dp, tm = lax.axis_index("dp"), lax.axis_index("tm")
        self.core, self.z, self.y = tm % CORES, (tm // CORES) % ZEDS, tm // SPAN

    def at(self, y, z, core):
        return (self.dp, (y % LINES) * SPAN + z * CORES + core)

    def sibling(self):
        return self.at(self.y, self.z, 1 - self.core)

    def line(self, step):
        return self.at(self.y + step + LINES, self.z, self.core)

    def zed(self, z):
        return self.at(self.y, z, self.core)

    def other_dp(self, step):
        dp_size = lax.axis_size("dp")
        return (self.dp + step + dp_size) % dp_size

    def on_dp(self, dp):
        return (dp, self.at(self.y, self.z, self.core)[1])


def remote(source, target, send_sem, recv_sem, device):
    return pltpu.make_async_remote_copy(
        src_ref=source,
        dst_ref=target,
        send_sem=send_sem,
        recv_sem=recv_sem,
        device_id=device,
        device_id_type=MESH,
    )


class Trade:
    def __init__(self, size, rank, place, source, held, send_sem, recv_sem):
        self.size, self.rank, self.place, self.source = size, rank, place, source
        self.held, self.send_sem, self.recv_sem = held, send_sem, recv_sem

    def copy(self, k):
        peer = (self.rank + k) % self.size
        return remote(
            self.source(peer),
            self.held.at[self.rank],
            self.send_sem.at[k],
            self.recv_sem.at[self.rank],
            self.place(peer),
        )

    def each(self, act):
        def step(k, carry):
            act(k)
            return carry

        lax.fori_loop(1, self.size, step, 0)

    def start(self):
        self.each(lambda k: self.copy(k).start())

    def finish(self):
        def arrival(k):
            origin = (self.rank + k) % self.size
            ref = self.held.at[origin]
            remote(
                ref, ref, self.send_sem.at[k], self.recv_sem.at[origin], self.place(origin)
            ).wait_recv()

        self.each(arrival)
        self.each(lambda k: self.copy(k).wait_send())


class Hop:
    def __init__(self, source, target, stays, device, sems):
        self.stays = stays
        self.local = pltpu.make_async_copy(source, target, sems.at[0])
        self.far = remote(source, target, sems.at[1], sems.at[2], device)

    def start(self):
        pl.when(self.stays)(self.local.start)
        pl.when(jnp.logical_not(self.stays))(self.far.start)

    def finish(self):
        pl.when(self.stays)(self.local.wait)

        @pl.when(jnp.logical_not(self.stays))
        def _():
            self.far.wait_recv()
            self.far.wait_send()


def look(table, index):
    value = table[0]
    for i, entry in enumerate(table):
        value = jnp.where(index == i, entry, value)
    return value


def work_line(place):
    table = [[row[line] for row in TURN].index(turn) for line in range(LINES) for turn in range(HALF)]
    return look(table, place.y * HALF + place.z % HALF)


def home_line(place):
    table = [row.index(turn) for row in TURN for turn in range(HALF)]
    return look(table, place.y * HALF + place.z % HALF)


def moments_merge(held, count):
    means = held[:, 0, :]
    mean = jnp.sum(means, axis=0) / means.shape[0]
    spread = means - mean[None]
    squares = jnp.sum(held[:, 1, :], axis=0) + count * jnp.sum(spread * spread, axis=0)
    return jnp.stack([mean, squares])


def moments_kernel(
    count,
    x_ref,
    w_in_ref,
    w_out_ref,
    o_ref,
    w_in_share,
    w_out_share,
    near_held,
    far_held,
    w_in_mid,
    w_out_mid,
    near_send,
    near_recv,
    far_send,
    far_recv,
    y_sems,
    z_sems,
):
    groups, place = Groups(), Place()
    near_held[groups.near_rank] = x_ref[...]
    line = work_line(place)
    zed = place.z // HALF * HALF + home_line(place)
    y_hops, z_hops = [], []
    cargo = ((w_in_ref, w_in_mid, w_in_share), (w_out_ref, w_out_mid, w_out_share))
    for i, (source, mid, share) in enumerate(cargo):
        depth = share.shape[0]
        mine = source.at[pl.ds(pl.multiple_of(place.dp * depth, depth), depth)]
        y_hops.append(Hop(mine, mid, line == place.y, place.at(line, place.z, place.core), y_sems.at[i]))
        z_hops.append(Hop(mid, share, zed == place.z, place.zed(zed), z_sems.at[i]))
    groups.enter()
    mine = near_held.at[groups.near_rank]
    near = Trade(
        groups.near_size, groups.near_rank, groups.near, lambda p: mine, near_held, near_send, near_recv
    )
    near.start()
    for hop in y_hops:
        hop.start()
    near.finish()
    far_held[groups.far_rank] = moments_merge(near_held[...], float(count))
    mine_far = far_held.at[groups.far_rank]
    far = Trade(
        groups.far_size, groups.far_rank, groups.far, lambda p: mine_far, far_held, far_send, far_recv
    )
    far.start()
    for y_hop, z_hop in zip(y_hops, z_hops):
        y_hop.finish()
        z_hop.start()
    far.finish()
    o_ref[...] = moments_merge(far_held[...], float(count * groups.near_size))
    for hop in z_hops:
        hop.finish()


def moments_and_weights(x, count, w_in, w_out, collective_id):
    dp_size = lax.axis_size("dp")
    far_size = dp_size * (lax.axis_size("tm") // NEAR)
    shares = [
        jax.ShapeDtypeStruct((w.shape[0] // dp_size, w.shape[1]), w.dtype) for w in (w_in, w_out)
    ]
    dma = pltpu.SemaphoreType.DMA
    return pl.pallas_call(
        functools.partial(moments_kernel, count),
        out_shape=(jax.ShapeDtypeStruct(x.shape, x.dtype), *shares),
        in_specs=[pl.BlockSpec(memory_space=pltpu.VMEM)] + [pl.BlockSpec(memory_space=pl.ANY)] * 2,
        out_specs=[pl.BlockSpec(memory_space=pltpu.VMEM)] + [pl.BlockSpec(memory_space=pl.ANY)] * 2,
        scratch_shapes=[
            pltpu.VMEM((NEAR,) + x.shape, x.dtype),
            pltpu.VMEM((far_size,) + x.shape, x.dtype),
            *[pltpu.VMEM(share.shape, share.dtype) for share in shares],
            dma((NEAR,)),
            dma((NEAR,)),
            dma((far_size,)),
            dma((far_size,)),
            dma((2, 3)),
            dma((2, 3)),
        ],
        compiler_params=pltpu.CompilerParams(
            collective_id=collective_id, has_side_effects=True, vmem_limit_bytes=16 << 20
        ),
    )(x, w_in, w_out)


SIDE = 16


def last_kernel(
    count,
    x_ref,
    grad_ref,
    norm_ref,
    resid_ref,
    scale_ref,
    taps_ref,
    g0_ref,
    g1_ref,
    o_ref,
    frames_ref,
    h0_ref,
    h1_ref,
    near_held,
    far_held,
    mids,
    rims,
    wide,
    near_send,
    near_recv,
    far_send,
    far_recv,
    out_send,
    out_recv,
    y_sems,
    z_sems,
    rim_send,
    rim_recv,
):
    groups, place = Groups(), Place()
    rank = groups.near_rank
    length = grad_ref.shape[0]
    tm, tm_size = groups.tm, lax.axis_size("tm")
    after, before = (groups.dp, (tm + 1) % tm_size), (groups.dp, (tm + tm_size - 1) % tm_size)
    near_held[rank] = x_ref[rank]
    half, line = place.z // HALF * HALF, place.z % HALF
    turn = look([entry for row in TURN for entry in row], place.y * HALF + line)
    home = home_line(place)
    y_hops, z_hops = [], []
    for i, (source, target) in enumerate(((g0_ref, h0_ref), (g1_ref, h1_ref))):
        z_hops.append(
            Hop(source, mids.at[i], half + turn == place.z, place.zed(half + turn), z_sems.at[i])
        )
        y_hops.append(
            Hop(mids.at[i], target, home == place.y, place.at(home, place.z, place.core), y_sems.at[i])
        )
    rim_copies = []
    for i, ref in enumerate((grad_ref, norm_ref)):
        for side, rows, device in ((0, length - SIDE, after), (1, 0, before)):
            rim_copies.append(
                remote(
                    ref.at[pl.ds(rows, SIDE)],
                    rims.at[i, side],
                    rim_send.at[i, side],
                    rim_recv.at[i, side],
                    device,
                )
            )
    groups.enter((after, before))
    near = Trade(
        groups.near_size, rank, groups.near, lambda p: x_ref.at[p], near_held, near_send, near_recv
    )
    near.start()
    for copy in rim_copies:
        copy.start()
    for hop in z_hops:
        hop.start()
    near.finish()
    far_held[groups.far_rank] = jnp.sum(near_held[...], axis=0)
    mine = far_held.at[groups.far_rank]
    far = Trade(
        groups.far_size, groups.far_rank, groups.far, lambda p: mine, far_held, far_send, far_recv
    )
    far.start()
    for y_hop, z_hop in zip(y_hops, z_hops):
        z_hop.finish()
        y_hop.start()
    for copy in rim_copies:
        copy.wait_recv()
    far.finish()
    total = jnp.sum(far_held[...], axis=0)
    o_ref[rank] = total
    done = o_ref.at[rank]
    out = Trade(groups.near_size, rank, groups.near, lambda p: done, o_ref, out_send, out_recv)
    out.start()
    first, second = total[-2:-1] / count, total[-1:] / count

    def conv_gradient(grad, norm):
        value = scale_ref[...] * (grad - first - norm * second)
        return value.astype(jnp.bfloat16).astype(jnp.float32)

    for side, rows, edge in ((0, 0, tm == 0), (1, SIDE + length, tm == tm_size - 1)):
        value = conv_gradient(rims[0, side], rims[1, side])
        wide[pl.ds(rows, SIDE)] = jnp.where(edge, 0.0, value)
    wide[pl.ds(SIDE, length)] = conv_gradient(grad_ref[...], norm_ref[...])

    def columns_of(j, carry):
        columns = pl.ds(pl.multiple_of(j * 128, 128), 128)
        value = resid_ref[:, columns]
        for lag in range(TAPS):
            start = SIDE + TAPS // 2 - lag
            value = value + taps_ref[pl.ds(lag, 1), columns] * wide[pl.ds(start, length), columns]
        frames_ref[:, columns] = value.astype(frames_ref.dtype)
        return carry

    lax.fori_loop(0, resid_ref.shape[1] // 128, columns_of, 0)
    out.finish()
    for hop in y_hops:
        hop.finish()
    for copy in rim_copies:
        copy.wait_send()


def last_step(x, grad, norm, resid, scale, taps, g0, g1, count, collective_id):
    far_size = lax.axis_size("dp") * (lax.axis_size("tm") // NEAR)
    length, f32, dma = grad.shape[0], jnp.float32, pltpu.SemaphoreType.DMA
    gradient = jax.ShapeDtypeStruct(g0.shape, g0.dtype)
    vmem, anywhere = pl.BlockSpec(memory_space=pltpu.VMEM), pl.BlockSpec(memory_space=pl.ANY)
    return pl.pallas_call(
        functools.partial(last_kernel, count),
        out_shape=(
            jax.ShapeDtypeStruct(x.shape, x.dtype),
            jax.ShapeDtypeStruct(grad.shape, jnp.bfloat16),
            gradient,
            gradient,
        ),
        in_specs=[vmem] * 6 + [anywhere] * 2,
        out_specs=[vmem] * 2 + [anywhere] * 2,
        scratch_shapes=[
            pltpu.VMEM(x.shape, x.dtype),
            pltpu.VMEM((far_size,) + x.shape[1:], x.dtype),
            pltpu.VMEM((2,) + g0.shape, g0.dtype),
            pltpu.VMEM((2, 2, SIDE, D), f32),
            pltpu.VMEM((length + 2 * SIDE, D), f32),
            dma((NEAR,)),
            dma((NEAR,)),
            dma((far_size,)),
            dma((far_size,)),
            dma((NEAR,)),
            dma((NEAR,)),
            dma((2, 3)),
            dma((2, 3)),
            dma((2, 2)),
            dma((2, 2)),
        ],
        compiler_params=pltpu.CompilerParams(
            collective_id=collective_id, has_side_effects=True, vmem_limit_bytes=24 << 20
        ),
    )(x, grad, norm, resid, scale, taps, g0, g1)


CHUNKS = ((2, 0, 1, None), (2, 1, -1, None), (1, 1, 1, None), (3, 0, -1, None), (1, 0, 1, 0), (3, 1, -1, 1), (0, 0, 0, None), (0, 1, 0, None))
LEAVING = 6
LAG = 4
WIDE = 512


def experts_kernel(shares, x_ref, u_ref, in_share, out_share, lags_ref, *refs):
    o_refs, g_refs, sums_ref, refs = refs[:2], refs[2:4], refs[4], refs[5:]
    (
        rows_x,
        rows_u,
        w_in,
        w_out,
        pre_held,
        hid_held,
        dpre_held,
        results,
        pair_held,
        line_held,
        gradient,
        parting,
        parts,
        near_held,
        far_held,
        near_send,
        near_recv,
        far_send,
        far_recv,
        out_send,
        out_recv,
        weight_own,
        weight_send,
        weight_recv,
        part_send,
        part_recv,
        own_sem,
        zin_send,
        zin_recv,
        share_send,
        share_recv,
        yin_send,
        yin_recv,
        pair_send,
        pair_recv,
        y_send,
        y_recv,
        z_send,
        z_recv,
    ) = refs
    place, groups = Place(), Groups()
    y, z, core = place.y, place.z, place.core
    arrays = ((x_ref, rows_x), (u_ref, rows_u))
    rank = groups.near_rank
    near_held[rank] = lags_ref[rank]
    near = Trade(
        groups.near_size, rank, groups.near, lambda p: lags_ref.at[p], near_held, near_send, near_recv
    )
    mine = far_held.at[groups.far_rank]
    far = Trade(
        groups.far_size, groups.far_rank, groups.far, lambda p: mine, far_held, far_send, far_recv
    )
    done = sums_ref.at[rank]
    out = Trade(groups.near_size, rank, groups.near, lambda p: done, sums_ref, out_send, out_recv)
    waits = []

    weights = ((in_share, w_in), (out_share, w_out))

    def weight_own_copy(i):
        share, held = weights[i]
        return pltpu.make_async_copy(share, held.at[place.dp], weight_own.at[i])

    def weight_copy(i, step):
        share, held = weights[i]
        return remote(
            share,
            held.at[place.dp],
            weight_send.at[i, step],
            weight_recv.at[i, step],
            place.on_dp(place.other_dp(step)),
        )

    def weights_arrive():
        for i, (_, held) in enumerate(weights):
            weight_own_copy(i).wait()
            for step in range(1, shares):
                ref = held.at[place.other_dp(-step)]
                remote(
                    ref, ref, weight_send.at[i, step], weight_recv.at[i, step], place.sibling()
                ).wait_recv()


    def zin_copy(a, k):
        source, rows = arrays[a]
        target = (z + k) % ZEDS
        return remote(
            source.at[target], rows.at[core, y, z], zin_send.at[a, k], zin_recv.at[a, k], place.zed(target)
        )

    def own_copy(a):
        source, rows = arrays[a]
        return pltpu.make_async_copy(source.at[z], rows.at[core, y, z], own_sem.at[a])

    def block(a, from_core, step, k):
        return arrays[a][1].at[from_core, (y + step + LINES) % LINES, (z - k + ZEDS) % ZEDS]

    def pass_on(a, step, k, send_sem, recv_sem, device):
        ref = block(a, core, step, k)
        copy = remote(ref, ref, send_sem, recv_sem, device)
        copy.start()
        waits.append(copy)

    def arrived(a, from_core, step, k, send_sem, recv_sem):
        ref = block(a, from_core, step, k)
        remote(ref, ref, send_sem, recv_sem, place.sibling()).wait_recv()

    def share(a, step, k):
        index = step % LINES * ZEDS + k
        pass_on(a, step, k, share_send.at[a, index], share_recv.at[a, index], place.sibling())

    def spread(a, m):
        if m < ZEDS:
            k = SWEEP[m]
            if k == 0:
                own_copy(a).wait()
            else:
                arrived(a, core, 0, k, zin_send.at[a, k], zin_recv.at[a, k])
            for way, step in ((0, 1), (1, -1)):
                pass_on(a, 0, k, yin_send.at[a, way, k], yin_recv.at[a, way, k], place.line(step))
            share(a, 0, k)
        if 0 <= m - LAG // 2 < ZEDS:
            i = m - LAG // 2
            k = SWEEP[i]
            for way, step in ((0, 1), (1, -1)):
                arrived(a, core, -step, k, yin_send.at[a, way, k], yin_recv.at[a, way, k])
                if i % 2 == way:
                    pass_on(a, -step, k, yin_send.at[a, 2, k], yin_recv.at[a, 2, k], place.line(step))
                share(a, -step, k)
        if 0 <= m - LAG < ZEDS:
            k = SWEEP[m - LAG]
            arrived(a, core, 2, k, yin_send.at[a, 2, k], yin_recv.at[a, 2, k])
            share(a, 2, k)

    def all_shared(a):
        for step in range(LINES):
            for k in range(ZEDS):
                index = step * ZEDS + k
                arrived(a, 1 - core, step, k, share_send.at[a, index], share_recv.at[a, index])


    def chunk_of(ref, i):
        step, half = CHUNKS[i][:2]
        return ref.at[:, (y + step) % LINES, pl.ds(half * HALF, HALF)]

    def flat(value):
        return value.reshape(-1, value.shape[-1])

    def keep(ref, i, value):
        target = chunk_of(ref, i)
        target[...] = value.astype(ref.dtype).reshape(target.shape)

    def put(a, i, columns, value):
        target = results.at[a, i, :, :, :, pl.ds(columns, WIDE)]
        target[...] = value.astype(results.dtype).reshape(target.shape)

    w_in_rows, w_out_rows = w_in.shape[1] * shares, w_out.shape[1] * shares

    def forward(i):
        pre = jnp.dot(
            flat(chunk_of(rows_x, i)[...]),
            w_in[...].reshape(w_in_rows, -1),
            preferred_element_type=jnp.float32,
        )
        keep(pre_held, i, pre)
        hidden = (pre * jax.nn.sigmoid(pre)).astype(jnp.bfloat16)
        keep(hid_held, i, hidden)
        for columns in range(0, D, WIDE):
            weights = w_out[:, :, pl.ds(columns, WIDE)].reshape(w_out_rows, WIDE)
            put(0, i, columns, jnp.dot(hidden, weights, preferred_element_type=jnp.float32))
        pair_copy(0, i).start()

    def backward(i):
        dhidden = lax.dot_general(
            flat(chunk_of(rows_u, i)[...]),
            w_out[...].reshape(w_out_rows, -1),
            CONTRACT_COLS,
            preferred_element_type=jnp.float32,
        )
        dpre = (dhidden * swish_slope(flat(chunk_of(pre_held, i)[...]))).astype(jnp.bfloat16)
        keep(dpre_held, i, dpre)
        weights_all = w_in[...].reshape(w_in_rows, -1)
        for columns in range(0, D, WIDE):
            weights = weights_all[columns : columns + WIDE]
            put(
                1,
                i,
                columns,
                lax.dot_general(dpre, weights, CONTRACT_COLS, preferred_element_type=jnp.float32),
            )
        pair_copy(1, i).start()

    def part_copy(i, step):
        target = place.other_dp(step)
        return remote(
            parting.at[i, target],
            parts.at[i, place.dp],
            part_send.at[i, step],
            part_recv.at[i, step],
            place.on_dp(target),
        )

    def weight_gradient(i, left, right):
        def line(step, carry):
            for columns in range(0, D, WIDE):
                value = lax.dot_general(
                    flat(left[:, step]),
                    flat(right[:, step, :, :, pl.ds(columns, WIDE)]),
                    CONTRACT_ROWS,
                    preferred_element_type=jnp.float32,
                )
                gradient[:, pl.ds(columns, WIDE)] += value
            return carry

        gradient[...] = jnp.zeros_like(gradient)
        lax.fori_loop(0, LINES, line, 0)
        width = D // shares
        for part in range(shares):
            parting[i, part] = gradient[:, part * width : (part + 1) * width].astype(parting.dtype)
        for step in range(1, shares):
            part_copy(i, step).start()

    def gather_gradient(i):
        total = parting[i, place.dp].astype(jnp.float32)
        for step in range(1, shares):
            origin = place.other_dp(-step)
            ref = parts.at[i, origin]
            remote(
                ref, ref, part_send.at[i, step], part_recv.at[i, step], place.sibling()
            ).wait_recv()
            total = total + parts[i, origin].astype(jnp.float32)
        g_refs[i][...] = total.astype(g_refs[i].dtype)


    def pair_copy(a, i):
        return remote(
            results.at[a, i, 1 - core],
            pair_held.at[a, i],
            pair_send.at[a, i],
            pair_recv.at[a, i],
            place.sibling(),
        )

    def y_copy(a, i):
        return remote(
            results.at[a, i, core],
            line_held.at[a, i],
            y_send.at[a, i],
            y_recv.at[a, i],
            place.line(CHUNKS[i][2]),
        )

    def z_copy(a, target):
        source = results.at[a, LEAVING + target // HALF, core, target % HALF]
        return remote(source, o_refs[a].at[z], z_send.at[a, target], z_recv.at[a, z], place.zed(target))

    def settle(a, i, extras):
        pair_copy(a, i).wait_recv()
        for extra in extras:
            y_copy(a, extra).wait_recv()

        def one(j, carry):
            value = results[a, i, core, j].astype(jnp.float32) + pair_held[a, i, j].astype(jnp.float32)
            for extra in extras:
                value = value + line_held[a, extra, j].astype(jnp.float32)
            results[a, i, core, j] = value.astype(results.dtype)
            return carry

        lax.fori_loop(0, HALF, one, 0)

    def leave(a, i):
        extra = CHUNKS[i][3]
        settle(a, i, () if extra is None else (extra,))
        y_copy(a, i).start()

    def finish(a, half):
        settle(a, LEAVING + half, (4, 3) if half == 0 else (2, 5))
        for j in range(HALF):
            target = half * HALF + j

            @pl.when(target != z)
            def _():
                z_copy(a, target).start()

            @pl.when(target == z)
            def _():
                o_refs[a][target] = results[a, LEAVING + half, core, j]

    groups.enter()
    for a in range(2):
        own_copy(a).start()
        for k in SWEEP[1:]:
            zin_copy(a, k).start()
    for i in range(2):
        weight_own_copy(i).start()
        for step in range(1, shares):
            weight_copy(i, step).start()
    for m in range(ZEDS + LAG):
        spread(0, m)
    all_shared(0)
    weights_arrive()
    near.start()
    for m in range(ZEDS + LAG):
        spread(1, m)
        if m < len(CHUNKS):
            forward(m)
        if 1 <= m <= 4:
            leave(0, m - 1)
    for i in (4, 5):
        leave(0, i)
    all_shared(1)
    near.finish()
    far_held[groups.far_rank] = jnp.sum(near_held[...], axis=0)
    far.start()
    for i in range(len(CHUNKS)):
        backward(i)
        if 1 <= i <= 4:
            leave(1, i - 1)
        if i == 6:
            finish(0, 0)
        if i == 7:
            finish(0, 1)
    far.finish()
    sums_ref[rank] = jnp.sum(far_held[...], axis=0)
    out.start()
    weight_gradient(1, hid_held, rows_u)
    for i in (4, 5):
        leave(1, i)
    weight_gradient(0, dpre_held, rows_x)
    for half in range(2):
        finish(1, half)
    for i in (1, 0):
        gather_gradient(i)
    out.finish()
    for a in range(2):
        for k in range(1, ZEDS):
            other = (z + k) % ZEDS
            ref = o_refs[a].at[other]
            remote(ref, ref, z_send.at[a, other], z_recv.at[a, other], place.zed(other)).wait_recv()
    for a in range(2):
        for k in SWEEP[1:]:
            zin_copy(a, k).wait_send()
        for i in range(len(CHUNKS)):
            pair_copy(a, i).wait_send()
        for i in range(LEAVING):
            y_copy(a, i).wait_send()
        for k in range(1, ZEDS):
            z_copy(a, (z + k) % ZEDS).wait_send()
    for copy in waits:
        copy.wait_send()
    for i in range(2):
        for step in range(1, shares):
            weight_copy(i, step).wait_send()
            part_copy(i, step).wait_send()


def experts(x, u, in_share, out_share, lags, collective_id):
    shares = lax.axis_size("dp")
    hidden = in_share.shape[1]
    tile = x.shape[1:]
    lines = (CORES, LINES, ZEDS)
    chunk = (HALF,) + tile
    bf16, f32, dma = jnp.bfloat16, jnp.float32, pltpu.SemaphoreType.DMA
    out = jax.ShapeDtypeStruct(x.shape, bf16)
    gradient = jax.ShapeDtypeStruct((hidden, D // shares), bf16)
    held = lines + (tile[0], hidden)
    far_size = shares * (lax.axis_size("tm") // NEAR)
    sems = [
        (NEAR,),
        (NEAR,),
        (far_size,),
        (far_size,),
        (NEAR,),
        (NEAR,),
        (2,),
        (2, shares),
        (2, shares),
        (2, shares),
        (2, shares),
        (2,),
        (2, ZEDS),
        (2, ZEDS),
        (2, LINES * ZEDS),
        (2, LINES * ZEDS),
        (2, 3, ZEDS),
        (2, 3, ZEDS),
        (2, len(CHUNKS)),
        (2, len(CHUNKS)),
        (2, LEAVING),
        (2, LEAVING),
        (2, ZEDS),
        (2, ZEDS),
    ]
    return pl.pallas_call(
        functools.partial(experts_kernel, shares),
        out_shape=(out, out, gradient, gradient, jax.ShapeDtypeStruct(lags.shape, lags.dtype)),
        in_specs=[pl.BlockSpec(memory_space=pl.ANY)] * 4 + [pl.BlockSpec(memory_space=pltpu.VMEM)],
        out_specs=[pl.BlockSpec(memory_space=pltpu.VMEM)] * 5,
        scratch_shapes=[
            pltpu.VMEM(lines + tile, bf16),
            pltpu.VMEM(lines + tile, bf16),
            pltpu.VMEM((shares,) + in_share.shape, bf16),
            pltpu.VMEM((shares,) + out_share.shape, bf16),
            pltpu.VMEM(held, f32),
            pltpu.VMEM(held, bf16),
            pltpu.VMEM(held, bf16),
            pltpu.VMEM((2, len(CHUNKS), CORES) + chunk, bf16),
            pltpu.VMEM((2, len(CHUNKS)) + chunk, bf16),
            pltpu.VMEM((2, LEAVING) + chunk, bf16),
            pltpu.VMEM((hidden, D), f32),
            pltpu.VMEM((2, shares) + gradient.shape, bf16),
            pltpu.VMEM((2, shares) + gradient.shape, bf16),
            pltpu.VMEM(lags.shape, lags.dtype),
            pltpu.VMEM((far_size,) + lags.shape[1:], lags.dtype),
        ]
        + [dma(shape) for shape in sems],
        compiler_params=pltpu.CompilerParams(
            collective_id=collective_id, has_side_effects=True, vmem_limit_bytes=58 << 20
        ),
    )(x, u, in_share, out_share, lags)


def body(
    frames,
    taps,
    batchnorm_gain_scale,
    batchnorm_shift_bias,
    w_router,
    w_in,
    w_out,
    choices,
    cotangent,
):
    length = frames.shape[1]
    half = TAPS // 2
    element_count = lax.axis_size("dp") * lax.axis_size("tm") * length
    capacity = length * TOP // EXPERTS
    signal = frames[0].astype(jnp.float32)
    rimmed = extended(frames, (("tm", 1),), half)[0].astype(jnp.float32)
    conv = conv_lags(rimmed, taps, length, False)
    local_mean = jnp.sum(conv, axis=0) / length
    local_spread = conv - local_mean
    moments, w_in_share, w_out_share = moments_and_weights(
        jnp.stack([local_mean, jnp.sum(local_spread * local_spread, axis=0)]), length, w_in, w_out, 0
    )
    mean, variance = moments[0], moments[1] / element_count
    centered_values = conv - mean
    inverse_deviation = lax.rsqrt(variance + EPS)
    normalized_input = centered_values * inverse_deviation
    before_activation = normalized_input * batchnorm_gain_scale + batchnorm_shift_bias
    resid = signal + jax.nn.silu(before_activation)
    lcent = resid - jnp.mean(resid, axis=-1, keepdims=True)
    lrstd = lax.rsqrt(jnp.mean(lcent * lcent, axis=-1, keepdims=True) + EPS)
    vhat = lcent * lrstd
    normed = vhat.astype(jnp.bfloat16)
    logits = jnp.dot(normed, w_router, preferred_element_type=jnp.float32)
    ids = choices[0]
    onehot = (ids[:, :, None] == jnp.arange(EXPERTS, dtype=jnp.int32)[None, None, :]).astype(
        jnp.float32
    )
    picked = jnp.sum(onehot * logits[:, None, :], axis=-1)
    first = jax.nn.sigmoid(picked[:, 0] - picked[:, 1])
    gates = jnp.stack([first, 1.0 - first], axis=1)
    flat_ids = ids.reshape(-1)
    expert_hot = (flat_ids[:, None] == jnp.arange(EXPERTS, dtype=jnp.int32)[None, :]).astype(
        jnp.int32
    )
    slots = jnp.sum((jnp.cumsum(expert_hot, axis=0) - 1) * expert_hot, axis=1)
    places = (position(flat_ids) * capacity + slots).reshape(length, TOP)
    place_hot = places[:, :, None] == jnp.arange(EXPERTS * capacity, dtype=jnp.int32)[None, None, :]
    place_any = jnp.any(place_hot, axis=1).astype(jnp.bfloat16)
    place_hot = place_hot.astype(jnp.float32)
    gate_rows = jnp.sum(place_hot * gates[:, :, None], axis=(0, 1))

    def bucketed(rows):
        return lax.dot_general(place_any, rows, CONTRACT_ROWS, preferred_element_type=jnp.float32)

    buffer = bucketed(normed).astype(jnp.bfloat16).reshape(EXPERTS, capacity, D)
    sent_buffer = (gate_rows[:, None] * bucketed(cotangent[0])).astype(jnp.bfloat16)
    sent_buffer = sent_buffer.reshape(EXPERTS, capacity, D)
    signal_lags = [jnp.sum(rimmed[lag : lag + length], axis=0) for lag in range(TAPS)]
    lags = by_rank(signal_lags + lag_sums(normalized_input, rimmed))
    combined, back, grad_in_local, grad_out_local, lags = experts(
        buffer, sent_buffer, w_in_share, w_out_share, lags, 1
    )
    combined = combined.reshape(EXPERTS * capacity, D).astype(jnp.float32)
    back = back.reshape(EXPERTS * capacity, D).astype(jnp.float32)
    expert_out = [
        jnp.dot(place_hot[:, k], combined, precision=EXACT) for k in range(TOP)
    ]
    mixed = (resid + sum(gates[:, k, None] * expert_out[k] for k in range(TOP))).astype(jnp.bfloat16)
    upstream = cotangent[0].astype(jnp.float32)
    dgate = [jnp.sum(upstream * expert_out[k], axis=-1) for k in range(TOP)]
    dpick = (dgate[0] - dgate[1]) * first * (1.0 - first)
    dlogits = (onehot[:, 0] - onehot[:, 1]) * dpick[:, None]
    dnormed = jnp.dot(dlogits, w_router.astype(jnp.float32).T, precision=EXACT)
    dnormed = dnormed + jnp.dot(jnp.sum(place_hot, axis=1), back, precision=EXACT)
    dmean = jnp.mean(dnormed, axis=-1, keepdims=True)
    dproj = jnp.mean(dnormed * vhat, axis=-1, keepdims=True)
    dresid = upstream + lrstd * (dnormed - dmean - vhat * dproj)
    normalized_gradient = dresid * swish_slope(before_activation) * batchnorm_gain_scale
    moment_rows = jnp.stack(
        [
            jnp.sum(normalized_gradient, axis=0),
            jnp.sum(normalized_gradient * normalized_input, axis=0),
        ]
    )
    to_sum = jnp.concatenate(
        [
            by_rank(lag_sums(normalized_gradient, rimmed)),
            jnp.broadcast_to(moment_rows[None], (NEAR,) + moment_rows.shape),
        ],
        axis=1,
    )
    summed, grad_frames, grad_w_in, grad_w_out = last_step(
        to_sum,
        normalized_gradient,
        normalized_input,
        dresid,
        inverse_deviation[None],
        taps,
        grad_in_local,
        grad_out_local,
        element_count,
        2,
    )
    lag_rows = lags.reshape(-1, D)
    grad_taps = inverse_deviation * (
        summed[:, :-2].reshape(-1, D)[:TAPS]
        - summed[0, -2] / element_count * lag_rows[:TAPS]
        - summed[0, -1] / element_count * lag_rows[TAPS : 2 * TAPS]
    )
    grad_w_in, grad_w_out = grad_w_in.T.astype(jnp.float32), grad_w_out.astype(jnp.float32)
    return (mixed[None], grad_frames[None], grad_taps, grad_w_in, grad_w_out)


def solution(mesh):
    return jax.shard_map(
        body,
        mesh=mesh,
        in_specs=(
            P("dp", "tm", None),
            P(),
            P(),
            P(),
            P(),
            P(None, "tm"),
            P("tm", None),
            P("dp", "tm", None),
            P("dp", "tm", None),
        ),
        out_specs=(P("dp", "tm", None), P("dp", "tm", None), P(), P("dp", "tm"), P("tm", "dp")),
        check_vma=False,
    )
```

```python
import functools

import jax
import jax.numpy as jnp
from jax import lax
from jax.experimental import pallas as pl
from jax.experimental.pallas import tpu as pltpu
from jax.sharding import PartitionSpec as P

D = 1536
EXPERTS = 8
TOP = 2
TAPS = 31
EPS = 1e-05
NEAR = 16
MESH = pl.DeviceIdType.MESH
CONTRACT_ROWS = (((0,), (0,)), ((), ()))
CONTRACT_COLS = (((1,), (1,)), ((), ()))
EXACT = lax.Precision.HIGHEST


def swish_slope(pre):
    sigma = jax.nn.sigmoid(pre)
    return sigma * (1.0 + pre * (1.0 - sigma))


class Groups:
    def __init__(self):
        dp_size, tm_size = lax.axis_size("dp"), lax.axis_size("tm")
        self.dp, self.tm = lax.axis_index("dp"), lax.axis_index("tm")
        self.lines = tm_size // NEAR
        self.near_size, self.far_size = NEAR, dp_size * self.lines
        self.near_rank = self.tm % NEAR
        self.far_rank = self.dp * self.lines + self.tm // NEAR

    def near(self, rank):
        return (self.dp, (self.tm // NEAR) * NEAR + rank)

    def far(self, rank):
        return (rank // self.lines, (rank % self.lines) * NEAR + self.near_rank)

    def greet(self, others=()):
        barrier = pltpu.get_barrier_semaphore()
        for other in others:
            pl.semaphore_signal(barrier, inc=1, device_id=other, device_id_type=MESH)

        def greet(size, rank, place):
            def step(k, carry):
                pl.semaphore_signal(
                    barrier, inc=1, device_id=place((rank + k) % size), device_id_type=MESH
                )
                return carry

            lax.fori_loop(1, size, step, 0)

        greet(self.near_size, self.near_rank, self.near)
        greet(self.far_size, self.far_rank, self.far)
        return self.near_size + self.far_size - 2 + len(others)

    def wait(self, signals):
        pl.semaphore_wait(pltpu.get_barrier_semaphore(), signals)


CORES = 2
LINES = 4
ZEDS = EXPERTS
SPAN = ZEDS * CORES
HALF = ZEDS // 2
TURN = ((3, 1, 0, 2), (1, 3, 2, 0), (0, 2, 1, 3), (2, 0, 3, 1))
SWEEP = (0, 1, 7, 2, 6, 3, 5, 4)


def position(ids):
    return HALF * (ids % 2) + ids // 2


class Place:
    def __init__(self):
        self.dp, tm = lax.axis_index("dp"), lax.axis_index("tm")
        self.core, self.z, self.y = tm % CORES, (tm // CORES) % ZEDS, tm // SPAN

    def at(self, y, z, core):
        return (self.dp, (y % LINES) * SPAN + z * CORES + core)

    def sibling(self):
        return self.at(self.y, self.z, 1 - self.core)

    def line(self, step):
        return self.at(self.y + step + LINES, self.z, self.core)

    def zed(self, z):
        return self.at(self.y, z, self.core)

    def other_dp(self, step):
        dp_size = lax.axis_size("dp")
        return (self.dp + step + dp_size) % dp_size

    def on_dp(self, dp):
        return (dp, self.at(self.y, self.z, self.core)[1])


def remote(source, target, send_sem, recv_sem, device):
    return pltpu.make_async_remote_copy(
        src_ref=source,
        dst_ref=target,
        send_sem=send_sem,
        recv_sem=recv_sem,
        device_id=device,
        device_id_type=MESH,
    )


class Trade:
    def __init__(self, size, rank, place, source, held, send_sem, recv_sem):
        self.size, self.rank, self.place, self.source = size, rank, place, source
        self.held, self.send_sem, self.recv_sem = held, send_sem, recv_sem

    def copy(self, k):
        peer = (self.rank + k) % self.size
        return remote(
            self.source(peer),
            self.held.at[self.rank],
            self.send_sem.at[k],
            self.recv_sem.at[self.rank],
            self.place(peer),
        )

    def each(self, act):
        def step(k, carry):
            act(k)
            return carry

        lax.fori_loop(1, self.size, step, 0)

    def start(self):
        self.each(lambda k: self.copy(k).start())

    def finish(self):
        def arrival(k):
            origin = (self.rank + k) % self.size
            ref = self.held.at[origin]
            remote(
                ref, ref, self.send_sem.at[k], self.recv_sem.at[origin], self.place(origin)
            ).wait_recv()

        self.each(arrival)
        self.each(lambda k: self.copy(k).wait_send())


class Hop:
    def __init__(self, source, target, stays, device, sems):
        self.stays = stays
        self.local = pltpu.make_async_copy(source, target, sems.at[0])
        self.far = remote(source, target, sems.at[1], sems.at[2], device)

    def start(self):
        pl.when(self.stays)(self.local.start)
        pl.when(jnp.logical_not(self.stays))(self.far.start)

    def finish(self):
        pl.when(self.stays)(self.local.wait)

        @pl.when(jnp.logical_not(self.stays))
        def _():
            self.far.wait_recv()
            self.far.wait_send()


def look(table, index):
    value = table[0]
    for i, entry in enumerate(table):
        value = jnp.where(index == i, entry, value)
    return value


def work_line(place):
    table = [[row[line] for row in TURN].index(turn) for line in range(LINES) for turn in range(HALF)]
    return look(table, place.y * HALF + place.z % HALF)


def home_line(place):
    table = [row.index(turn) for row in TURN for turn in range(HALF)]
    return look(table, place.y * HALF + place.z % HALF)


def moments_merge(held, count):
    means = held[:, 0, :]
    mean = jnp.sum(means, axis=0) / means.shape[0]
    spread = means - mean[None]
    squares = jnp.sum(held[:, 1, :], axis=0) + count * jnp.sum(spread * spread, axis=0)
    return jnp.stack([mean, squares])


SIDE = 16
LAG = 4


def place_row(ref, row, columns, value):
    depth = ref.shape[1]
    ref[row // depth, pl.ds(row % depth, 1), columns] = value


def row_of(ref, row):
    depth = ref.shape[1]
    return ref[row // depth, pl.ds(row % depth, 1), :]


class Spread:
    SEMS = ((1,), (ZEDS,), (ZEDS,), (LINES * ZEDS,), (LINES * ZEDS,), (3, ZEDS), (3, ZEDS))

    def __init__(self, place, source, rows, sems):
        self.place, self.source, self.rows = place, source, rows
        self.own, self.z_send, self.z_recv = sems[:3]
        self.share_send, self.share_recv, self.y_send, self.y_recv = sems[3:]
        self.waits = []

    def z_copy(self, k):
        place = self.place
        target = (place.z + k) % ZEDS
        mine = self.rows.at[place.core, place.y, place.z]
        return remote(
            self.source.at[target], mine, self.z_send.at[k], self.z_recv.at[k], place.zed(target)
        )

    def own_copy(self):
        place = self.place
        mine = self.rows.at[place.core, place.y, place.z]
        return pltpu.make_async_copy(self.source.at[place.z], mine, self.own.at[0])

    def block(self, core, step, k):
        place = self.place
        return self.rows.at[core, (place.y + step + LINES) % LINES, (place.z - k + ZEDS) % ZEDS]

    def pass_on(self, step, k, send_sem, recv_sem, device):
        ref = self.block(self.place.core, step, k)
        copy = remote(ref, ref, send_sem, recv_sem, device)
        copy.start()
        self.waits.append(copy)

    def arrived(self, core, step, k, send_sem, recv_sem):
        ref = self.block(core, step, k)
        remote(ref, ref, send_sem, recv_sem, self.place.sibling()).wait_recv()

    def share(self, step, k):
        index = step % LINES * ZEDS + k
        self.pass_on(
            step, k, self.share_send.at[index], self.share_recv.at[index], self.place.sibling()
        )

    def start(self):
        self.own_copy().start()
        for k in SWEEP[1:]:
            self.z_copy(k).start()

    def step(self, m):
        place, core = self.place, self.place.core
        if m < ZEDS:
            k = SWEEP[m]
            if k == 0:
                self.own_copy().wait()
            else:
                self.arrived(core, 0, k, self.z_send.at[k], self.z_recv.at[k])
            for way, step in ((0, 1), (1, -1)):
                self.pass_on(0, k, self.y_send.at[way, k], self.y_recv.at[way, k], place.line(step))
            self.share(0, k)
        if 0 <= m - LAG // 2 < ZEDS:
            i = m - LAG // 2
            k = SWEEP[i]
            for way, step in ((0, 1), (1, -1)):
                self.arrived(core, -step, k, self.y_send.at[way, k], self.y_recv.at[way, k])
                if i % 2 == way:
                    self.pass_on(-step, k, self.y_send.at[2, k], self.y_recv.at[2, k], place.line(step))
                self.share(-step, k)
        if 0 <= m - LAG < ZEDS:
            k = SWEEP[m - LAG]
            self.arrived(core, 2, k, self.y_send.at[2, k], self.y_recv.at[2, k])
            self.share(2, k)

    def arrive(self):
        for step in range(LINES):
            for k in range(ZEDS):
                index = step * ZEDS + k
                self.arrived(
                    1 - self.place.core, step, k, self.share_send.at[index], self.share_recv.at[index]
                )

    def finish(self):
        for k in SWEEP[1:]:
            self.z_copy(k).wait_send()
        for copy in self.waits:
            copy.wait_send()


def first_kernel(
    frames_ref,
    taps_ref,
    w_in_ref,
    w_out_ref,
    u_ref,
    o_ref,
    conv_ref,
    wide_ref,
    lags_ref,
    w_in_share,
    w_out_share,
    rows_ref,
    near_held,
    far_held,
    w_in_mid,
    w_out_mid,
    rims,
    near_send,
    near_recv,
    far_send,
    far_recv,
    y_sems,
    z_sems,
    rim_send,
    rim_recv,
    *spread_sems,
):
    groups, place = Groups(), Place()
    length = frames_ref.shape[0]
    tm, tm_size = groups.tm, lax.axis_size("tm")
    after, before = (groups.dp, (tm + 1) % tm_size), (groups.dp, (tm + tm_size - 1) % tm_size)
    spread = Spread(place, u_ref, rows_ref, spread_sems)
    line = work_line(place)
    zed = place.z // HALF * HALF + home_line(place)
    y_hops, z_hops = [], []
    cargo = ((w_in_ref, w_in_mid, w_in_share), (w_out_ref, w_out_mid, w_out_share))
    for i, (source, mid, share) in enumerate(cargo):
        depth = share.shape[0]
        mine = source.at[pl.ds(pl.multiple_of(place.dp * depth, depth), depth)]
        y_hops.append(Hop(mine, mid, line == place.y, place.at(line, place.z, place.core), y_sems.at[i]))
        z_hops.append(Hop(mid, share, zed == place.z, place.zed(zed), z_sems.at[i]))
    rim_copies = [
        remote(
            frames_ref.at[pl.ds(rows, SIDE)], rims.at[side], rim_send.at[side], rim_recv.at[side], device
        )
        for side, rows, device in ((0, length - SIDE, after), (1, 0, before))
    ]
    mine = near_held.at[groups.near_rank]
    near = Trade(
        groups.near_size, groups.near_rank, groups.near, lambda p: mine, near_held, near_send, near_recv
    )
    mine_far = far_held.at[groups.far_rank]
    far = Trade(
        groups.far_size, groups.far_rank, groups.far, lambda p: mine_far, far_held, far_send, far_recv
    )
    groups.wait(groups.greet((after, before)))
    for copy in rim_copies:
        copy.start()
    spread.start()
    for hop in y_hops:
        hop.start()
    wide_ref[pl.ds(SIDE, length)] = frames_ref[...].astype(jnp.float32)
    for copy in rim_copies:
        copy.wait_recv()
    for side, rows, edge in ((0, 0, tm == 0), (1, SIDE + length, tm == tm_size - 1)):
        wide_ref[pl.ds(rows, SIDE)] = jnp.where(edge, 0.0, rims[side].astype(jnp.float32))

    def columns_of(j, carry):
        columns = pl.ds(pl.multiple_of(j * 128, 128), 128)
        value = jnp.zeros((length, 128), jnp.float32)
        for lag in range(TAPS):
            start = SIDE - TAPS // 2 + lag
            value = value + taps_ref[pl.ds(lag, 1), columns] * wide_ref[pl.ds(start, length), columns]
        conv_ref[:, columns] = value
        mean = jnp.sum(value, axis=0, keepdims=True) / length
        spread_out = value - mean
        near_held[groups.near_rank, pl.ds(0, 1), columns] = mean
        near_held[groups.near_rank, pl.ds(1, 1), columns] = jnp.sum(
            spread_out * spread_out, axis=0, keepdims=True
        )
        return carry

    def lags_of(j, carry):
        columns = pl.ds(pl.multiple_of(j * 128, 128), 128)
        mean = near_held[groups.near_rank, pl.ds(0, 1), columns]
        value = conv_ref[:, columns] - mean
        for lag in range(TAPS):
            shifted = wide_ref[pl.ds(SIDE - TAPS // 2 + lag, length), columns]
            place_row(lags_ref, lag, columns, jnp.sum(shifted, axis=0, keepdims=True))
            place_row(lags_ref, TAPS + lag, columns, jnp.sum(value * shifted, axis=0, keepdims=True))
        return carry

    tiles = frames_ref.shape[1] // 128
    for m in range(3):
        spread.step(m)
        lax.fori_loop(m * tiles // 3, (m + 1) * tiles // 3, columns_of, 0)
    near.start()
    zeros = jnp.zeros((1, D), jnp.float32)
    for row in range(2 * TAPS, lags_ref.shape[0] * lags_ref.shape[1]):
        place_row(lags_ref, row, pl.ds(0, D), zeros)
    for m in range(3, 6):
        spread.step(m)
        lax.fori_loop((m - 3) * tiles // 3, (m - 2) * tiles // 3, lags_of, 0)
    near.finish()
    far_held[groups.far_rank] = moments_merge(near_held[...], float(length))
    far.start()
    for m in range(6, 8):
        spread.step(m)
    for y_hop, z_hop in zip(y_hops, z_hops):
        y_hop.finish()
        z_hop.start()
    far.finish()
    moments = moments_merge(far_held[...], float(length * groups.near_size))
    o_ref[...] = moments
    scale = lax.rsqrt(moments[1:] / (length * groups.near_size * groups.far_size) + EPS)
    shift = near_held[groups.near_rank, pl.ds(0, 1), :] - moments[:1]
    for lag in range(TAPS):
        value = row_of(lags_ref, TAPS + lag) + shift * row_of(lags_ref, lag)
        place_row(lags_ref, TAPS + lag, pl.ds(0, D), scale * value)
    for m in range(8, ZEDS + LAG):
        spread.step(m)
    spread.arrive()
    for hop in z_hops:
        hop.finish()
    for copy in rim_copies:
        copy.wait_send()
    spread.finish()


def first_step(frames, taps, w_in, w_out, u, collective_id):
    dp_size = lax.axis_size("dp")
    far_size = dp_size * (lax.axis_size("tm") // NEAR)
    shares = [
        jax.ShapeDtypeStruct((w.shape[0] // dp_size, w.shape[1]), w.dtype) for w in (w_in, w_out)
    ]
    f32, dma = jnp.float32, pltpu.SemaphoreType.DMA
    length = frames.shape[0]
    vmem, anywhere = pl.BlockSpec(memory_space=pltpu.VMEM), pl.BlockSpec(memory_space=pl.ANY)
    return pl.pallas_call(
        first_kernel,
        out_shape=(
            jax.ShapeDtypeStruct((2, D), f32),
            jax.ShapeDtypeStruct((length, D), f32),
            jax.ShapeDtypeStruct((length + 2 * SIDE, D), f32),
            jax.ShapeDtypeStruct((NEAR, -(-2 * TAPS // NEAR), D), f32),
            *shares,
            jax.ShapeDtypeStruct((CORES, LINES) + u.shape, u.dtype),
        ),
        in_specs=[vmem] * 2 + [anywhere] * 3,
        out_specs=[vmem] * 4 + [anywhere] * 3,
        scratch_shapes=[
            pltpu.VMEM((NEAR, 2, D), f32),
            pltpu.VMEM((far_size, 2, D), f32),
            *[pltpu.VMEM(share.shape, share.dtype) for share in shares],
            pltpu.VMEM((2, SIDE, D), frames.dtype),
            dma((NEAR,)),
            dma((NEAR,)),
            dma((far_size,)),
            dma((far_size,)),
            dma((2, 3)),
            dma((2, 3)),
            dma((2,)),
            dma((2,)),
            *[dma(shape) for shape in Spread.SEMS],
        ],
        compiler_params=pltpu.CompilerParams(
            collective_id=collective_id, has_side_effects=True, vmem_limit_bytes=24 << 20
        ),
    )(frames, taps, w_in, w_out, u)


def last_kernel(
    count,
    signal_ref,
    grad_ref,
    norm_ref,
    resid_ref,
    scale_ref,
    taps_ref,
    g0_ref,
    g1_ref,
    o_ref,
    frames_ref,
    h0_ref,
    h1_ref,
    near_held,
    far_held,
    mids,
    rims,
    wide,
    x_ref,
    near_send,
    near_recv,
    far_send,
    far_recv,
    out_send,
    out_recv,
    y_sems,
    z_sems,
    rim_send,
    rim_recv,
):
    groups, place = Groups(), Place()
    rank = groups.near_rank
    length = grad_ref.shape[0]
    tm, tm_size = groups.tm, lax.axis_size("tm")
    after, before = (groups.dp, (tm + 1) % tm_size), (groups.dp, (tm + tm_size - 1) % tm_size)
    half, line = place.z // HALF * HALF, place.z % HALF
    turn = look([entry for row in TURN for entry in row], place.y * HALF + line)
    home = home_line(place)
    y_hops, z_hops = [], []
    for i, (source, target) in enumerate(((g0_ref, h0_ref), (g1_ref, h1_ref))):
        z_hops.append(
            Hop(source, mids.at[i], half + turn == place.z, place.zed(half + turn), z_sems.at[i])
        )
        y_hops.append(
            Hop(mids.at[i], target, home == place.y, place.at(home, place.z, place.core), y_sems.at[i])
        )
    rim_copies = []
    for i, ref in enumerate((grad_ref, norm_ref)):
        for side, rows, device in ((0, length - SIDE, after), (1, 0, before)):
            rim_copies.append(
                remote(
                    ref.at[pl.ds(rows, SIDE)],
                    rims.at[i, side],
                    rim_send.at[i, side],
                    rim_recv.at[i, side],
                    device,
                )
            )
    signals = groups.greet((after, before))
    rows = x_ref.shape[1] - 2

    def lags_of(j, carry):
        columns = pl.ds(pl.multiple_of(j * 128, 128), 128)
        value = grad_ref[:, columns]
        for lag in range(TAPS):
            shifted = signal_ref[pl.ds(SIDE - TAPS // 2 + lag, length), columns]
            x_ref[lag // rows, pl.ds(lag % rows, 1), columns] = jnp.sum(
                value * shifted, axis=0, keepdims=True
            )
        first_row = jnp.sum(value, axis=0, keepdims=True)
        second_row = jnp.sum(value * norm_ref[:, columns], axis=0, keepdims=True)
        for p in range(x_ref.shape[0]):
            x_ref[p, pl.ds(rows, 1), columns] = first_row
            x_ref[p, pl.ds(rows + 1, 1), columns] = second_row
        return carry

    for lag in range(TAPS, rows * x_ref.shape[0]):
        x_ref[lag // rows, pl.ds(lag % rows, 1), :] = jnp.zeros((1, D), jnp.float32)
    lax.fori_loop(0, D // 128, lags_of, 0)
    near_held[rank] = x_ref[rank]
    groups.wait(signals)
    near = Trade(
        groups.near_size, rank, groups.near, lambda p: x_ref.at[p], near_held, near_send, near_recv
    )
    near.start()
    for copy in rim_copies:
        copy.start()
    for hop in z_hops:
        hop.start()
    near.finish()
    far_held[groups.far_rank] = jnp.sum(near_held[...], axis=0)
    mine = far_held.at[groups.far_rank]
    far = Trade(
        groups.far_size, groups.far_rank, groups.far, lambda p: mine, far_held, far_send, far_recv
    )
    far.start()
    for y_hop, z_hop in zip(y_hops, z_hops):
        z_hop.finish()
        y_hop.start()
    for copy in rim_copies:
        copy.wait_recv()
    far.finish()
    total = jnp.sum(far_held[...], axis=0)
    o_ref[rank] = total
    done = o_ref.at[rank]
    out = Trade(groups.near_size, rank, groups.near, lambda p: done, o_ref, out_send, out_recv)
    out.start()
    first, second = total[-2:-1] / count, total[-1:] / count

    def conv_gradient(grad, norm):
        value = scale_ref[...] * (grad - first - norm * second)
        return value.astype(jnp.bfloat16).astype(jnp.float32)

    for side, rows, edge in ((0, 0, tm == 0), (1, SIDE + length, tm == tm_size - 1)):
        value = conv_gradient(rims[0, side], rims[1, side])
        wide[pl.ds(rows, SIDE)] = jnp.where(edge, 0.0, value)
    wide[pl.ds(SIDE, length)] = conv_gradient(grad_ref[...], norm_ref[...])

    def columns_of(j, carry):
        columns = pl.ds(pl.multiple_of(j * 128, 128), 128)
        value = resid_ref[:, columns]
        for lag in range(TAPS):
            start = SIDE + TAPS // 2 - lag
            value = value + taps_ref[pl.ds(lag, 1), columns] * wide[pl.ds(start, length), columns]
        frames_ref[:, columns] = value.astype(frames_ref.dtype)
        return carry

    lax.fori_loop(0, resid_ref.shape[1] // 128, columns_of, 0)
    out.finish()
    for hop in y_hops:
        hop.finish()
    for copy in rim_copies:
        copy.wait_send()


def last_step(signal, grad, norm, resid, scale, taps, g0, g1, count, collective_id):
    far_size = lax.axis_size("dp") * (lax.axis_size("tm") // NEAR)
    length, f32, dma = grad.shape[0], jnp.float32, pltpu.SemaphoreType.DMA
    sums = jax.ShapeDtypeStruct((NEAR, -(-TAPS // NEAR) + 2, D), f32)
    gradient = jax.ShapeDtypeStruct(g0.shape, g0.dtype)
    vmem, anywhere = pl.BlockSpec(memory_space=pltpu.VMEM), pl.BlockSpec(memory_space=pl.ANY)
    return pl.pallas_call(
        functools.partial(last_kernel, count),
        out_shape=(
            sums,
            jax.ShapeDtypeStruct(grad.shape, jnp.bfloat16),
            gradient,
            gradient,
        ),
        in_specs=[vmem] * 6 + [anywhere] * 2,
        out_specs=[vmem] * 2 + [anywhere] * 2,
        scratch_shapes=[
            pltpu.VMEM(sums.shape, f32),
            pltpu.VMEM((far_size,) + sums.shape[1:], f32),
            pltpu.VMEM((2,) + g0.shape, g0.dtype),
            pltpu.VMEM((2, 2, SIDE, D), f32),
            pltpu.VMEM((length + 2 * SIDE, D), f32),
            pltpu.VMEM(sums.shape, f32),
            dma((NEAR,)),
            dma((NEAR,)),
            dma((far_size,)),
            dma((far_size,)),
            dma((NEAR,)),
            dma((NEAR,)),
            dma((2, 3)),
            dma((2, 3)),
            dma((2, 2)),
            dma((2, 2)),
        ],
        compiler_params=pltpu.CompilerParams(
            collective_id=collective_id, has_side_effects=True, vmem_limit_bytes=24 << 20
        ),
    )(signal, grad, norm, resid, scale, taps, g0, g1)


STEPS = (2, 1, 3, 0)
PART = HALF // 2
WIDE = 512
EXTRA = 128


def experts_kernel(shares, x_ref, rows_ref, in_share, out_share, lags_ref, *refs):
    o_refs, g_refs, sums_ref, refs = refs[:2], refs[2:4], refs[4], refs[5:]
    (
        rows_x,
        rows_u,
        w_in,
        w_out,
        pre_held,
        hid_held,
        dpre_held,
        results,
        pair_held,
        line_held,
        gradient,
        parting,
        parts,
        near_held,
        far_held,
        near_send,
        near_recv,
        far_send,
        far_recv,
        out_send,
        out_recv,
        weight_own,
        weight_send,
        weight_recv,
        part_send,
        part_recv,
        load_sem,
        pair_send,
        pair_recv,
        y_send,
        y_recv,
        z_send,
        z_recv,
    ) = refs[:33]
    place, groups = Place(), Groups()
    y, z, core = place.y, place.z, place.core
    spread = Spread(place, x_ref, rows_x, refs[33:])
    rank = groups.near_rank
    near_held[rank] = lags_ref[rank]
    near = Trade(
        groups.near_size, rank, groups.near, lambda p: lags_ref.at[p], near_held, near_send, near_recv
    )
    mine = far_held.at[groups.far_rank]
    far = Trade(
        groups.far_size, groups.far_rank, groups.far, lambda p: mine, far_held, far_send, far_recv
    )
    done = sums_ref.at[rank]
    out = Trade(groups.near_size, rank, groups.near, lambda p: done, sums_ref, out_send, out_recv)
    weights = ((in_share, w_in), (out_share, w_out))

    def load_copy():
        return pltpu.make_async_copy(rows_ref, rows_u, load_sem.at[0])

    def weight_own_copy(i):
        share, held = weights[i]
        return pltpu.make_async_copy(share, held.at[place.dp], weight_own.at[i])

    def weight_copy(i, step):
        share, held = weights[i]
        return remote(
            share,
            held.at[place.dp],
            weight_send.at[i, step],
            weight_recv.at[i, step],
            place.on_dp(place.other_dp(step)),
        )

    def weights_arrive():
        for i, (_, held) in enumerate(weights):
            weight_own_copy(i).wait()
            for step in range(1, shares):
                ref = held.at[place.other_dp(-step)]
                remote(
                    ref, ref, weight_send.at[i, step], weight_recv.at[i, step], place.sibling()
                ).wait_recv()


    def chunk_of(ref, step, half, start=0, width=None):
        width = ref.shape[-1] if width is None else width
        return ref.at[:, (y + step) % LINES, pl.ds(half * HALF, HALF), :, pl.ds(start, width)]

    def flat(value):
        return value.reshape(-1, value.shape[-1])

    def keep(ref, step, half, value):
        target = chunk_of(ref, step, half)
        target[...] = value.astype(ref.dtype).reshape(target.shape)

    def put(a, step, half, columns, value):
        target = results.at[a, step, half, :, :, :, pl.ds(columns, WIDE)]
        target[...] = value.astype(results.dtype).reshape(target.shape)

    w_in_rows, w_out_rows = w_in.shape[1] * shares, w_out.shape[1] * shares

    def forward(step, half):
        pre = jnp.dot(
            flat(chunk_of(rows_x, step, half, 0, D)[...]),
            w_in[...].reshape(w_in_rows, -1),
            preferred_element_type=jnp.float32,
        )
        keep(pre_held, step, half, pre)
        hidden = (pre * jax.nn.sigmoid(pre)).astype(jnp.bfloat16)
        keep(hid_held, step, half, hidden)
        for columns in range(0, D, WIDE):
            block = w_out[:, :, pl.ds(columns, WIDE)].reshape(w_out_rows, WIDE)
            put(0, step, half, columns, jnp.dot(hidden, block, preferred_element_type=jnp.float32))

    def backward(step, half):
        gates = flat(chunk_of(rows_x, step, half, D, EXTRA)[...]).astype(jnp.float32)
        gates = gates[:, :1] + gates[:, EXTRA // 2 : EXTRA // 2 + 1]
        upstream = flat(chunk_of(rows_u, step, half)[...]).astype(jnp.float32)
        sent = (upstream * gates).astype(jnp.bfloat16)
        keep(rows_u, step, half, sent)
        dhidden = lax.dot_general(
            sent,
            w_out[...].reshape(w_out_rows, -1),
            CONTRACT_COLS,
            preferred_element_type=jnp.float32,
        )
        dpre = (dhidden * swish_slope(flat(chunk_of(pre_held, step, half)[...]))).astype(jnp.bfloat16)
        keep(dpre_held, step, half, dpre)
        weights_all = w_in[...].reshape(w_in_rows, -1)
        for columns in range(0, D, WIDE):
            block = weights_all[columns : columns + WIDE]
            put(
                1,
                step,
                half,
                columns,
                lax.dot_general(dpre, block, CONTRACT_COLS, preferred_element_type=jnp.float32),
            )

    def part_copy(i, step):
        target = place.other_dp(step)
        return remote(
            parting.at[i, target],
            parts.at[i, place.dp],
            part_send.at[i, step],
            part_recv.at[i, step],
            place.on_dp(target),
        )

    def weight_gradient(i, left, right):
        def line(step, carry):
            for columns in range(0, D, WIDE):
                value = lax.dot_general(
                    flat(left[:, step]),
                    flat(right[:, step, :, :, pl.ds(columns, WIDE)]),
                    CONTRACT_ROWS,
                    preferred_element_type=jnp.float32,
                )
                gradient[:, pl.ds(columns, WIDE)] += value
            return carry

        gradient[...] = jnp.zeros_like(gradient)
        lax.fori_loop(0, LINES, line, 0)
        width = D // shares
        for part in range(shares):
            parting[i, part] = gradient[:, part * width : (part + 1) * width].astype(parting.dtype)
        for step in range(1, shares):
            part_copy(i, step).start()

    def gather_gradient(i):
        total = parting[i, place.dp].astype(jnp.float32)
        for step in range(1, shares):
            origin = place.other_dp(-step)
            ref = parts.at[i, origin]
            remote(
                ref, ref, part_send.at[i, step], part_recv.at[i, step], place.sibling()
            ).wait_recv()
            total = total + parts[i, origin].astype(jnp.float32)
        g_refs[i][...] = total.astype(g_refs[i].dtype)


    def pair_copy(a, step, half):
        return remote(
            results.at[a, step, half, 1 - core],
            pair_held.at[a, step, half],
            pair_send.at[a, step, half],
            pair_recv.at[a, step, half],
            place.sibling(),
        )

    def way(step, part):
        return {2: (1, -1)[part], 1: 1, 3: -1}[step]

    def y_copy(a, step, half, part):
        blocks = pl.ds(part * PART, PART)
        return remote(
            results.at[a, step, half, core, blocks],
            line_held.at[a, step - 1, half, blocks],
            y_send.at[a, step, half, part],
            y_recv.at[a, step, half, part],
            place.line(way(step, part)),
        )

    def z_copy(a, target):
        source = results.at[a, 0, target // HALF, core, target % HALF]
        return remote(source, o_refs[a].at[z], z_send.at[a, target], z_recv.at[a, z], place.zed(target))

    def settle(a, step, half, part, extras):
        for extra in extras:
            y_copy(a, extra, half, part).wait_recv()

        def one(j, carry):
            value = results[a, step, half, core, j].astype(jnp.float32)
            value = value + pair_held[a, step, half, j].astype(jnp.float32)
            for extra in extras:
                value = value + line_held[a, extra - 1, half, j].astype(jnp.float32)
            results[a, step, half, core, j] = value.astype(results.dtype)
            return carry

        lax.fori_loop(part * PART, (part + 1) * PART, one, 0)

    def leave(a, step, half, part, extras=()):
        settle(a, step, half, part, extras)
        y_copy(a, step, half, part).start()

    def work(a, half):
        make = (forward, backward)[a]
        before = None
        for step in STEPS:
            make(step, half)
            pair_copy(a, step, half).start()
            if before is not None:
                pair_copy(a, before, half).wait_recv()
            if before == 2:
                leave(a, 2, half, 0)
                leave(a, 2, half, 1)
            elif before == 1:
                leave(a, 1, half, 1)
            elif before == 3:
                leave(a, 3, half, 0)
            before = step
        pair_copy(a, 0, half).wait_recv()

    def relay(a, half):
        leave(a, 1, half, 0, (2,))
        leave(a, 3, half, 1, (2,))

    def finish(a, half):
        for part in (1, 0):
            settle(a, 0, half, part, (1, 3))
        for j in range(HALF):
            target = half * HALF + j

            @pl.when(target != z)
            def _():
                z_copy(a, target).start()

            @pl.when(target == z)
            def _():
                o_refs[a][target] = results[a, 0, half, core, j]

    groups.wait(groups.greet())
    spread.start()
    for i in range(2):
        weight_own_copy(i).start()
        for step in range(1, shares):
            weight_copy(i, step).start()
    load_copy().start()
    for m in range(ZEDS):
        spread.step(m)
    near.start()
    for m in range(ZEDS, ZEDS + LAG):
        spread.step(m)
    spread.arrive()
    weights_arrive()
    load_copy().wait()
    work(0, 0)
    near.finish()
    far_held[groups.far_rank] = jnp.sum(near_held[...], axis=0)
    far.start()
    work(0, 1)
    relay(0, 0)
    far.finish()
    sums_ref[rank] = jnp.sum(far_held[...], axis=0)
    out.start()
    work(1, 0)
    relay(0, 1)
    finish(0, 0)
    work(1, 1)
    relay(1, 0)
    weight_gradient(1, hid_held, rows_u)
    finish(0, 1)
    relay(1, 1)
    weight_gradient(0, dpre_held, rows_x)
    finish(1, 0)
    finish(1, 1)
    for i in (1, 0):
        gather_gradient(i)
    out.finish()
    for a in range(2):
        for k in range(1, ZEDS):
            other = (z + k) % ZEDS
            ref = o_refs[a].at[other]
            remote(ref, ref, z_send.at[a, other], z_recv.at[a, other], place.zed(other)).wait_recv()
    for a in range(2):
        for half in range(2):
            for step in STEPS:
                pair_copy(a, step, half).wait_send()
                for part in range(2):
                    if step != 0:
                        y_copy(a, step, half, part).wait_send()
        for k in range(1, ZEDS):
            z_copy(a, (z + k) % ZEDS).wait_send()
    spread.finish()
    for i in range(2):
        for step in range(1, shares):
            weight_copy(i, step).wait_send()
            part_copy(i, step).wait_send()


def experts(x, rows_u, in_share, out_share, lags, collective_id):
    shares = lax.axis_size("dp")
    hidden = in_share.shape[1]
    slots = x.shape[1]
    lines = (CORES, LINES, ZEDS)
    chunk = (HALF, slots, D)
    bf16, f32, dma = jnp.bfloat16, jnp.float32, pltpu.SemaphoreType.DMA
    out = jax.ShapeDtypeStruct((ZEDS, slots, D), bf16)
    gradient = jax.ShapeDtypeStruct((hidden, D // shares), bf16)
    held = lines + (slots, hidden)
    far_size = shares * (lax.axis_size("tm") // NEAR)
    sems = [
        (NEAR,),
        (NEAR,),
        (far_size,),
        (far_size,),
        (NEAR,),
        (NEAR,),
        (2,),
        (2, shares),
        (2, shares),
        (2, shares),
        (2, shares),
        (1,),
        (2, LINES, 2),
        (2, LINES, 2),
        (2, LINES, 2, 2),
        (2, LINES, 2, 2),
        (2, ZEDS),
        (2, ZEDS),
        *Spread.SEMS,
    ]
    vmem, anywhere = pl.BlockSpec(memory_space=pltpu.VMEM), pl.BlockSpec(memory_space=pl.ANY)
    return pl.pallas_call(
        functools.partial(experts_kernel, shares),
        out_shape=(out, out, gradient, gradient, jax.ShapeDtypeStruct(lags.shape, lags.dtype)),
        in_specs=[anywhere] * 4 + [vmem],
        out_specs=[vmem] * 5,
        scratch_shapes=[
            pltpu.VMEM(lines + x.shape[1:], bf16),
            pltpu.VMEM(lines + (slots, D), bf16),
            pltpu.VMEM((shares,) + in_share.shape, bf16),
            pltpu.VMEM((shares,) + out_share.shape, bf16),
            pltpu.VMEM(held, f32),
            pltpu.VMEM(held, bf16),
            pltpu.VMEM(held, bf16),
            pltpu.VMEM((2, LINES, 2, CORES) + chunk, bf16),
            pltpu.VMEM((2, LINES, 2) + chunk, bf16),
            pltpu.VMEM((2, LINES - 1, 2) + chunk, bf16),
            pltpu.VMEM((hidden, D), f32),
            pltpu.VMEM((2, shares) + gradient.shape, bf16),
            pltpu.VMEM((2, shares) + gradient.shape, bf16),
            pltpu.VMEM(lags.shape, lags.dtype),
            pltpu.VMEM((far_size,) + lags.shape[1:], lags.dtype),
        ]
        + [dma(shape) for shape in sems],
        compiler_params=pltpu.CompilerParams(
            collective_id=collective_id, has_side_effects=True, vmem_limit_bytes=60 << 20
        ),
    )(x, rows_u, in_share, out_share, lags)


def body(
    frames,
    taps,
    batchnorm_gain_scale,
    batchnorm_shift_bias,
    w_router,
    w_in,
    w_out,
    choices,
    cotangent,
):
    length = frames.shape[1]
    element_count = lax.axis_size("dp") * lax.axis_size("tm") * length
    capacity = length * TOP // EXPERTS
    ids = choices[0]
    onehot = (ids[:, :, None] == jnp.arange(EXPERTS, dtype=jnp.int32)[None, None, :]).astype(
        jnp.float32
    )
    flat_ids = ids.reshape(-1)
    expert_hot = (flat_ids[:, None] == jnp.arange(EXPERTS, dtype=jnp.int32)[None, :]).astype(
        jnp.int32
    )
    slots = jnp.sum((jnp.cumsum(expert_hot, axis=0) - 1) * expert_hot, axis=1)
    places = (position(flat_ids) * capacity + slots).reshape(length, TOP)
    place_hot = places[:, :, None] == jnp.arange(EXPERTS * capacity, dtype=jnp.int32)[None, None, :]
    place_any = jnp.any(place_hot, axis=1).astype(jnp.bfloat16)
    place_hot = place_hot.astype(jnp.float32)

    def bucketed(rows):
        return lax.dot_general(place_any, rows, CONTRACT_ROWS, preferred_element_type=jnp.float32)

    up_buffer = bucketed(cotangent[0]).astype(jnp.bfloat16).reshape(EXPERTS, capacity, D)
    moments, conv, wide, lags, w_in_share, w_out_share, rows_u = first_step(
        frames[0], taps, w_in, w_out, up_buffer, 0
    )
    signal = frames[0].astype(jnp.float32)
    mean, variance = moments[0], moments[1] / element_count
    centered_values = conv - mean
    inverse_deviation = lax.rsqrt(variance + EPS)
    normalized_input = centered_values * inverse_deviation
    before_activation = normalized_input * batchnorm_gain_scale + batchnorm_shift_bias
    resid = signal + jax.nn.silu(before_activation)
    lcent = resid - jnp.mean(resid, axis=-1, keepdims=True)
    lrstd = lax.rsqrt(jnp.mean(lcent * lcent, axis=-1, keepdims=True) + EPS)
    vhat = lcent * lrstd
    normed = vhat.astype(jnp.bfloat16)
    logits = jnp.dot(normed, w_router, preferred_element_type=jnp.float32)
    picked = jnp.sum(onehot * logits[:, None, :], axis=-1)
    first = jax.nn.sigmoid(picked[:, 0] - picked[:, 1])
    gates = jnp.stack([first, 1.0 - first], axis=1)
    gate_rows = jnp.sum(place_hot * gates[:, :, None], axis=(0, 1))

    gate_high = lax.reduce_precision(gate_rows, 8, 7)
    gate_parts = jnp.stack([gate_high, gate_rows - gate_high], axis=1).astype(jnp.bfloat16)
    buffer = jnp.concatenate(
        [bucketed(normed).astype(jnp.bfloat16), jnp.repeat(gate_parts, EXTRA // 2, axis=1)], axis=1
    ).reshape(EXPERTS, capacity, D + EXTRA)
    combined, back, grad_in_local, grad_out_local, lags = experts(
        buffer, rows_u, w_in_share, w_out_share, lags, 1
    )
    combined = combined.reshape(EXPERTS * capacity, D).astype(jnp.float32)
    back = back.reshape(EXPERTS * capacity, D).astype(jnp.float32)
    expert_out = [
        jnp.dot(place_hot[:, k], combined, precision=EXACT) for k in range(TOP)
    ]
    mixed = (resid + sum(gates[:, k, None] * expert_out[k] for k in range(TOP))).astype(jnp.bfloat16)
    upstream = cotangent[0].astype(jnp.float32)
    dgate = [jnp.sum(upstream * expert_out[k], axis=-1) for k in range(TOP)]
    dpick = (dgate[0] - dgate[1]) * first * (1.0 - first)
    dlogits = (onehot[:, 0] - onehot[:, 1]) * dpick[:, None]
    dnormed = jnp.dot(dlogits, w_router.astype(jnp.float32).T, precision=EXACT)
    dnormed = dnormed + jnp.dot(jnp.sum(place_hot, axis=1), back, precision=EXACT)
    dmean = jnp.mean(dnormed, axis=-1, keepdims=True)
    dproj = jnp.mean(dnormed * vhat, axis=-1, keepdims=True)
    dresid = upstream + lrstd * (dnormed - dmean - vhat * dproj)
    normalized_gradient = dresid * swish_slope(before_activation) * batchnorm_gain_scale
    summed, grad_frames, grad_w_in, grad_w_out = last_step(
        wide,
        normalized_gradient,
        normalized_input,
        dresid,
        inverse_deviation[None],
        taps,
        grad_in_local,
        grad_out_local,
        element_count,
        2,
    )
    lag_rows = lags.reshape(-1, D)
    grad_taps = inverse_deviation * (
        summed[:, :-2].reshape(-1, D)[:TAPS]
        - summed[0, -2] / element_count * lag_rows[:TAPS]
        - summed[0, -1] / element_count * lag_rows[TAPS : 2 * TAPS]
    )
    grad_w_in, grad_w_out = grad_w_in.T.astype(jnp.float32), grad_w_out.astype(jnp.float32)
    return (mixed[None], grad_frames[None], grad_taps, grad_w_in, grad_w_out)


def solution(mesh):
    return jax.shard_map(
        body,
        mesh=mesh,
        in_specs=(
            P("dp", "tm", None),
            P(),
            P(),
            P(),
            P(),
            P(None, "tm"),
            P("tm", None),
            P("dp", "tm", None),
            P("dp", "tm", None),
        ),
        out_specs=(P("dp", "tm", None), P("dp", "tm", None), P(), P("dp", "tm"), P("tm", "dp")),
        check_vma=False,
    )
```

```python
import functools

import jax
import jax.numpy as jnp
from jax import lax
from jax.experimental import pallas as pl
from jax.experimental.pallas import tpu as pltpu
from jax.sharding import PartitionSpec as P

D = 1536
EXPERTS = 8
TOP = 2
TAPS = 31
EPS = 1e-05
NEAR = 16
MESH = pl.DeviceIdType.MESH
CONTRACT_ROWS = (((0,), (0,)), ((), ()))
CONTRACT_COLS = (((1,), (1,)), ((), ()))
EXACT = lax.Precision.HIGHEST


def swish_slope(pre):
    sigma = jax.nn.sigmoid(pre)
    return sigma * (1.0 + pre * (1.0 - sigma))


class Groups:
    def __init__(self):
        dp_size, tm_size = lax.axis_size("dp"), lax.axis_size("tm")
        self.dp, self.tm = lax.axis_index("dp"), lax.axis_index("tm")
        self.lines = tm_size // NEAR
        self.near_size, self.far_size = NEAR, dp_size * self.lines
        self.near_rank = self.tm % NEAR
        self.far_rank = self.dp * self.lines + self.tm // NEAR

    def near(self, rank):
        return (self.dp, (self.tm // NEAR) * NEAR + rank)

    def far(self, rank):
        return (rank // self.lines, (rank % self.lines) * NEAR + self.near_rank)

    def greet(self, others=()):
        barrier = pltpu.get_barrier_semaphore()
        for other in others:
            pl.semaphore_signal(barrier, inc=1, device_id=other, device_id_type=MESH)

        def greet(size, rank, place):
            def step(k, carry):
                pl.semaphore_signal(
                    barrier, inc=1, device_id=place((rank + k) % size), device_id_type=MESH
                )
                return carry

            lax.fori_loop(1, size, step, 0)

        greet(self.near_size, self.near_rank, self.near)
        greet(self.far_size, self.far_rank, self.far)
        return self.near_size + self.far_size - 2 + len(others)

    def wait(self, signals):
        pl.semaphore_wait(pltpu.get_barrier_semaphore(), signals)


CORES = 2
LINES = 4
ZEDS = EXPERTS
SPAN = ZEDS * CORES
HALF = ZEDS // 2
TURN = ((3, 1, 0, 2), (1, 3, 2, 0), (0, 2, 1, 3), (2, 0, 3, 1))
SWEEP = (0, 1, 7, 2, 6, 3, 5, 4)


def position(ids):
    return HALF * (ids % 2) + ids // 2


class Place:
    def __init__(self):
        self.dp, tm = lax.axis_index("dp"), lax.axis_index("tm")
        self.core, self.z, self.y = tm % CORES, (tm // CORES) % ZEDS, tm // SPAN

    def at(self, y, z, core):
        return (self.dp, (y % LINES) * SPAN + z * CORES + core)

    def sibling(self):
        return self.at(self.y, self.z, 1 - self.core)

    def line(self, step):
        return self.at(self.y + step + LINES, self.z, self.core)

    def zed(self, z):
        return self.at(self.y, z, self.core)

    def other_dp(self, step):
        dp_size = lax.axis_size("dp")
        return (self.dp + step + dp_size) % dp_size

    def on_dp(self, dp):
        return (dp, self.at(self.y, self.z, self.core)[1])


def remote(source, target, send_sem, recv_sem, device):
    return pltpu.make_async_remote_copy(
        src_ref=source,
        dst_ref=target,
        send_sem=send_sem,
        recv_sem=recv_sem,
        device_id=device,
        device_id_type=MESH,
    )


class Trade:
    def __init__(self, size, rank, place, source, held, send_sem, recv_sem):
        self.size, self.rank, self.place, self.source = size, rank, place, source
        self.held, self.send_sem, self.recv_sem = held, send_sem, recv_sem

    def copy(self, k):
        peer = (self.rank + k) % self.size
        return remote(
            self.source(peer),
            self.held.at[self.rank],
            self.send_sem.at[k],
            self.recv_sem.at[self.rank],
            self.place(peer),
        )

    def each(self, act):
        def step(k, carry):
            act(k)
            return carry

        lax.fori_loop(1, self.size, step, 0)

    def start(self):
        self.each(lambda k: self.copy(k).start())

    def finish(self):
        def arrival(k):
            origin = (self.rank + k) % self.size
            ref = self.held.at[origin]
            remote(
                ref, ref, self.send_sem.at[k], self.recv_sem.at[origin], self.place(origin)
            ).wait_recv()

        self.each(arrival)
        self.each(lambda k: self.copy(k).wait_send())


class Hop:
    def __init__(self, source, target, stays, device, sems):
        self.stays = stays
        self.local = pltpu.make_async_copy(source, target, sems.at[0])
        self.far = remote(source, target, sems.at[1], sems.at[2], device)

    def start(self):
        pl.when(self.stays)(self.local.start)
        pl.when(jnp.logical_not(self.stays))(self.far.start)

    def finish(self):
        pl.when(self.stays)(self.local.wait)

        @pl.when(jnp.logical_not(self.stays))
        def _():
            self.far.wait_recv()
            self.far.wait_send()


def look(table, index):
    value = table[0]
    for i, entry in enumerate(table):
        value = jnp.where(index == i, entry, value)
    return value


def work_line(place):
    table = [[row[line] for row in TURN].index(turn) for line in range(LINES) for turn in range(HALF)]
    return look(table, place.y * HALF + place.z % HALF)


def home_line(place):
    table = [row.index(turn) for row in TURN for turn in range(HALF)]
    return look(table, place.y * HALF + place.z % HALF)


def moments_merge(held, count):
    means = held[:, 0, :]
    mean = jnp.sum(means, axis=0) / means.shape[0]
    spread = means - mean[None]
    squares = jnp.sum(held[:, 1, :], axis=0) + count * jnp.sum(spread * spread, axis=0)
    return jnp.stack([mean, squares])


SIDE = 16
LAG = 4


def place_row(ref, row, columns, value):
    depth = ref.shape[1]
    ref[row // depth, pl.ds(row % depth, 1), columns] = value


def row_of(ref, row):
    depth = ref.shape[1]
    return ref[row // depth, pl.ds(row % depth, 1), :]


class Spread:
    SEMS = ((1,), (ZEDS,), (ZEDS,), (LINES * ZEDS,), (LINES * ZEDS,), (3, ZEDS), (3, ZEDS))

    def __init__(self, place, source, rows, sems):
        self.place, self.source, self.rows = place, source, rows
        self.own, self.z_send, self.z_recv = sems[:3]
        self.share_send, self.share_recv, self.y_send, self.y_recv = sems[3:]
        self.waits = []

    def z_copy(self, k):
        place = self.place
        target = (place.z + k) % ZEDS
        mine = self.rows.at[place.core, place.y, place.z]
        return remote(
            self.source.at[target], mine, self.z_send.at[k], self.z_recv.at[k], place.zed(target)
        )

    def own_copy(self):
        place = self.place
        mine = self.rows.at[place.core, place.y, place.z]
        return pltpu.make_async_copy(self.source.at[place.z], mine, self.own.at[0])

    def block(self, core, step, k):
        place = self.place
        return self.rows.at[core, (place.y + step + LINES) % LINES, (place.z - k + ZEDS) % ZEDS]

    def pass_on(self, step, k, send_sem, recv_sem, device):
        ref = self.block(self.place.core, step, k)
        copy = remote(ref, ref, send_sem, recv_sem, device)
        copy.start()
        self.waits.append(copy)

    def arrived(self, core, step, k, send_sem, recv_sem):
        ref = self.block(core, step, k)
        remote(ref, ref, send_sem, recv_sem, self.place.sibling()).wait_recv()

    def share(self, step, k):
        index = step % LINES * ZEDS + k
        self.pass_on(
            step, k, self.share_send.at[index], self.share_recv.at[index], self.place.sibling()
        )

    def start(self):
        self.own_copy().start()
        for k in SWEEP[1:]:
            self.z_copy(k).start()

    def step(self, m):
        place, core = self.place, self.place.core
        if m < ZEDS:
            k = SWEEP[m]
            if k == 0:
                self.own_copy().wait()
            else:
                self.arrived(core, 0, k, self.z_send.at[k], self.z_recv.at[k])
            for way, step in ((0, 1), (1, -1)):
                self.pass_on(0, k, self.y_send.at[way, k], self.y_recv.at[way, k], place.line(step))
            self.share(0, k)
        if 0 <= m - LAG // 2 < ZEDS:
            i = m - LAG // 2
            k = SWEEP[i]
            for way, step in ((0, 1), (1, -1)):
                self.arrived(core, -step, k, self.y_send.at[way, k], self.y_recv.at[way, k])
                if i % 2 == way:
                    self.pass_on(-step, k, self.y_send.at[2, k], self.y_recv.at[2, k], place.line(step))
                self.share(-step, k)
        if 0 <= m - LAG < ZEDS:
            k = SWEEP[m - LAG]
            self.arrived(core, 2, k, self.y_send.at[2, k], self.y_recv.at[2, k])
            self.share(2, k)

    def arrive(self):
        for step in range(LINES):
            for k in range(ZEDS):
                index = step * ZEDS + k
                self.arrived(
                    1 - self.place.core, step, k, self.share_send.at[index], self.share_recv.at[index]
                )

    def finish(self):
        for k in SWEEP[1:]:
            self.z_copy(k).wait_send()
        for copy in self.waits:
            copy.wait_send()


def last_kernel(
    count,
    signal_ref,
    grad_ref,
    norm_ref,
    resid_ref,
    scale_ref,
    taps_ref,
    g0_ref,
    g1_ref,
    o_ref,
    frames_ref,
    h0_ref,
    h1_ref,
    near_held,
    far_held,
    mids,
    rims,
    wide,
    x_ref,
    near_send,
    near_recv,
    far_send,
    far_recv,
    out_send,
    out_recv,
    y_sems,
    z_sems,
    rim_send,
    rim_recv,
):
    groups, place = Groups(), Place()
    rank = groups.near_rank
    length = grad_ref.shape[0]
    tm, tm_size = groups.tm, lax.axis_size("tm")
    after, before = (groups.dp, (tm + 1) % tm_size), (groups.dp, (tm + tm_size - 1) % tm_size)
    half, line = place.z // HALF * HALF, place.z % HALF
    turn = look([entry for row in TURN for entry in row], place.y * HALF + line)
    home = home_line(place)
    y_hops, z_hops = [], []
    for i, (source, target) in enumerate(((g0_ref, h0_ref), (g1_ref, h1_ref))):
        z_hops.append(
            Hop(source, mids.at[i], half + turn == place.z, place.zed(half + turn), z_sems.at[i])
        )
        y_hops.append(
            Hop(mids.at[i], target, home == place.y, place.at(home, place.z, place.core), y_sems.at[i])
        )
    rim_copies = []
    for i, ref in enumerate((grad_ref, norm_ref)):
        for side, rows, device in ((0, length - SIDE, after), (1, 0, before)):
            rim_copies.append(
                remote(
                    ref.at[pl.ds(rows, SIDE)],
                    rims.at[i, side],
                    rim_send.at[i, side],
                    rim_recv.at[i, side],
                    device,
                )
            )
    signals = groups.greet((after, before))
    rows = x_ref.shape[1] - 2

    def lags_of(j, carry):
        columns = pl.ds(pl.multiple_of(j * 128, 128), 128)
        value = grad_ref[:, columns]
        for lag in range(TAPS):
            shifted = signal_ref[pl.ds(SIDE - TAPS // 2 + lag, length), columns]
            x_ref[lag // rows, pl.ds(lag % rows, 1), columns] = jnp.sum(
                value * shifted, axis=0, keepdims=True
            )
        first_row = jnp.sum(value, axis=0, keepdims=True)
        second_row = jnp.sum(value * norm_ref[:, columns], axis=0, keepdims=True)
        for p in range(x_ref.shape[0]):
            x_ref[p, pl.ds(rows, 1), columns] = first_row
            x_ref[p, pl.ds(rows + 1, 1), columns] = second_row
        return carry

    for lag in range(TAPS, rows * x_ref.shape[0]):
        x_ref[lag // rows, pl.ds(lag % rows, 1), :] = jnp.zeros((1, D), jnp.float32)
    lax.fori_loop(0, D // 128, lags_of, 0)
    near_held[rank] = x_ref[rank]
    groups.wait(signals)
    near = Trade(
        groups.near_size, rank, groups.near, lambda p: x_ref.at[p], near_held, near_send, near_recv
    )
    near.start()
    for copy in rim_copies:
        copy.start()
    for hop in z_hops:
        hop.start()
    near.finish()
    far_held[groups.far_rank] = jnp.sum(near_held[...], axis=0)
    mine = far_held.at[groups.far_rank]
    far = Trade(
        groups.far_size, groups.far_rank, groups.far, lambda p: mine, far_held, far_send, far_recv
    )
    far.start()
    for y_hop, z_hop in zip(y_hops, z_hops):
        z_hop.finish()
        y_hop.start()
    for copy in rim_copies:
        copy.wait_recv()
    far.finish()
    total = jnp.sum(far_held[...], axis=0)
    o_ref[rank] = total
    done = o_ref.at[rank]
    out = Trade(groups.near_size, rank, groups.near, lambda p: done, o_ref, out_send, out_recv)
    out.start()
    first, second = total[-2:-1] / count, total[-1:] / count

    def conv_gradient(grad, norm):
        value = scale_ref[...] * (grad - first - norm * second)
        return value.astype(jnp.bfloat16).astype(jnp.float32)

    for side, rows, edge in ((0, 0, tm == 0), (1, SIDE + length, tm == tm_size - 1)):
        value = conv_gradient(rims[0, side], rims[1, side])
        wide[pl.ds(rows, SIDE)] = jnp.where(edge, 0.0, value)
    wide[pl.ds(SIDE, length)] = conv_gradient(grad_ref[...], norm_ref[...])

    def columns_of(j, carry):
        columns = pl.ds(pl.multiple_of(j * 128, 128), 128)
        value = resid_ref[:, columns]
        for lag in range(TAPS):
            start = SIDE + TAPS // 2 - lag
            value = value + taps_ref[pl.ds(lag, 1), columns] * wide[pl.ds(start, length), columns]
        frames_ref[:, columns] = value.astype(frames_ref.dtype)
        return carry

    lax.fori_loop(0, resid_ref.shape[1] // 128, columns_of, 0)
    out.finish()
    for hop in y_hops:
        hop.finish()
    for copy in rim_copies:
        copy.wait_send()


def last_step(signal, grad, norm, resid, scale, taps, g0, g1, count, collective_id):
    far_size = lax.axis_size("dp") * (lax.axis_size("tm") // NEAR)
    length, f32, dma = grad.shape[0], jnp.float32, pltpu.SemaphoreType.DMA
    sums = jax.ShapeDtypeStruct((NEAR, -(-TAPS // NEAR) + 2, D), f32)
    gradient = jax.ShapeDtypeStruct(g0.shape, g0.dtype)
    vmem, anywhere = pl.BlockSpec(memory_space=pltpu.VMEM), pl.BlockSpec(memory_space=pl.ANY)
    return pl.pallas_call(
        functools.partial(last_kernel, count),
        out_shape=(
            sums,
            jax.ShapeDtypeStruct(grad.shape, jnp.bfloat16),
            gradient,
            gradient,
        ),
        in_specs=[vmem] * 6 + [anywhere] * 2,
        out_specs=[vmem] * 2 + [anywhere] * 2,
        scratch_shapes=[
            pltpu.VMEM(sums.shape, f32),
            pltpu.VMEM((far_size,) + sums.shape[1:], f32),
            pltpu.VMEM((2,) + g0.shape, g0.dtype),
            pltpu.VMEM((2, 2, SIDE, D), f32),
            pltpu.VMEM((length + 2 * SIDE, D), f32),
            pltpu.VMEM(sums.shape, f32),
            dma((NEAR,)),
            dma((NEAR,)),
            dma((far_size,)),
            dma((far_size,)),
            dma((NEAR,)),
            dma((NEAR,)),
            dma((2, 3)),
            dma((2, 3)),
            dma((2, 2)),
            dma((2, 2)),
        ],
        compiler_params=pltpu.CompilerParams(
            collective_id=collective_id, has_side_effects=True, vmem_limit_bytes=24 << 20
        ),
    )(signal, grad, norm, resid, scale, taps, g0, g1)


STEPS = (2, 1, 3, 0)
PART = HALF // 2
WIDE = 512
EXTRA = 128


def main_kernel(shares, *refs):
    refs = list(refs)

    def take(count):
        taken = refs[:count]
        del refs[:count]
        return taken

    frames_ref, taps_ref, gain_ref, bias_ref, router_ref, choose_ref, hot_ref = take(7)
    w_in_ref, w_out_ref, u_ref = take(3)
    o_refs, g_refs = take(2), take(2)
    sums_ref, moments_ref, wide_ref, norm_ref, resid_ref, vhat_ref, lrstd_ref, gate_ref = take(8)
    x_ref, normed, w_in_mid, w_out_mid, in_share, out_share, rims, lags_ref = take(8)
    rows_x, rows_u, w_in, w_out, hid_held, dpre_held, results, pair_held, line_held = take(9)
    gradient, parting, parts, near_held, far_held, near_moments, far_moments = take(7)
    near_send, near_recv, far_send, far_recv, out_send, out_recv = take(6)
    near_moments_send, near_moments_recv, far_moments_send, far_moments_recv = take(4)
    yhop_sems, zhop_sems, rim_send, rim_recv = take(4)
    weight_own, weight_send, weight_recv, part_send, part_recv = take(5)
    pair_send, pair_recv, y_send, y_recv, z_send, z_recv = take(6)
    place, groups = Place(), Groups()
    y, z, core = place.y, place.z, place.core
    spread_u = Spread(place, u_ref, rows_u, take(len(Spread.SEMS)))
    spread_x = Spread(place, x_ref, rows_x, take(len(Spread.SEMS)))
    length = frames_ref.shape[0]
    count = length * groups.near_size * groups.far_size
    tm, tm_size = groups.tm, lax.axis_size("tm")
    after, before_me = (groups.dp, (tm + 1) % tm_size), (groups.dp, (tm + tm_size - 1) % tm_size)

    line = work_line(place)
    zed = z // HALF * HALF + home_line(place)
    y_hops, z_hops = [], []
    cargo = ((w_in_ref, w_in_mid, in_share), (w_out_ref, w_out_mid, out_share))
    for i, (source, mid, share) in enumerate(cargo):
        depth = share.shape[0]
        part = source.at[pl.ds(pl.multiple_of(place.dp * depth, depth), depth)]
        y_hops.append(Hop(part, mid, line == y, place.at(line, z, core), yhop_sems.at[i]))
        z_hops.append(Hop(mid, share, zed == z, place.zed(zed), zhop_sems.at[i]))
    rim_copies = [
        remote(
            frames_ref.at[pl.ds(rows, SIDE)], rims.at[side], rim_send.at[side], rim_recv.at[side], device
        )
        for side, rows, device in ((0, length - SIDE, after), (1, 0, before_me))
    ]

    def trades(near_ref, far_ref, source, sems):
        mine = far_ref.at[groups.far_rank]
        return (
            Trade(groups.near_size, groups.near_rank, groups.near, source, near_ref, *sems[:2]),
            Trade(groups.far_size, groups.far_rank, groups.far, lambda p: mine, far_ref, *sems[2:]),
        )

    rank = groups.near_rank
    mine_near = near_moments.at[rank]
    moment_sems = (near_moments_send, near_moments_recv, far_moments_send, far_moments_recv)
    moment_near, moment_far = trades(near_moments, far_moments, lambda p: mine_near, moment_sems)
    lag_sems = (near_send, near_recv, far_send, far_recv)
    near, far = trades(near_held, far_held, lambda p: lags_ref.at[p], lag_sems)
    done = sums_ref.at[rank]
    out = Trade(groups.near_size, rank, groups.near, lambda p: done, sums_ref, out_send, out_recv)
    weights = ((in_share, w_in), (out_share, w_out))


    def conv_of(j, carry):
        columns = pl.ds(pl.multiple_of(j * 128, 128), 128)
        value = jnp.zeros((length, 128), jnp.float32)
        for lag in range(TAPS):
            start = SIDE - TAPS // 2 + lag
            value = value + taps_ref[pl.ds(lag, 1), columns] * wide_ref[pl.ds(start, length), columns]
        norm_ref[:, columns] = value
        mean = jnp.sum(value, axis=0, keepdims=True) / length
        centred = value - mean
        near_moments[rank, pl.ds(0, 1), columns] = mean
        near_moments[rank, pl.ds(1, 1), columns] = jnp.sum(centred * centred, axis=0, keepdims=True)
        return carry

    def lags_of(j, carry):
        columns = pl.ds(pl.multiple_of(j * 128, 128), 128)
        value = norm_ref[:, columns] - near_moments[rank, pl.ds(0, 1), columns]
        for lag in range(TAPS):
            shifted = wide_ref[pl.ds(SIDE - TAPS // 2 + lag, length), columns]
            place_row(lags_ref, lag, columns, jnp.sum(shifted, axis=0, keepdims=True))
            place_row(lags_ref, TAPS + lag, columns, jnp.sum(value * shifted, axis=0, keepdims=True))
        return carry

    def normalize(j, carry):
        rows = pl.ds(pl.multiple_of(j * SIDE, SIDE), SIDE)
        norm = (norm_ref[rows] - moments_ref[:1]) * lax.rsqrt(moments_ref[1:] / count + EPS)
        norm_ref[rows] = norm
        pre = norm * gain_ref[...] + bias_ref[...]
        resid = frames_ref[rows].astype(jnp.float32) + pre * jax.nn.sigmoid(pre)
        resid_ref[rows] = resid
        centred = resid - jnp.mean(resid, axis=-1, keepdims=True)
        lrstd = lax.rsqrt(jnp.mean(centred * centred, axis=-1, keepdims=True) + EPS)
        lrstd_ref[rows] = jnp.broadcast_to(lrstd, (SIDE, EXTRA))
        vhat = centred * lrstd
        vhat_ref[rows] = vhat
        normed[rows] = vhat.astype(jnp.bfloat16)
        return carry

    def bucket():
        logits = jnp.dot(normed[...], router_ref[...], preferred_element_type=jnp.float32)
        first = jax.nn.sigmoid(jnp.sum(logits * choose_ref[...], axis=-1, keepdims=True))
        gate_ref[...] = jnp.broadcast_to(first, gate_ref.shape)
        gates = jnp.zeros((hot_ref.shape[2], EXTRA), jnp.float32)
        for k, gate in enumerate((first, 1.0 - first)):
            high = gate.astype(jnp.bfloat16)
            low = (gate - high.astype(jnp.float32)).astype(jnp.bfloat16)
            wide_gate = jnp.concatenate(
                [jnp.broadcast_to(half, (length, EXTRA // 2)) for half in (high, low)], axis=1
            )
            gates = gates + lax.dot_general(
                hot_ref[k], wide_gate, CONTRACT_ROWS, preferred_element_type=jnp.float32
            )
        x_ref[:, :, pl.ds(D, EXTRA)] = gates.astype(jnp.bfloat16).reshape(ZEDS, -1, EXTRA)
        either = hot_ref[0] + hot_ref[1]
        for columns in range(0, D, WIDE):
            value = lax.dot_general(
                either,
                normed[:, pl.ds(columns, WIDE)],
                CONTRACT_ROWS,
                preferred_element_type=jnp.float32,
            )
            x_ref[:, :, pl.ds(columns, WIDE)] = value.astype(jnp.bfloat16).reshape(ZEDS, -1, WIDE)

    def weight_own_copy(i):
        share, held = weights[i]
        return pltpu.make_async_copy(share, held.at[place.dp], weight_own.at[i])

    ways = (1, shares - 1)

    def weight_copy(i, step):
        share, held = weights[i]
        if step == 2:
            origin, step_to = place.other_dp(-ways[i]), ways[i]
            source, slot = held.at[origin], origin
        else:
            source, slot, step_to = share, place.dp, step
        return remote(
            source,
            held.at[slot],
            weight_send.at[i, step],
            weight_recv.at[i, step],
            place.on_dp(place.other_dp(step_to)),
        )

    def weight_arrives(i, step):
        ref = weights[i][1].at[place.other_dp(-step)]
        remote(ref, ref, weight_send.at[i, step], weight_recv.at[i, step], place.sibling()).wait_recv()

    def weights_start():
        for i in range(2):
            weight_own_copy(i).start()
            for step in ways:
                weight_copy(i, step).start()

    def weights_relay():
        for i in range(2):
            weight_arrives(i, ways[i])
            weight_copy(i, 2).start()

    def weights_arrive():
        for i in range(2):
            weight_own_copy(i).wait()
            weight_arrives(i, ways[1 - i])
            weight_arrives(i, 2)


    def chunk_of(ref, step, half, start=0, width=None):
        width = ref.shape[-1] if width is None else width
        return ref.at[:, (y + step) % LINES, pl.ds(half * HALF, HALF), :, pl.ds(start, width)]

    def flat(value):
        return value.reshape(-1, value.shape[-1])

    def keep(ref, step, half, value):
        target = chunk_of(ref, step, half)
        target[...] = value.astype(ref.dtype).reshape(target.shape)

    def put(a, step, half, columns, value):
        target = results.at[a, step, half, :, :, :, pl.ds(columns, WIDE)]
        target[...] = value.astype(results.dtype).reshape(target.shape)

    w_in_rows, w_out_rows = w_in.shape[1] * shares, w_out.shape[1] * shares

    def pre_of(step, half):
        return jnp.dot(
            flat(chunk_of(rows_x, step, half, 0, D)[...]),
            w_in[...].reshape(w_in_rows, -1),
            preferred_element_type=jnp.float32,
        )

    def forward(step, half):
        pre = pre_of(step, half)
        hidden = (pre * jax.nn.sigmoid(pre)).astype(jnp.bfloat16)
        keep(hid_held, step, half, hidden)
        for columns in range(0, D, WIDE):
            block = w_out[:, :, pl.ds(columns, WIDE)].reshape(w_out_rows, WIDE)
            put(0, step, half, columns, jnp.dot(hidden, block, preferred_element_type=jnp.float32))

    def backward(step, half):
        gates = flat(chunk_of(rows_x, step, half, D, EXTRA)[...]).astype(jnp.float32)
        gates = gates[:, :1] + gates[:, EXTRA // 2 : EXTRA // 2 + 1]
        upstream = flat(chunk_of(rows_u, step, half)[...]).astype(jnp.float32)
        sent = (upstream * gates).astype(jnp.bfloat16)
        keep(rows_u, step, half, sent)
        dhidden = lax.dot_general(
            sent,
            w_out[...].reshape(w_out_rows, -1),
            CONTRACT_COLS,
            preferred_element_type=jnp.float32,
        )
        dpre = (dhidden * swish_slope(pre_of(step, half))).astype(jnp.bfloat16)
        keep(dpre_held, step, half, dpre)
        weights_all = w_in[...].reshape(w_in_rows, -1)
        for columns in range(0, D, WIDE):
            block = weights_all[columns : columns + WIDE]
            put(
                1,
                step,
                half,
                columns,
                lax.dot_general(dpre, block, CONTRACT_COLS, preferred_element_type=jnp.float32),
            )

    def part_copy(i, step):
        target = place.other_dp(step)
        return remote(
            parting.at[i, target],
            parts.at[i, place.dp],
            part_send.at[i, step],
            part_recv.at[i, step],
            place.on_dp(target),
        )

    def weight_gradient(i, left, right):
        def line(step, carry):
            for columns in range(0, D, WIDE):
                value = lax.dot_general(
                    flat(left[:, step]),
                    flat(right[:, step, :, :, pl.ds(columns, WIDE)]),
                    CONTRACT_ROWS,
                    preferred_element_type=jnp.float32,
                )
                gradient[:, pl.ds(columns, WIDE)] += value
            return carry

        gradient[...] = jnp.zeros_like(gradient)
        lax.fori_loop(0, LINES, line, 0)
        width = D // shares
        for part in range(shares):
            parting[i, part] = gradient[:, part * width : (part + 1) * width].astype(parting.dtype)
        for step in range(1, shares):
            part_copy(i, step).start()

    def gather_gradient(i):
        total = parting[i, place.dp].astype(jnp.float32)
        for step in range(1, shares):
            origin = place.other_dp(-step)
            ref = parts.at[i, origin]
            remote(
                ref, ref, part_send.at[i, step], part_recv.at[i, step], place.sibling()
            ).wait_recv()
            total = total + parts[i, origin].astype(jnp.float32)
        g_refs[i][...] = total.astype(g_refs[i].dtype)


    def pair_copy(a, step, half):
        return remote(
            results.at[a, step, half, 1 - core],
            pair_held.at[a, step, half],
            pair_send.at[a, step, half],
            pair_recv.at[a, step, half],
            place.sibling(),
        )

    def way(step, part):
        return {2: (1, -1)[part], 1: 1, 3: -1}[step]

    def y_copy(a, step, half, part):
        blocks = pl.ds(part * PART, PART)
        return remote(
            results.at[a, step, half, core, blocks],
            line_held.at[a, step - 1, half, blocks],
            y_send.at[a, step, half, part],
            y_recv.at[a, step, half, part],
            place.line(way(step, part)),
        )

    def z_copy(a, target):
        source = results.at[a, 0, target // HALF, core, target % HALF]
        return remote(source, o_refs[a].at[z], z_send.at[a, target], z_recv.at[a, z], place.zed(target))

    def settle(a, step, half, part, extras):
        for extra in extras:
            y_copy(a, extra, half, part).wait_recv()

        def one(j, carry):
            value = results[a, step, half, core, j].astype(jnp.float32)
            value = value + pair_held[a, step, half, j].astype(jnp.float32)
            for extra in extras:
                value = value + line_held[a, extra - 1, half, j].astype(jnp.float32)
            results[a, step, half, core, j] = value.astype(results.dtype)
            return carry

        lax.fori_loop(part * PART, (part + 1) * PART, one, 0)

    def leave(a, step, half, part, extras=()):
        settle(a, step, half, part, extras)
        y_copy(a, step, half, part).start()

    def work(a, half):
        make = (forward, backward)[a]
        before = None
        for step in STEPS:
            make(step, half)
            pair_copy(a, step, half).start()
            if before is not None:
                pair_copy(a, before, half).wait_recv()
            if before == 2:
                leave(a, 2, half, 0)
                leave(a, 2, half, 1)
            elif before == 1:
                leave(a, 1, half, 1)
            elif before == 3:
                leave(a, 3, half, 0)
            before = step
        pair_copy(a, 0, half).wait_recv()

    def relay(a, half):
        leave(a, 1, half, 0, (2,))
        leave(a, 3, half, 1, (2,))

    def finish(a, half):
        for part in (1, 0):
            settle(a, 0, half, part, (1, 3))
        for j in range(HALF):
            target = half * HALF + j

            @pl.when(target != z)
            def _():
                z_copy(a, target).start()

            @pl.when(target == z)
            def _():
                o_refs[a][target] = results[a, 0, half, core, j]

    signals = groups.greet((after, before_me))
    wide_ref[pl.ds(SIDE, length)] = frames_ref[...].astype(jnp.float32)
    zeros = jnp.zeros((1, D), jnp.float32)
    for row in range(2 * TAPS, lags_ref.shape[0] * lags_ref.shape[1]):
        place_row(lags_ref, row, pl.ds(0, D), zeros)
    groups.wait(signals)
    for copy in rim_copies:
        copy.start()
    spread_u.start()
    for hop in y_hops:
        hop.start()
    for copy in rim_copies:
        copy.wait_recv()
    for side, rows, edge in ((0, 0, tm == 0), (1, SIDE + length, tm == tm_size - 1)):
        wide_ref[pl.ds(rows, SIDE)] = jnp.where(edge, 0.0, rims[side].astype(jnp.float32))
    tiles = D // 128
    for m in range(3):
        spread_u.step(m)
        lax.fori_loop(m * tiles // 3, (m + 1) * tiles // 3, conv_of, 0)
    moment_near.start()
    for m in range(3, 6):
        spread_u.step(m)
        lax.fori_loop((m - 3) * tiles // 3, (m - 2) * tiles // 3, lags_of, 0)
    moment_near.finish()
    far_moments[groups.far_rank] = moments_merge(near_moments[...], float(length))
    moment_far.start()
    for y_hop, z_hop in zip(y_hops, z_hops):
        y_hop.finish()
        z_hop.start()
    for m in range(6, ZEDS):
        spread_u.step(m)
    moment_far.finish()
    moments_ref[...] = moments_merge(far_moments[...], float(length * groups.near_size))
    lax.fori_loop(0, length // SIDE, normalize, 0)
    bucket()
    spread_x.start()
    for hop in z_hops:
        hop.finish()
    weights_start()
    for m in range(ZEDS, ZEDS + LAG):
        spread_u.step(m)
    scale = lax.rsqrt(moments_ref[1:] / count + EPS)
    shift = near_moments[rank, pl.ds(0, 1), :] - moments_ref[:1]
    for lag in range(TAPS):
        value = row_of(lags_ref, TAPS + lag) + shift * row_of(lags_ref, lag)
        place_row(lags_ref, TAPS + lag, pl.ds(0, D), scale * value)
    near_held[rank] = lags_ref[rank]
    for m in range(4):
        spread_x.step(m)
    weights_relay()
    for m in range(4, ZEDS):
        spread_x.step(m)
    near.start()
    for m in range(ZEDS, ZEDS + LAG):
        spread_x.step(m)
    spread_u.arrive()
    spread_u.finish()
    spread_x.arrive()
    weights_arrive()
    work(0, 0)
    near.finish()
    far_held[groups.far_rank] = jnp.sum(near_held[...], axis=0)
    far.start()
    work(0, 1)
    relay(0, 0)
    far.finish()
    sums_ref[rank] = jnp.sum(far_held[...], axis=0)
    out.start()
    work(1, 0)
    relay(0, 1)
    finish(0, 0)
    work(1, 1)
    relay(1, 0)
    weight_gradient(1, hid_held, rows_u)
    finish(0, 1)
    relay(1, 1)
    weight_gradient(0, dpre_held, rows_x)
    finish(1, 0)
    finish(1, 1)
    for i in (1, 0):
        gather_gradient(i)
    out.finish()
    for a in range(2):
        for k in range(1, ZEDS):
            other = (z + k) % ZEDS
            ref = o_refs[a].at[other]
            remote(ref, ref, z_send.at[a, other], z_recv.at[a, other], place.zed(other)).wait_recv()
    for a in range(2):
        for half in range(2):
            for step in STEPS:
                pair_copy(a, step, half).wait_send()
                for part in range(2):
                    if step != 0:
                        y_copy(a, step, half, part).wait_send()
        for k in range(1, ZEDS):
            z_copy(a, (z + k) % ZEDS).wait_send()
    spread_x.finish()
    for copy in rim_copies:
        copy.wait_send()
    for i in range(2):
        for step in range(1, shares):
            weight_copy(i, step).wait_send()
            part_copy(i, step).wait_send()


def main_step(frames, taps, gain, bias, router, choose, hot, w_in, w_out, u, collective_id):
    shares = lax.axis_size("dp")
    hidden, slots, length = w_in.shape[1], u.shape[1], frames.shape[0]
    lines = (CORES, LINES, ZEDS)
    chunk = (HALF, slots, D)
    bf16, f32, dma = jnp.bfloat16, jnp.float32, pltpu.SemaphoreType.DMA
    shape = jax.ShapeDtypeStruct
    gradient = (hidden, D // shares)
    held = lines + (slots, hidden)
    far_size = shares * (lax.axis_size("tm") // NEAR)
    lags = (NEAR, -(-2 * TAPS // NEAR), D)
    in_share, out_share = (w_in.shape[0] // shares, hidden), (w_out.shape[0] // shares, D)
    trade_sems = [(NEAR,), (NEAR,), (far_size,), (far_size,)]
    sems = [
        *trade_sems,
        (NEAR,),
        (NEAR,),
        *trade_sems,
        (2, 3),
        (2, 3),
        (2,),
        (2,),
        (2,),
        (2, shares),
        (2, shares),
        (2, shares),
        (2, shares),
        (2, LINES, 2),
        (2, LINES, 2),
        (2, LINES, 2, 2),
        (2, LINES, 2, 2),
        (2, ZEDS),
        (2, ZEDS),
        *Spread.SEMS,
        *Spread.SEMS,
    ]
    scratch = [
        ((ZEDS, slots, D + EXTRA), bf16),
        ((length, D), bf16),
        (in_share, bf16),
        (out_share, bf16),
        (in_share, bf16),
        (out_share, bf16),
        ((2, SIDE, D), bf16),
        (lags, f32),
        (lines + (slots, D + EXTRA), bf16),
        (lines + (slots, D), bf16),
        ((shares,) + in_share, bf16),
        ((shares,) + out_share, bf16),
        (held, bf16),
        (held, bf16),
        ((2, LINES, 2, CORES) + chunk, bf16),
        ((2, LINES, 2) + chunk, bf16),
        ((2, LINES - 1, 2) + chunk, bf16),
        ((hidden, D), f32),
        ((2, shares) + gradient, bf16),
        ((2, shares) + gradient, bf16),
        (lags, f32),
        ((far_size,) + lags[1:], f32),
        ((NEAR, 2, D), f32),
        ((far_size, 2, D), f32),
    ]
    vmem, anywhere = pl.BlockSpec(memory_space=pltpu.VMEM), pl.BlockSpec(memory_space=pl.ANY)
    outs = (
        [shape((ZEDS, slots, D), bf16)] * 2
        + [shape(gradient, bf16)] * 2
        + [shape(lags, f32), shape((2, D), f32), shape((length + 2 * SIDE, D), f32)]
        + [shape((length, D), f32)] * 3
        + [shape((length, EXTRA), f32)] * 2
    )
    return pl.pallas_call(
        functools.partial(main_kernel, shares),
        out_shape=tuple(outs),
        in_specs=[vmem] * 7 + [anywhere] * 3,
        out_specs=[vmem] * len(outs),
        scratch_shapes=[pltpu.VMEM(*entry) for entry in scratch] + [dma(entry) for entry in sems],
        compiler_params=pltpu.CompilerParams(
            collective_id=collective_id, has_side_effects=True, vmem_limit_bytes=62 << 20
        ),
    )(frames, taps, gain, bias, router, choose, hot, w_in, w_out, u)


def body(
    frames,
    taps,
    batchnorm_gain_scale,
    batchnorm_shift_bias,
    w_router,
    w_in,
    w_out,
    choices,
    cotangent,
):
    length = frames.shape[1]
    element_count = lax.axis_size("dp") * lax.axis_size("tm") * length
    capacity = length * TOP // EXPERTS
    ids = choices[0]
    onehot = (ids[:, :, None] == jnp.arange(EXPERTS, dtype=jnp.int32)[None, None, :]).astype(
        jnp.float32
    )
    flat_ids = ids.reshape(-1)
    expert_hot = (flat_ids[:, None] == jnp.arange(EXPERTS, dtype=jnp.int32)[None, :]).astype(
        jnp.int32
    )
    slots = jnp.sum((jnp.cumsum(expert_hot, axis=0) - 1) * expert_hot, axis=1)
    places = (position(flat_ids) * capacity + slots).reshape(length, TOP)
    place_hot = places[:, :, None] == jnp.arange(EXPERTS * capacity, dtype=jnp.int32)[None, None, :]
    place_any = jnp.any(place_hot, axis=1).astype(jnp.bfloat16)
    place_hot = place_hot.astype(jnp.float32)

    def bucketed(rows):
        return lax.dot_general(place_any, rows, CONTRACT_ROWS, preferred_element_type=jnp.float32)

    up_buffer = bucketed(cotangent[0]).astype(jnp.bfloat16).reshape(EXPERTS, capacity, D)
    choose = onehot[:, 0] - onehot[:, 1]
    (
        combined,
        back,
        grad_in_local,
        grad_out_local,
        lags,
        moments,
        wide,
        normalized_input,
        resid,
        vhat,
        lrstd,
        gate,
    ) = main_step(
        frames[0],
        taps,
        batchnorm_gain_scale[None],
        batchnorm_shift_bias[None],
        jnp.pad(w_router, ((0, 0), (0, EXTRA - EXPERTS))),
        jnp.pad(choose, ((0, 0), (0, EXTRA - EXPERTS))),
        jnp.stack([place_hot[:, k] for k in range(TOP)]).astype(jnp.bfloat16),
        w_in,
        w_out,
        up_buffer,
        0,
    )
    lrstd, first = lrstd[:, :1], gate[:, 0]
    gates = jnp.stack([first, 1.0 - first], axis=1)
    inverse_deviation = lax.rsqrt(moments[1] / element_count + EPS)
    before_activation = normalized_input * batchnorm_gain_scale + batchnorm_shift_bias
    combined = combined.reshape(EXPERTS * capacity, D).astype(jnp.float32)
    back = back.reshape(EXPERTS * capacity, D).astype(jnp.float32)
    expert_out = [
        jnp.dot(place_hot[:, k], combined, precision=EXACT) for k in range(TOP)
    ]
    mixed = (resid + sum(gates[:, k, None] * expert_out[k] for k in range(TOP))).astype(jnp.bfloat16)
    upstream = cotangent[0].astype(jnp.float32)
    dgate = [jnp.sum(upstream * expert_out[k], axis=-1) for k in range(TOP)]
    dpick = (dgate[0] - dgate[1]) * first * (1.0 - first)
    dlogits = choose * dpick[:, None]
    dnormed = jnp.dot(dlogits, w_router.astype(jnp.float32).T, precision=EXACT)
    dnormed = dnormed + jnp.dot(jnp.sum(place_hot, axis=1), back, precision=EXACT)
    dmean = jnp.mean(dnormed, axis=-1, keepdims=True)
    dproj = jnp.mean(dnormed * vhat, axis=-1, keepdims=True)
    dresid = upstream + lrstd * (dnormed - dmean - vhat * dproj)
    normalized_gradient = dresid * swish_slope(before_activation) * batchnorm_gain_scale
    summed, grad_frames, grad_w_in, grad_w_out = last_step(
        wide,
        normalized_gradient,
        normalized_input,
        dresid,
        inverse_deviation[None],
        taps,
        grad_in_local,
        grad_out_local,
        element_count,
        2,
    )
    lag_rows = lags.reshape(-1, D)
    grad_taps = inverse_deviation * (
        summed[:, :-2].reshape(-1, D)[:TAPS]
        - summed[0, -2] / element_count * lag_rows[:TAPS]
        - summed[0, -1] / element_count * lag_rows[TAPS : 2 * TAPS]
    )
    grad_w_in, grad_w_out = grad_w_in.T.astype(jnp.float32), grad_w_out.astype(jnp.float32)
    return (mixed[None], grad_frames[None], grad_taps, grad_w_in, grad_w_out)


def solution(mesh):
    return jax.shard_map(
        body,
        mesh=mesh,
        in_specs=(
            P("dp", "tm", None),
            P(),
            P(),
            P(),
            P(),
            P(None, "tm"),
            P("tm", None),
            P("dp", "tm", None),
            P("dp", "tm", None),
        ),
        out_specs=(P("dp", "tm", None), P("dp", "tm", None), P(), P("dp", "tm"), P("tm", "dp")),
        check_vma=False,
    )
```
